32 devices in a mesh: dp: 4 (over z), pos: 8 (over y, x, core).
Axes of the slice: x: 2, y: 2, z: 4, core: 2. Of those that a mesh axis runs over, the one named last changes fastest.
Arguments:
- inputs: bfloat16 [512, 256, 512], P(('dp', 'pos')), may hold values from -6 to 6
- cotangent: bfloat16 [512, 256, 512], P(('dp', 'pos')), may hold values from -6 to 6
- counts: int32 [4, 8], P('dp'), may hold values from 1 to 16, 64 in all within a row
- seq_rank: int32 [4, 64], P('dp'), may hold values from 0 to 63, each once within a row
- first_gain: bfloat16 [512], P(('dp', 'pos')), may hold values from 0.25 to 1.75
- first_bias: bfloat16 [512], P(('dp', 'pos')), may hold values from -1.796875 to 1.796875
- query_weight: bfloat16 [512, 512], P(('dp', 'pos')), may hold values from -0.25 to 0.25
- key_weight: bfloat16 [512, 512], P(('dp', 'pos')), may hold values from -0.25 to 0.25
- value_weight: bfloat16 [512, 512], P(('dp', 'pos')), may hold values from -0.25 to 0.25
- output_weight: bfloat16 [512, 512], P(('dp', 'pos')), may hold values from -0.75 to 0.75
- second_gain: bfloat16 [512], P(('dp', 'pos')), may hold values from 0.25 to 1.75
- second_bias: bfloat16 [512], P(('dp', 'pos')), may hold values from -1.796875 to 1.796875
- control_weight: bfloat16 [512, 8], P(('dp', 'pos')), may hold values from -0.21875 to 0.21875
- expert_in: bfloat16 [8, 512, 2048], P(None, ('dp', 'pos')), may hold values from -1 to 1
- expert_out: bfloat16 [8, 2048, 512], P(None, ('dp', 'pos')), may hold values from -0.125 to 0.125
Outputs:
- layer_output: bfloat16 [512, 256, 512], P(('dp', 'pos'))
- input_grad: bfloat16 [512, 256, 512], P(('dp', 'pos'))
- first_gain_grad: float32 [512], P(('dp', 'pos'))
- first_bias_grad: float32 [512], P(('dp', 'pos'))
- query_grad: float32 [512, 512], P(('dp', 'pos'))
- key_grad: float32 [512, 512], P(('dp', 'pos'))
- value_grad: float32 [512, 512], P(('dp', 'pos'))
- output_grad: float32 [512, 512], P(('dp', 'pos'))
- second_gain_grad: float32 [512], P(('dp', 'pos'))
- second_bias_grad: float32 [512], P(('dp', 'pos'))
- control_grad: float32 [512, 8], P(('dp', 'pos'))
- expert_in_grad: float32 [8, 512, 2048], P(None, ('dp', 'pos'))
- expert_out_grad: float32 [8, 2048, 512], P(None, ('dp', 'pos'))
The draws below stay inside these ranges and needn't reach their ends.
Inputs may be any that keep to these rules, and one draw needn't show every extreme that they name: Each row of counts sums to 64, and its largest entry is 16. Each row of seq_rank holds every number of 0 to 63 once.
All inputs are finite; a program needn't handle non-finite values.
Results may differ from the reference program's by a relative error of at most 0.023.
Values may be sent and summed in bfloat16 or wider, within the bound.
A program may use at most 256 MiB of HBM per device.

```python
import math
import jax
import jax.numpy as jnp
import numpy as np
from jax import lax

D = 512
HEADS = 8
HEAD = 64
FFE = 2048
MIXED_SEQUENCES = 32
EXPERTS = 8
LEN = 256
SEQ_CAP = 16
SEQ_ROW = 64
SLOTS = 512
N_DP = 4
N_POS = 8


def block_levels(rng, dims, cuts, least, high):
    loudness, own = 1.0, jax.random.fold_in(rng, 6)
    for position, parts in cuts:
        steps = jnp.exp(jax.random.uniform(jax.random.fold_in(own, position), (parts,), jnp.float32, least / len(cuts), high / len(cuts)))
        loudness = loudness * jnp.repeat(steps, dims[position] // parts).reshape([-1 if axis == position else 1 for axis in range(len(dims))])
    return loudness


def profile(number_of, total, bound, skew):
    weights = [(1 << 20) // math.isqrt(standing ** skew) + 1 for standing in range(2, number_of + 1)]
    spare, holding = total - bound - (number_of - 1), [1] * (number_of - 1)
    while spare > 0:
        movable = [i for i in range(number_of - 1) if holding[i] < bound]
        mass, budget = sum([weights[i] for i in movable]), spare
        for i in movable:
            more = min(bound - holding[i], max(1, budget * weights[i] // mass), spare)
            holding[i] = holding[i] + more
            spare = spare - more
    return np.array([bound] + holding)


def ragged(key, count, total, most, skew):
    if count == 2:
        one = jax.random.randint(key, (), max(1, total - most), min(most, total - 1) + 1)
        return jnp.stack([one, total - one])
    lengths = jnp.asarray(profile(count, total, most, skew), jnp.int32)
    couples = (count - 1) // 2
    source_of, taker = lengths[1:1 + 2 * couples:2], lengths[2:2 + 2 * couples:2]
    margin = jnp.minimum(source_of - 1, most - taker)
    passed = jax.random.randint(jax.random.fold_in(key, 1), (couples,), 0, 1 << 20) % (margin + 1)
    lengths = lengths.at[1:1 + 2 * couples:2].set(source_of - passed).at[2:2 + 2 * couples:2].set(taker + passed)
    return lengths[jax.random.permutation(jax.random.fold_in(key, 2), count)]


def scatter_about(key, dims, scale, bound, split=(), kind=jnp.bfloat16):
    array = jax.random.normal(key, dims, jnp.float32) * scale
    if len(split) > 0:
        array = block_levels(key, dims, split, -0.22, 0.18) * array
    return jnp.clip(array, min=-bound, max=bound).astype(kind)


def setup_inputs(seed: int = 0) -> dict:
    arg_keys = jax.random.split(jax.random.key(seed), 16)
    return {
        "inputs": scatter_about(arg_keys[0], (SLOTS, LEN, D), 1.0, 6.0, ((0, 32),)),
        "cotangent": scatter_about(arg_keys[1], (SLOTS, LEN, D), 1.0, 6.0, ((0, 32),)),
        "counts": jax.vmap(lambda own: ragged(own, N_POS, SEQ_ROW, SEQ_CAP, 2))(jax.random.split(arg_keys[2], N_DP)).reshape((N_DP, N_POS)).astype(jnp.int32),
        "seq_rank": jax.vmap(lambda own: jax.random.permutation(own, SEQ_ROW))(jax.random.split(arg_keys[3], N_DP)).reshape((N_DP, SEQ_ROW)).astype(jnp.int32),
        "first_gain": jnp.clip(1.0 + 0.15 * jax.random.normal(arg_keys[4], (D,), jnp.float32), 0.25, 1.75).astype(jnp.bfloat16),
        "first_bias": scatter_about(arg_keys[5], (D,), 0.3, 1.796875, ((0, 32),)),
        "query_weight": scatter_about(arg_keys[6], (D, D), D ** -0.5, 0.25, ((0, 32),)),
        "key_weight": scatter_about(arg_keys[7], (D, D), D ** -0.5, 0.25, ((0, 32),)),
        "value_weight": scatter_about(arg_keys[8], (D, D), D ** -0.5, 0.25, ((0, 32),)),
        "output_weight": scatter_about(arg_keys[9], (D, D), (D // 8) ** -0.5, 0.75, ((0, 32),)),
        "second_gain": jnp.clip(1.0 + 0.15 * jax.random.normal(arg_keys[10], (D,), jnp.float32), 0.25, 1.75).astype(jnp.bfloat16),
        "second_bias": scatter_about(arg_keys[11], (D,), 0.3, 1.796875, ((0, 32),)),
        "control_weight": scatter_about(arg_keys[12], (D, EXPERTS), (D * 3 // 2) ** -0.5, 0.21875, ((0, 32),)),
        "expert_in": scatter_about(arg_keys[13], (EXPERTS, D, FFE), (D // 16) ** -0.5, 1.0, ((1, 32),)),
        "expert_out": scatter_about(arg_keys[14], (EXPERTS, FFE, D), FFE ** -0.5, 0.125, ((1, 32),)),
    }


exact_precision = lax.Precision.HIGHEST
NORM_EPS = 1e-05
MASKED = -1e+30

@jax.custom_vjp
def reduced_input(v):
    return lax.optimization_barrier(v.astype(jnp.bfloat16)).astype(jnp.float32)

@jax.custom_vjp
def reduced_gradient(v):
    return v

def low_keep(v):
    return (reduced_input(v), None)

def low_pass(kept, grad):
    return (grad,)

def back_keep(v):
    return (v, None)

def back_low(kept, grad):
    return (reduced_input(grad),)
reduced_input.defvjp(low_keep, low_pass)
reduced_gradient.defvjp(back_keep, back_low)

def layer_norm(values, norm_gain, norm_bias):
    center = values - lax.optimization_barrier(jnp.mean(values, axis=-1, keepdims=True))
    spread = lax.optimization_barrier(jnp.mean(center * center, axis=-1, keepdims=True))
    return center * lax.rsqrt(spread + NORM_EPS) * norm_gain + norm_bias

def reference(inputs, cotangent, counts, seq_rank, first_gain, first_bias, query_weight, key_weight, value_weight, output_weight, second_gain, second_bias, control_weight, expert_in, expert_out):
    slot_count = inputs.shape[0]
    slot_index = jnp.arange(slot_count, dtype=jnp.int32)
    device_index = slot_index // SEQ_CAP
    row_index = device_index // N_POS
    column_index = device_index % N_POS
    within = slot_index % SEQ_CAP
    starts = (jnp.cumsum(counts, axis=1) - counts).astype(jnp.int32)
    live_slot = within < counts[row_index, column_index]
    seq_order = jnp.where(live_slot, starts[row_index, column_index] + within, 0).astype(jnp.int32)
    groups_row = SEQ_ROW // MIXED_SEQUENCES
    group_id = row_index * groups_row + seq_rank[row_index, seq_order] // MIXED_SEQUENCES
    member = ((group_id[None, :] == jnp.arange(N_DP * groups_row, dtype=jnp.int32)[:, None]) & live_slot[None, :]).astype(jnp.float32)
    member_cells = member[:, :, None, None]
    live_cells = live_slot[:, None, None]
    scaling = 1.0 / math.sqrt(HEAD)
    causal = lax.broadcasted_iota(jnp.int32, (LEN, LEN), 1) <= lax.broadcasted_iota(jnp.int32, (LEN, LEN), 0)

    def block_layer(source, gain_one, bias_one, w_query, w_key, w_value, output_matrix, gain_two, bias_two, router_weight, w_up, w_down):

        def holder(block_rows):
            seqs = block_rows.shape[0]
            normalized_rows = reduced_input(layer_norm(block_rows, gain_one, bias_one))

            def project(weight_matrix):
                relocated_rows = jnp.einsum('vwm,mx->vwx', normalized_rows, weight_matrix, precision=exact_precision)
                return reduced_gradient(reduced_input(relocated_rows)).reshape(seqs, LEN, HEADS, HEAD)
            queries, key_rows, value_rows = (project(w_query), project(w_key), project(w_value))
            scores = reduced_gradient(jnp.einsum('bqhc,bkhc->bhqk', queries, key_rows, precision=exact_precision) * scaling)
            scores = jnp.where(causal[None, None], scores, MASKED)
            exponent = jnp.exp(scores - lax.optimization_barrier(jnp.max(scores, axis=-1, keepdims=True)))
            attn_probs = exponent / lax.optimization_barrier(jnp.sum(exponent, axis=-1, keepdims=True))
            context_rows = jnp.einsum('bhqk,bkhc->bqhc', reduced_input(attn_probs), value_rows, precision=exact_precision)
            context_rows = reduced_gradient(reduced_input(context_rows.reshape(seqs, LEN, D)))
            attention_output = reduced_gradient(jnp.einsum('vwm,mx->vwx', context_rows, output_matrix, precision=exact_precision))
            residual = block_rows + attention_output
            mixture_input = reduced_gradient(reduced_input(layer_norm(residual, gain_two, bias_two)))
            return (residual, mixture_input)
        blocks = source.reshape(slot_count // SEQ_CAP, SEQ_CAP, LEN, D)
        residual, mixture_input = lax.map(jax.checkpoint(holder), blocks)
        residual = residual.reshape(slot_count, LEN, D)
        mixture_input = mixture_input.reshape(slot_count, LEN, D)
        router_logits = reduced_gradient(jnp.einsum('vwm,mx->vwx', mixture_input, router_weight, precision=exact_precision))
        group_peak = lax.optimization_barrier(jnp.max(jnp.where(member_cells > 0, router_logits[None], MASKED), axis=1))
        slot_peak = lax.optimization_barrier(jnp.sum(member_cells * group_peak[:, None], axis=0))
        exponent = jnp.where(live_cells, jnp.exp(router_logits - slot_peak), 0.0)
        group_total = lax.optimization_barrier(jnp.sum(member_cells * exponent[None], axis=1))
        slot_total = jnp.where(live_cells, lax.optimization_barrier(jnp.sum(member_cells * group_total[:, None], axis=0)), 1.0)
        token_share = reduced_input(exponent / slot_total)
        routing_weights = member_cells * token_share[None]
        expert_mixture = reduced_gradient(reduced_input(jnp.einsum('pzqm,zqr->qpmr', routing_weights, mixture_input, precision=exact_precision)))
        hidden_pre = reduced_gradient(jnp.einsum('lged,edf->lgef', expert_mixture, w_up, precision=exact_precision))
        hidden = reduced_gradient(reduced_input(jax.nn.gelu(hidden_pre)))
        expert_output_rows = reduced_gradient(reduced_input(jnp.einsum('lgef,efd->lged', hidden, w_down, precision=exact_precision)))
        returned_rows = reduced_input(MIXED_SEQUENCES * jnp.einsum('vjrc,rvco->jro', routing_weights, expert_output_rows, precision=exact_precision))
        return jnp.where(live_cells, residual + returned_rows, 0.0)
    float_args = (inputs.astype(jnp.float32), first_gain.astype(jnp.float32), first_bias.astype(jnp.float32), query_weight.astype(jnp.float32), key_weight.astype(jnp.float32), value_weight.astype(jnp.float32), output_weight.astype(jnp.float32), second_gain.astype(jnp.float32), second_bias.astype(jnp.float32), control_weight.astype(jnp.float32), expert_in.astype(jnp.float32), expert_out.astype(jnp.float32))
    result, pullback = jax.vjp(block_layer, *float_args)
    gradients = pullback(cotangent.astype(jnp.float32))
    return (result.astype(jnp.bfloat16), gradients[0].astype(jnp.bfloat16), gradients[1], gradients[2], gradients[3], gradients[4], gradients[5], gradients[6], gradients[7], gradients[8], gradients[9], gradients[10], gradients[11])
```

```python
import math
import jax
import jax.numpy as jnp
from jax import lax
from jax.experimental import pallas as pl
from jax.experimental.pallas import tpu as pltpu

HEADS = 8
HEAD = 64
NORM_EPS = 1e-05
MASKED = -1e30
F32 = jnp.float32
BF16 = jnp.bfloat16
MIB = 1 << 20


def dot(a, b, ca=1, cb=0):
    return lax.dot_general(a, b, (((ca,), (cb,)), ((), ())), preferred_element_type=F32)


def normalize(v):
    center = v - jnp.mean(v, axis=-1, keepdims=True)
    spread = jnp.mean(center * center, axis=-1, keepdims=True)
    scale = lax.rsqrt(spread + NORM_EPS)
    return center * scale, scale


def head_rows(array_t, head):
    rows = array_t[head * HEAD : (head + 1) * HEAD, :]
    zero = jnp.zeros_like(rows)
    return jnp.concatenate([rows, zero] if head % 2 == 0 else [zero, rows], axis=0)


def forward_kernel(count, x, w_t, wk, wo, small, q_t, k, v_t, ctx_t, x1, h, lse):
    g1, b1, g2, b2 = (small[i : i + 1] for i in range(4))
    slots, length, width = x.shape
    wq_t, wv_t = w_t.at[:width], w_t.at[2 * width :]
    half = length // 2
    causal = lax.broadcasted_iota(jnp.int32, (half, half), 0) <= lax.broadcasted_iota(
        jnp.int32, (half, half), 1
    )

    def one():
        source = x[...].reshape(slots * length, width).astype(F32)
        xhat, _ = normalize(source)
        a = (xhat * g1 + b1).astype(BF16)
        qs = (dot(wq_t[...], a, 1, 1).astype(BF16) * 0.125).astype(BF16)
        ks = dot(a, wk[...]).astype(BF16)
        vs = dot(wv_t[...], a, 1, 1).astype(BF16)
        k[...] = ks.reshape(slots, length, width)
        ones = jnp.ones((16, length), BF16)
        parts = [[] for _ in range(slots)]
        sums = [[] for _ in range(slots)]
        cols = [slice(s * length, (s + 1) * length) for s in range(slots)]
        for s in range(slots):
            q_t[s] = qs[:, cols[s]]
            v_t[s] = vs[:, cols[s]]
        for head in range(HEADS):
            for s in range(slots):
                pair = ks[cols[s], (head // 2) * 128 : (head // 2) * 128 + 128]
                st = dot(pair, head_rows(qs[:, cols[s]], head))
                s00 = jnp.where(causal, st[:half, :half], MASKED)
                s01 = st[:half, half:]
                s11 = jnp.where(causal, st[half:, half:], MASKED)
                m0 = jnp.max(s00, axis=0, keepdims=True)
                m1 = jnp.maximum(
                    jnp.max(s01, axis=0, keepdims=True), jnp.max(s11, axis=0, keepdims=True)
                )
                e00 = jnp.exp(s00 - m0).astype(BF16)
                e01 = jnp.exp(s01 - m1).astype(BF16)
                e11 = jnp.exp(s11 - m1).astype(BF16)
                et = jnp.concatenate(
                    [
                        jnp.concatenate([e00, e01], axis=1),
                        jnp.concatenate([jnp.zeros_like(e00), e11], axis=1),
                    ],
                    axis=0,
                )
                va = jnp.concatenate([vs[head * HEAD : (head + 1) * HEAD, cols[s]], ones], axis=0)
                full = dot(va, et)
                total = full[HEAD : HEAD + 1]
                parts[s].append((full[:HEAD] * (1.0 / total)).astype(BF16))
                sums[s].append(jnp.concatenate([m0, m1], axis=1) + jnp.log(total))
        outs = []
        for s in range(slots):
            ctx = jnp.concatenate(parts[s], axis=0)
            ctx_t[s] = ctx
            lse[s] = jnp.concatenate(sums[s], axis=0)
            outs.append(dot(ctx, wo[...], 0, 0))
        residual = source + jnp.concatenate(outs, axis=0)
        x1[...] = residual.reshape(slots, length, width)
        xhat2, _ = normalize(residual)
        h[...] = (xhat2 * g2 + b2).astype(BF16).reshape(slots, length, width)

    live = pl.program_id(0) * slots < count[0]
    pl.when(live)(one)

    @pl.when(jnp.logical_not(live))
    def _():
        h[...] = jnp.zeros((slots, length, width), BF16)


def forward(count, x, w_t, wk, wo, small, block=1):
    slots, length, width = x.shape
    per = lambda rows, cols: pl.BlockSpec((block, rows, cols), lambda i, c: (i, 0, 0))
    whole = lambda a: pl.BlockSpec(a.shape, lambda i, c: (0,) * a.ndim)
    shape = lambda rows, cols, kind: jax.ShapeDtypeStruct((slots, rows, cols), kind)
    return pl.pallas_call(
        forward_kernel,
        grid_spec=pltpu.PrefetchScalarGridSpec(
            num_scalar_prefetch=1,
            grid=(slots // block,),
            in_specs=[per(length, width)]
            + [whole(a) for a in (w_t, wk, wo, small)],
            out_specs=[
                per(width, length),
                per(length, width),
                per(width, length),
                per(width, length),
                per(length, width),
                per(length, width),
                per(HEADS, length),
            ],
        ),
        out_shape=[
            shape(width, length, BF16),
            shape(length, width, BF16),
            shape(width, length, BF16),
            shape(width, length, BF16),
            shape(length, width, F32),
            shape(length, width, BF16),
            shape(HEADS, length, F32),
        ],
        compiler_params=pltpu.CompilerParams(vmem_limit_bytes=48 * MIB),
        cost_estimate=pl.CostEstimate(
            flops=40_000_000_000, bytes_accessed=40 * MIB, transcendentals=8_000_000
        ),
        name="attention_forward",
    )(count, x, w_t, wk, wo, small)


def norm_back(grad, xhat, scale):
    return scale * (
        grad
        - jnp.mean(grad, axis=-1, keepdims=True)
        - xhat * jnp.mean(grad * xhat, axis=-1, keepdims=True)
    )


def backward_kernel(
    count, x, cot, x1, mix, dh, dc, q_t, k, v_t, ctx_t, lse, w_t, wo, small,
    lo, dx, grad_t, out_grad, vecs, back_t,
):
    slots, length, width = x.shape
    half = length // 2
    causal = lax.broadcasted_iota(jnp.int32, (half, half), 0) <= lax.broadcasted_iota(
        jnp.int32, (half, half), 1
    )
    step = pl.program_id(0)

    @pl.when(step == 0)
    def _():
        grad_t[...] = jnp.zeros_like(grad_t)
        out_grad[...] = jnp.zeros_like(out_grad)
        vecs[...] = jnp.zeros_like(vecs)

    g1, b1, g2, b2 = (small[i : i + 1] for i in range(4))
    router = small[8:16].astype(BF16)

    def one():
        tokens = slots * length
        cols = [slice(s * length, (s + 1) * length) for s in range(slots)]
        row = lax.broadcasted_iota(jnp.int32, (tokens, 1), 0) // length + step * slots
        live = row < count[0]
        keep = lambda v: v if slots == 1 else jnp.where(live, v, 0.0)
        residual = x1[...].reshape(tokens, width)
        xhat2, scale2 = normalize(residual)
        lo[...] = (
            keep(residual + mix[...].reshape(tokens, width).astype(F32))
            .astype(BF16)
            .reshape(slots, length, width)
        )
        hidden = (xhat2 * g2 + b2).astype(BF16)
        routed = []
        for s in range(slots):
            routed.append(dot(dc[s], router, 0, 0))
            vecs[8:16] += dot(dc[s], hidden[cols[s], :])
        grad_h = (
            (dh[...].reshape(tokens, width).astype(F32) + jnp.concatenate(routed, axis=0))
            .astype(BF16)
            .astype(F32)
        )
        vecs[0:1] += jnp.sum(grad_h * xhat2, axis=0, keepdims=True)
        vecs[1:2] += jnp.sum(grad_h, axis=0, keepdims=True)
        dx1 = keep(
            cot[...].reshape(tokens, width).astype(F32) + norm_back(grad_h * g2, xhat2, scale2)
        )
        datt = dx1.astype(BF16)
        dctx = dot(wo[...], datt, 1, 1).astype(BF16)
        partial = None
        for s in range(slots):
            term = dot(ctx_t[s], datt[cols[s], :])
            partial = term if partial is None else partial + term
        out_grad[...] += partial
        for s in range(slots):
            kt = jnp.transpose(k[s])
            vn = jnp.transpose(v_t[s])
            for head in range(HEADS):
                rows = slice(head * HEAD, (head + 1) * HEAD)
                pair = slice((head // 2) * 128, (head // 2) * 128 + 128)
                st = dot(k[s, :, pair], head_rows(q_t[s], head))
                stat = lse[s, head : head + 1, :]
                p00 = jnp.exp(jnp.where(causal, st[:half, :half], MASKED) - stat[:, :half])
                p01 = jnp.exp(st[:half, half:] - stat[:, half:])
                p11 = jnp.exp(jnp.where(causal, st[half:, half:], MASKED) - stat[:, half:])
                dctx_s = dctx[:, cols[s]]
                dp = dot(vn[:, pair], head_rows(dctx_s, head))
                inner = jnp.sum(
                    ctx_t[s, rows, :].astype(F32) * dctx_s[rows, :].astype(F32),
                    axis=0,
                    keepdims=True,
                )
                d00 = (p00 * (dp[:half, :half] - inner[:, :half])).astype(BF16)
                d01 = (p01 * (dp[:half, half:] - inner[:, half:])).astype(BF16)
                d11 = (p11 * (dp[half:, half:] - inner[:, half:])).astype(BF16)
                zero = jnp.zeros((half, half), BF16)

                def whole(c00, c01, c11):
                    return jnp.concatenate(
                        [
                            jnp.concatenate([c00, c01], axis=1),
                            jnp.concatenate([zero, c11], axis=1),
                        ],
                        axis=0,
                    )

                ds = whole(d00, d01, d11)
                pt = whole(p00.astype(BF16), p01.astype(BF16), p11.astype(BF16))
                dq = dot(kt[rows, :], ds) * 0.125
                dk = dot(q_t[s, rows, :], ds, 1, 1)
                dv = dot(dctx_s[rows, :], pt, 1, 1)
                back_t[rows, cols[s]] = dq.astype(BF16)
                back_t[width + head * HEAD : width + (head + 1) * HEAD, cols[s]] = dk.astype(BF16)
                back_t[2 * width + head * HEAD : 2 * width + (head + 1) * HEAD, cols[s]] = dv.astype(
                    BF16
                )
        source = x[...].reshape(tokens, width).astype(F32)
        xhat1, scale1 = normalize(source)
        a = (xhat1 * g1 + b1).astype(BF16)
        back = back_t[...]
        grad_t[...] += dot(back, a)
        da = dot(back, w_t[...], 0, 0)
        vecs[2:3] += jnp.sum(da * xhat1, axis=0, keepdims=True)
        vecs[3:4] += jnp.sum(da, axis=0, keepdims=True)
        dx[...] = (
            keep(dx1 + norm_back(da * g1, xhat1, scale1))
            .astype(BF16)
            .reshape(slots, length, width)
        )

    some = step * slots < count[0]
    pl.when(some)(one)

    @pl.when(jnp.logical_not(some))
    def _():
        dx[...] = jnp.zeros((slots, length, width), BF16)
        lo[...] = jnp.zeros((slots, length, width), BF16)


def backward(count, x, cot, x1, mix, dh, dc, q_t, k, v_t, ctx_t, lse, w_t, wo, small, block=1):
    slots, length, width = x.shape
    per = lambda a: pl.BlockSpec((block,) + a.shape[1:], lambda i, c: (i, 0, 0))
    whole = lambda a: pl.BlockSpec(a.shape, lambda i, c: (0,) * len(a.shape))
    outs = [
        jax.ShapeDtypeStruct((3 * width, width), F32),
        jax.ShapeDtypeStruct((width, width), F32),
        jax.ShapeDtypeStruct((16, width), F32),
    ]
    batched = (x, cot, x1, mix, dh, dc, q_t, k, v_t, ctx_t, lse)
    shared = (w_t, wo, small)
    return pl.pallas_call(
        backward_kernel,
        grid_spec=pltpu.PrefetchScalarGridSpec(
            num_scalar_prefetch=1,
            grid=(slots // block,),
            in_specs=[per(a) for a in batched] + [whole(a) for a in shared],
            out_specs=[per(x), per(x)] + [whole(a) for a in outs],
            scratch_shapes=[pltpu.VMEM((3 * width, block * length), BF16)],
        ),
        out_shape=[jax.ShapeDtypeStruct(x.shape, BF16)] * 2 + outs,
        compiler_params=pltpu.CompilerParams(vmem_limit_bytes=56 * MIB),
        cost_estimate=pl.CostEstimate(
            flops=100_000_000_000, bytes_accessed=60 * MIB, transcendentals=8_000_000
        ),
        name="attention_backward",
    )(count, *batched, *shared)


MESH = pl.DeviceIdType.MESH
TILE = 16


def bits_of(size):
    return size.bit_length() - 1


def orders(count):
    first = list(range(count))
    second = list(first)
    if count > 2:
        second[1], second[2] = second[2], second[1]
    return first, second


def greet(peers):
    barrier = pltpu.get_barrier_semaphore()
    for peer in peers:
        pl.semaphore_signal(barrier, inc=1, device_id=peer, device_id_type=MESH)
    pl.semaphore_wait(barrier, len(peers))


def my_bits(place, count):
    return [lax.rem(place // (1 << bit), 2) for bit in range(count)]


def across(place, bits, bit):
    return place + (1 - 2 * bits[bit]) * (1 << bit)


def pick(remaining, chosen):
    return tuple(chosen[bit] if bit in chosen else slice(None) for bit in remaining)


def remote(src, dst, send, recv, device):
    return pltpu.make_async_remote_copy(
        src_ref=src,
        dst_ref=dst,
        send_sem=send,
        recv_sem=recv,
        device_id=device,
        device_id_type=MESH,
    )


def gather_kernel(dp, pos, wq, wk, wv, wo, small, w_t, wk_out, wo_out, vt, held, send, recv):
    count = bits_of(pos)
    row, place = lax.axis_index("dp"), lax.axis_index("pos")
    bits = my_bits(place, count)
    others = [lax.rem(row + step, dp) for step in range(1, dp)]
    greet(
        [(other, place) for other in others]
        + [(row, across(place, bits, bit)) for bit in range(count)]
    )
    width = wq.shape[1]
    every = list(range(count))[::-1]
    mine = {bit: bits[bit] for bit in every}
    here = pick(every, mine)
    for index, weight in enumerate((wq, wk, wv, wo)):
        held[(row,) + here + (slice(None), slice(index * width, (index + 1) * width))] = weight[...]
    held[(row,) + here + (slice(None), slice(4 * width, 4 * width + 128))] = small[...]
    copies = []
    for step, other in enumerate(others):
        spot = held.at[(row,) + here]
        copies.append(remote(spot, spot, send.at[step], recv.at[step], (other, place)))
        copies[-1].start()
    for copy in copies:
        copy.wait()
    used = dp - 1
    halves = (slice(0, dp // 2), slice(dp // 2, dp))
    first, second = orders(count)
    for stage in range(count):
        copies = []
        for half, order in zip(halves, (first[::-1], second[::-1])):
            done = order[:stage]
            bit = order[stage]
            spot = held.at[(half,) + pick(every, {b: bits[b] for b in every if b not in done})]
            copies.append(
                remote(
                    spot, spot, send.at[used], recv.at[used], (row, across(place, bits, bit))
                )
            )
            used += 1
        for copy in copies:
            copy.start()
        for copy in copies:
            copy.wait()
    full = held[...].reshape(dp * pos * wq.shape[0], 4 * width + 128)
    for index in range(3):
        w_t[index * width : (index + 1) * width, :] = jnp.transpose(
            full[:, index * width : (index + 1) * width]
        )
    wk_out[...] = full[:, width : 2 * width]
    wo_out[...] = full[:, 3 * width : 4 * width]
    vt[...] = jnp.transpose(full[:, 4 * width :])[:16, :].astype(F32)


def gather_weights(dp, pos, wq, wk, wv, wo, small):
    rows, width = wq.shape
    whole = rows * dp * pos
    vmem = pl.BlockSpec(memory_space=pltpu.VMEM)
    total = dp - 1 + 2 * bits_of(pos)
    return pl.pallas_call(
        lambda *refs: gather_kernel(dp, pos, *refs),
        out_shape=[
            jax.ShapeDtypeStruct((3 * width, whole), BF16),
            jax.ShapeDtypeStruct((whole, width), BF16),
            jax.ShapeDtypeStruct((whole, width), BF16),
            jax.ShapeDtypeStruct((16, whole), F32),
        ],
        in_specs=[vmem] * 5,
        out_specs=[vmem] * 4,
        scratch_shapes=[
            pltpu.VMEM((dp,) + (2,) * bits_of(pos) + (rows, 4 * width + 128), BF16),
            pltpu.SemaphoreType.DMA((total,)),
            pltpu.SemaphoreType.DMA((total,)),
        ],
        compiler_params=pltpu.CompilerParams(
            collective_id=0, has_side_effects=True, vmem_limit_bytes=40 * MIB
        ),
        name="gather_weights",
    )(wq, wk, wv, wo, small)


def scatter_kernel(dp, pos, grad_t, out_grad, vecs, out, held, *rest):
    count = bits_of(pos)
    buffers, slots, (send, recv) = rest[: 2 * count], rest[2 * count], rest[2 * count + 1 :]
    row, place = lax.axis_index("dp"), lax.axis_index("pos")
    bits = my_bits(place, count)
    others = [lax.rem(row + step, dp) for step in range(1, dp)]
    greet(
        [(other, place) for other in others]
        + [(row, across(place, bits, bit)) for bit in range(count)]
    )
    width = out_grad.shape[1]
    lead = held.shape[:-1]
    for index in range(3):
        held[..., index * width : (index + 1) * width] = (
            jnp.transpose(grad_t[index * width : (index + 1) * width, :])
            .astype(BF16)
            .reshape(lead + (width,))
        )
    held[..., 3 * width : 4 * width] = out_grad[...].astype(BF16).reshape(lead + (width,))
    tail = jnp.concatenate([vecs[...], jnp.zeros((112, vecs.shape[1]), F32)], axis=0)
    held[..., 4 * width :] = jnp.transpose(tail).astype(BF16).reshape(lead + (128,))
    used = 0
    halves = (slice(0, dp // 2), slice(dp // 2, dp))
    plans = orders(count)
    current = [held.at[half] for half in halves]
    remaining = [list(range(count))[::-1] for _ in halves]
    for stage in range(count):
        copies = []
        for side in range(2):
            bit = plans[side][stage]
            away = (slice(None),) + pick(remaining[side], {bit: 1 - bits[bit]})
            copies.append(
                remote(
                    current[side].at[away],
                    buffers[side * count + stage],
                    send.at[used],
                    recv.at[used],
                    (row, across(place, bits, bit)),
                )
            )
            used += 1
        for copy in copies:
            copy.start()
        for side in range(2):
            copies[side].wait()
            bit = plans[side][stage]
            near = (slice(None),) + pick(remaining[side], {bit: bits[bit]})
            target = buffers[side * count + stage]
            target[...] = (
                target[...].astype(F32) + current[side][near].astype(F32)
            ).astype(BF16)
            current[side] = target
            remaining[side] = [b for b in remaining[side] if b != bit]
    joined = jnp.concatenate([current[0][...], current[1][...]], axis=0)
    slots[1] = joined
    copies = []
    for step, other in enumerate(others):
        copies.append(
            remote(
                slots.at[1, other],
                slots.at[0, row],
                send.at[used],
                recv.at[used],
                (other, place),
            )
        )
        used += 1
        copies[-1].start()
    for copy in copies:
        copy.wait()
    total = slots[1, row].astype(F32)
    for other in others:
        total = total + slots[0, other].astype(F32)
    out[...] = total


def scatter_weights(dp, pos, grad_t, out_grad, vecs):
    width = out_grad.shape[1]
    rows = out_grad.shape[0] // (dp * pos)
    wide = 4 * width + 128
    vmem = pl.BlockSpec(memory_space=pltpu.VMEM)
    count = bits_of(pos)
    total = dp - 1 + 2 * count
    return pl.pallas_call(
        lambda *refs: scatter_kernel(dp, pos, *refs),
        out_shape=jax.ShapeDtypeStruct((rows, wide), F32),
        in_specs=[vmem] * 3,
        out_specs=vmem,
        scratch_shapes=[pltpu.VMEM((dp,) + (2,) * count + (rows, wide), BF16)]
        + [
            pltpu.VMEM((dp // 2,) + (2,) * (count - 1 - stage) + (rows, wide), BF16)
            for _ in range(2)
            for stage in range(count)
        ]
        + [
            pltpu.VMEM((2, dp, rows, wide), BF16),
            pltpu.SemaphoreType.DMA((total,)),
            pltpu.SemaphoreType.DMA((total,)),
        ],
        compiler_params=pltpu.CompilerParams(
            collective_id=1, has_side_effects=True, vmem_limit_bytes=48 * MIB
        ),
        name="scatter_weights",
    )(grad_t, out_grad, vecs)


def spread(packed, lane, block):
    chosen = jnp.where(lane // TILE == block, packed, 0.0)
    return fold(chosen, jnp.add)


def fold(values, combine):
    size = values.shape[-1]
    shift = TILE
    while shift < size:
        values = combine(values, pltpu.roll(values, shift, 1))
        shift *= 2
    return values


def block_weights(share, member, groups):
    experts, lanes = share.shape
    rounded = share.astype(BF16).astype(F32)
    spot = (
        lax.broadcasted_iota(jnp.int32, (TILE, lanes), 0)
        == lax.rem(lax.broadcasted_iota(jnp.int32, (TILE, lanes), 1), TILE)
    ).astype(F32)
    mask = jnp.stack([spot * member[g : g + 1, :] for g in range(groups)])
    full = rounded[:, None, None, :] * mask[None]
    return full.reshape(experts * groups * TILE, lanes).astype(BF16), mask


def exchange(local, gathered, send, recv, row, place, pos):
    copies = []
    for step in range(1, pos):
        copies.append(
            remote(
                local,
                gathered.at[step - 1],
                send.at[step - 1],
                recv.at[step - 1],
                (row, lax.rem(place + step, pos)),
            )
        )
        copies[-1].start()
    for copy in copies:
        copy.wait()


def expert_kernel(
    pos, groups, h, cot, member, wc, win, wout,
    share, y_all, dm_all, gin, gout,
    logits, stats, gathered, m_part, dy_part, z, slope, du, own, *rest,
):
    count = bits_of(pos)
    buffers = rest[: 4 * count]
    asend, arecv, bsend, brecv, csend, crecv, lsem = rest[4 * count :]
    row, place = lax.axis_index("dp"), lax.axis_index("pos")
    bits = my_bits(place, count)
    greet([(row, lax.rem(place + step, pos)) for step in range(1, pos)])
    slots, length, width = h.shape
    blocks = length // TILE
    lanes = slots * TILE
    experts = wc.shape[0]
    lane = lax.broadcasted_iota(jnp.int32, (experts, lanes), 1)
    stats[...] = jnp.zeros_like(stats)
    router = wc[...].astype(BF16)

    def first(block, carry):
        rows = h[:, pl.ds(pl.multiple_of(block * TILE, TILE), TILE), :].reshape(lanes, width)
        logit = dot(router, rows, 1, 1)
        logits[block] = logit
        for g in range(groups):
            inside = member[g : g + 1, :] > 0
            peak = fold(jnp.where(inside, logit, MASKED), jnp.maximum)
            total = fold(jnp.where(inside, jnp.exp(logit - peak), 0.0), jnp.add)
            here = lane // TILE == block
            stats[g] = jnp.where(here, peak, stats[g])
            stats[groups + g] = jnp.where(here, total, stats[groups + g])
        return carry

    lax.fori_loop(0, blocks, first, 0)
    exchange(stats, gathered, asend, arecv, row, place, pos)
    for g in range(groups):
        peak = stats[g]
        for step in range(pos - 1):
            peak = jnp.maximum(peak, gathered[step, g])
        total = stats[groups + g] * jnp.exp(stats[g] - peak)
        for step in range(pos - 1):
            total = total + gathered[step, groups + g] * jnp.exp(gathered[step, g] - peak)
        stats[g] = peak
        stats[groups + g] = 1.0 / total

    lead = (2,) * (count + 1)
    live = jnp.sum(member[...], axis=0, keepdims=True) > 0

    def second(block, carry):
        where = pl.ds(pl.multiple_of(block * TILE, TILE), TILE)
        rows = h[:, where, :].reshape(lanes, width)
        peak = jnp.zeros((experts, lanes), F32)
        scale = jnp.zeros((experts, lanes), F32)
        for g in range(groups):
            inside = member[g : g + 1, :]
            peak = peak + inside * spread(stats[g], lane, block)
            scale = scale + inside * spread(stats[groups + g], lane, block)
        part = jnp.exp(jnp.where(live, logits[block] - peak, MASKED)) * scale
        share[block] = part
        weights, _ = block_weights(part, member, groups)
        m_part[..., where, :] = dot(weights, rows).astype(BF16).reshape(lead + (TILE, width))
        grads = cot[:, where, :].reshape(lanes, width)
        dy_part[..., where, :] = (
            (32.0 * dot(weights, grads)).astype(BF16).reshape(lead + (TILE, width))
        )
        return carry

    lax.fori_loop(0, blocks, second, 0)

    plans = orders(count)
    every = list(range(count))[::-1]
    sources = (m_part, dy_part)
    partner = lambda bit: (row, across(place, bits, bit))

    def start(which, side, stage):
        lane_of = 2 * which + side
        bit = plans[side][stage]
        left = [b for b in every if b not in plans[side][:stage]]
        away = pick(left, {bit: 1 - bits[bit]})
        src = (
            sources[which].at[away + (side,)]
            if stage == 0
            else buffers[lane_of * count + stage - 1].at[away]
        )
        copy = remote(
            src,
            buffers[lane_of * count + stage],
            bsend.at[lane_of * count + stage],
            brecv.at[lane_of * count + stage],
            partner(bit),
        )
        copy.start()
        return copy

    def finish(copy, which, side, stage):
        lane_of = 2 * which + side
        copy.wait()
        bit = plans[side][stage]
        left = [b for b in every if b not in plans[side][:stage]]
        near = pick(left, {bit: bits[bit]})
        target = buffers[lane_of * count + stage]
        if stage == 0:
            old = sources[which][near + (side,)]
        else:
            old = buffers[lane_of * count + stage - 1][near]
        target[...] = (target[...].astype(F32) + old.astype(F32)).astype(BF16)

    flying = {(which, side): start(which, side, 0) for which in range(2) for side in range(2)}
    for which in range(2):
        for stage in range(count):
            for side in range(2):
                finish(flying[which, side], which, side, stage)
                if stage + 1 < count:
                    flying[which, side] = start(which, side, stage + 1)
        if which == 0:
            rows = 2 * length
            m = jnp.concatenate(
                [buffers[side * count + count - 1][...] for side in range(2)], axis=0
            )
            hidden = win.shape[1]
            piece = 512
            y = jnp.zeros((rows, width), F32)
            for c in range(0, hidden, piece):
                u = dot(m, win[:, c : c + piece])
                inner = math.sqrt(2 / math.pi) * (u + 0.044715 * u * u * u)
                t = jnp.tanh(inner)
                active = (0.5 * u * (1.0 + t)).astype(BF16)
                z[:, c : c + piece] = active
                slope[:, c : c + piece] = 0.5 * (1.0 + t) + 0.5 * u * (1.0 - t * t) * (
                    math.sqrt(2 / math.pi) * (1.0 + 3 * 0.044715 * u * u)
                )
                y = y + dot(active, wout[c : c + piece, :])
            own[0] = y.astype(BF16).reshape(2, length, width)
    dy = jnp.concatenate(
        [buffers[(2 + side) * count + count - 1][...] for side in range(2)], axis=0
    )
    dm = jnp.zeros((rows, width), F32)
    for c in range(0, hidden, piece):
        dz = dot(dy, wout[c : c + piece, :], 1, 1).astype(BF16).astype(F32)
        grad = (dz * slope[:, c : c + piece]).astype(BF16)
        du[:, c : c + piece] = grad
        dm = dm + dot(grad, win[:, c : c + piece], 1, 1)
    own[1] = dm.astype(BF16).reshape(2, length, width)

    targets = (y_all, dm_all)
    mine = pick(every, {b: bits[b] for b in every})
    placed = []
    for which in range(2):
        for side in range(2):
            copy = pltpu.make_async_copy(
                own.at[which, side], targets[which].at[mine + (side,)], lsem.at[2 * which + side]
            )
            copy.start()
            placed.append(copy)

    def push(which, side, stage):
        lane_of = 2 * which + side
        order = plans[side][::-1]
        bit = order[stage]
        spot = targets[which].at[
            pick(every, {b: bits[b] for b in every if b not in order[:stage]}) + (side,)
        ]
        copy = remote(
            own.at[which, side] if stage == 0 else spot,
            spot,
            csend.at[lane_of * count + stage],
            crecv.at[lane_of * count + stage],
            partner(bit),
        )
        copy.start()
        return copy

    flying = {(which, side): push(which, side, 0) for which in range(2) for side in range(2)}
    for copy in placed:
        copy.wait()
    for c in range(0, hidden, piece):
        gin[:, c : c + piece] = dot(m, du[:, c : c + piece], 0, 0).astype(BF16)
        gout[c : c + piece, :] = dot(z[:, c : c + piece], dy, 0, 0).astype(BF16)
    for stage in range(count):
        for which in range(2):
            for side in range(2):
                flying[which, side].wait()
                if stage + 1 < count:
                    flying[which, side] = push(which, side, stage + 1)


def mix_experts(pos, groups, h, cot, member, wc, win, wout):
    slots, length, width = h.shape
    experts = wc.shape[0]
    lead = (2,) * (bits_of(pos) + 1)
    hidden = win.shape[1]
    blocks = length // TILE
    count = bits_of(pos)
    vmem = pl.BlockSpec(memory_space=pltpu.VMEM)
    hbm = pl.BlockSpec(memory_space=pl.ANY)
    rows = 2 * length
    return pl.pallas_call(
        lambda *refs: expert_kernel(pos, groups, *refs),
        out_shape=[
            jax.ShapeDtypeStruct((blocks, experts, slots * TILE), F32),
            jax.ShapeDtypeStruct(lead + (length, width), BF16),
            jax.ShapeDtypeStruct(lead + (length, width), BF16),
            jax.ShapeDtypeStruct((width, hidden), BF16),
            jax.ShapeDtypeStruct((hidden, width), BF16),
        ],
        in_specs=[vmem] * 6,
        out_specs=[vmem, hbm, hbm, vmem, vmem],
        scratch_shapes=[
            pltpu.VMEM((blocks, experts, slots * TILE), F32),
            pltpu.VMEM((2 * groups, experts, slots * TILE), F32),
            pltpu.VMEM((pos - 1, 2 * groups, experts, slots * TILE), F32),
            pltpu.VMEM(lead + (length, width), BF16),
            pltpu.VMEM(lead + (length, width), BF16),
            pltpu.VMEM((rows, hidden), BF16),
            pltpu.VMEM((rows, hidden), F32),
            pltpu.VMEM((rows, hidden), BF16),
            pltpu.VMEM((2, 2, length, width), BF16),
        ]
        + [
            pltpu.VMEM((2,) * (count - 1 - stage) + (length, width), BF16)
            for _ in range(4)
            for stage in range(count)
        ]
        + [
            pltpu.SemaphoreType.DMA((pos - 1,)),
            pltpu.SemaphoreType.DMA((pos - 1,)),
            pltpu.SemaphoreType.DMA((4 * count,)),
            pltpu.SemaphoreType.DMA((4 * count,)),
            pltpu.SemaphoreType.DMA((4 * count,)),
            pltpu.SemaphoreType.DMA((4 * count,)),
            pltpu.SemaphoreType.DMA((4,)),
        ],
        compiler_params=pltpu.CompilerParams(
            collective_id=2, has_side_effects=True, vmem_limit_bytes=62 * MIB
        ),
        name="mix_experts",
    )(h, cot, member, wc, win, wout)


def routing_kernel(
    pos, groups, y, dm, h, cot, share, member, mix, dh, dc, dw, local, gathered, send, recv
):
    row, place = lax.axis_index("dp"), lax.axis_index("pos")
    block = pl.program_id(0)
    units, _, width = y.shape
    blocks, experts, lanes = share.shape
    slots = lanes // TILE
    lane = lax.broadcasted_iota(jnp.int32, (experts, lanes), 1)

    @pl.when(block == 0)
    def _():
        greet([(row, lax.rem(place + step, pos)) for step in range(1, pos)])
        local[...] = jnp.zeros_like(local)

    part = share[block]
    weights, mask = block_weights(part, member, groups)
    yb = y[...].reshape(units * TILE, width)
    dmb = dm[...].reshape(units * TILE, width)
    mix[...] = (32.0 * dot(weights, yb, 0, 0)).astype(BF16).reshape(slots, TILE, width)
    dh[...] = dot(weights, dmb, 0, 0).astype(BF16).reshape(slots, TILE, width)
    whole = 32.0 * dot(yb, cot[...].reshape(lanes, width), 1, 1) + dot(
        dmb, h[...].reshape(lanes, width), 1, 1
    )
    picked = whole.reshape(experts, groups, TILE, lanes) * mask[None]
    grad = jnp.sum(jnp.sum(picked, axis=1), axis=1)
    dw[block] = grad
    here = lane // TILE == block
    for g in range(groups):
        inside = member[g : g + 1, :]
        local[g] = jnp.where(here, fold(inside * part * grad, jnp.add), local[g])

    @pl.when(block == blocks - 1)
    def _():
        exchange(local, gathered, send, recv, row, place, pos)
        for g in range(groups):
            total = local[g]
            for step in range(pos - 1):
                total = total + gathered[step, g]
            local[g] = total

        def last(b, carry):
            inner = jnp.zeros((experts, lanes), F32)
            for g in range(groups):
                inner = inner + member[g : g + 1, :] * spread(local[g], lane, b)
            dc[b] = (share[b] * (dw[b] - inner)).astype(BF16)
            return carry

        lax.fori_loop(0, blocks, last, 0)


def route_back(pos, groups, y, dm, h, cot, share, member):
    slots, length, width = h.shape
    units = y.shape[0]
    blocks, experts, lanes = share.shape
    per = lambda rows: pl.BlockSpec((rows, TILE, width), lambda b: (0, b, 0))
    whole = lambda a: pl.BlockSpec(a.shape, lambda b: (0,) * len(a.shape))
    return pl.pallas_call(
        lambda *refs: routing_kernel(pos, groups, *refs),
        grid=(blocks,),
        out_shape=[
            jax.ShapeDtypeStruct(h.shape, BF16),
            jax.ShapeDtypeStruct(h.shape, BF16),
            jax.ShapeDtypeStruct(share.shape, BF16),
        ],
        in_specs=[per(units), per(units), per(slots), per(slots), whole(share), whole(member)],
        out_specs=[per(slots), per(slots), whole(share)],
        scratch_shapes=[
            pltpu.VMEM(share.shape, F32),
            pltpu.VMEM((groups, experts, lanes), F32),
            pltpu.VMEM((pos - 1, groups, experts, lanes), F32),
            pltpu.SemaphoreType.DMA((pos - 1,)),
            pltpu.SemaphoreType.DMA((pos - 1,)),
        ],
        compiler_params=pltpu.CompilerParams(
            collective_id=3, has_side_effects=True, vmem_limit_bytes=40 * MIB
        ),
        name="route_back",
    )(y, dm, h, cot, share, member)


from jax.sharding import PartitionSpec as P

MIXED_SEQUENCES = 32


def body(
    inputs,
    cotangent,
    counts,
    seq_rank,
    first_gain,
    first_bias,
    query_weight,
    key_weight,
    value_weight,
    output_weight,
    second_gain,
    second_bias,
    control_weight,
    expert_in,
    expert_out,
):
    capacity, length, features = inputs.shape
    dp, pos = lax.axis_size("dp"), lax.axis_size("pos")
    experts = control_weight.shape[1]
    rows_in, hidden = expert_in.shape[1:]
    rows_out = expert_out.shape[1]
    copies = pos // experts
    groups = seq_rank.shape[1] // MIXED_SEQUENCES
    own = lax.axis_index("pos")

    row_counts = counts[0]
    place = jnp.arange(pos)
    count = jnp.sum(jnp.where(place == own, row_counts, 0))
    begin = jnp.sum(jnp.where(place < own, row_counts, 0))
    slot = jnp.arange(capacity)
    wanted = jnp.where(slot < count, begin + slot, -1)
    chosen = wanted[:, None] == jnp.arange(seq_rank.shape[1])[None, :]
    group_of = jnp.sum(jnp.where(chosen, seq_rank // MIXED_SEQUENCES + 1, 0), axis=1) - 1
    member = (jnp.repeat(group_of, TILE)[None, :] == jnp.arange(groups)[:, None]).astype(F32)
    count = count.reshape(1).astype(jnp.int32)

    small = jnp.concatenate(
        [
            jnp.stack([first_gain, first_bias, second_gain, second_bias], axis=1),
            jnp.zeros((features // (dp * pos), 4), BF16),
            control_weight,
            jnp.zeros((features // (dp * pos), 112), BF16),
        ],
        axis=1,
    )
    w_t, wk, wo, small = gather_weights(
        dp, pos, query_weight, key_weight, value_weight, output_weight, small
    )

    def whole_expert(shard):
        shard = jnp.repeat(shard, copies, axis=0) if copies > 1 else shard
        shard = lax.all_to_all(shard, "pos", split_axis=0, concat_axis=0, tiled=True)
        shard = shard.reshape(-1, shard.shape[-1])
        return lax.all_gather(shard, "dp", axis=0, tiled=True)

    win = whole_expert(expert_in)
    wout = whole_expert(expert_out)

    q_t, k, v_t, ctx_t, x1, h, lse = forward(count, inputs, w_t, wk, wo, small)
    share, y_all, dm_all, gin, gout = mix_experts(
        pos, groups, h, cotangent, member, small[8:], win, wout
    )
    units = experts * groups
    y_all = y_all.reshape(units, length, features)
    dm_all = dm_all.reshape(units, length, features)
    mix, dh, dc = route_back(pos, groups, y_all, dm_all, h, cotangent, share, member)
    dc = (
        dc.reshape(length // TILE, experts, capacity, TILE)
        .transpose(2, 1, 0, 3)
        .reshape(capacity, experts, length)
    )

    def expert_shard(grad, rows):
        grad = grad.reshape(dp, pos * rows, grad.shape[-1])
        grad = lax.all_to_all(grad, "dp", split_axis=0, concat_axis=0, tiled=True)
        grad = jnp.sum(grad.astype(F32), axis=0).astype(BF16).reshape(pos, rows, -1)
        grad = lax.all_to_all(grad, "pos", split_axis=0, concat_axis=0, tiled=True)
        return jnp.sum(grad.astype(F32).reshape(experts, copies, rows, -1), axis=1)

    expert_in_grad = expert_shard(gin, rows_in)
    expert_out_grad = expert_shard(gout, rows_out)

    layer_output, input_grad, grad_t, out_grad, vecs = backward(
        count, inputs, cotangent, x1, mix, dh, dc, q_t, k, v_t, ctx_t, lse, w_t, wo, small
    )
    shard = scatter_weights(dp, pos, grad_t, out_grad, vecs)
    tail = shard[:, 4 * features :]
    return (
        layer_output,
        input_grad,
        tail[:, 2],
        tail[:, 3],
        shard[:, :features],
        shard[:, features : 2 * features],
        shard[:, 2 * features : 3 * features],
        shard[:, 3 * features : 4 * features],
        tail[:, 0],
        tail[:, 1],
        tail[:, 8 : 8 + experts],
        expert_in_grad,
        expert_out_grad,
    )


def solution(mesh):
    both = ("dp", "pos")
    vector, matrix, cube = P(both), P(both, None), P(both, None, None)
    middle = P(None, both, None)
    return jax.shard_map(
        body,
        mesh=mesh,
        in_specs=(
            cube,
            cube,
            P("dp", None),
            P("dp", None),
            vector,
            vector,
            matrix,
            matrix,
            matrix,
            matrix,
            vector,
            vector,
            matrix,
            middle,
            middle,
        ),
        out_specs=(
            cube,
            cube,
            vector,
            vector,
            matrix,
            matrix,
            matrix,
            matrix,
            vector,
            vector,
            matrix,
            middle,
            middle,
        ),
        check_vma=False,
    )
```

```python
import math
import jax
import jax.numpy as jnp
from jax import lax
from jax.experimental import pallas as pl
from jax.experimental.pallas import tpu as pltpu

HEADS = 8
HEAD = 64
NORM_EPS = 1e-05
MASKED = -1e30
F32 = jnp.float32
BF16 = jnp.bfloat16
MIB = 1 << 20
VMEM_LIMIT = 62 * MIB


def dot(a, b, ca=1, cb=0):
    return lax.dot_general(a, b, (((ca,), (cb,)), ((), ())), preferred_element_type=F32)


def normalize(v):
    center = v - jnp.mean(v, axis=-1, keepdims=True)
    spread = jnp.mean(center * center, axis=-1, keepdims=True)
    scale = lax.rsqrt(spread + NORM_EPS)
    return center * scale, scale


def head_rows(array_t, head):
    rows = array_t[head * HEAD : (head + 1) * HEAD, :]
    zero = jnp.zeros_like(rows)
    return jnp.concatenate([rows, zero] if head % 2 == 0 else [zero, rows], axis=0)


def forward_kernel(count, x, w_t, wk, wo, small, q_t, k, v_t, ctx_t, x1, h, lse):
    g1, b1, g2, b2 = (small[i : i + 1] for i in range(4))
    slots, length, width = x.shape
    wq_t, wv_t = w_t.at[:width], w_t.at[2 * width :]
    half = length // 2
    causal = lax.broadcasted_iota(jnp.int32, (half, half), 0) <= lax.broadcasted_iota(
        jnp.int32, (half, half), 1
    )

    def one():
        source = x[...].reshape(slots * length, width).astype(F32)
        xhat, _ = normalize(source)
        a = (xhat * g1 + b1).astype(BF16)
        qs = (dot(wq_t[...], a, 1, 1).astype(BF16) * 0.125).astype(BF16)
        ks = dot(a, wk[...]).astype(BF16)
        vs = dot(wv_t[...], a, 1, 1).astype(BF16)
        k[...] = ks.reshape(slots, length, width)
        ones = jnp.ones((16, length), BF16)
        parts = [[] for _ in range(slots)]
        sums = [[] for _ in range(slots)]
        cols = [slice(s * length, (s + 1) * length) for s in range(slots)]
        for s in range(slots):
            q_t[s] = qs[:, cols[s]]
            v_t[s] = vs[:, cols[s]]
        for head in range(HEADS):
            for s in range(slots):
                pair = ks[cols[s], (head // 2) * 128 : (head // 2) * 128 + 128]
                st = dot(pair, head_rows(qs[:, cols[s]], head))
                s00 = jnp.where(causal, st[:half, :half], MASKED)
                s01 = st[:half, half:]
                s11 = jnp.where(causal, st[half:, half:], MASKED)
                m0 = jnp.max(s00, axis=0, keepdims=True)
                m1 = jnp.maximum(
                    jnp.max(s01, axis=0, keepdims=True), jnp.max(s11, axis=0, keepdims=True)
                )
                e00 = jnp.exp(s00 - m0).astype(BF16)
                e01 = jnp.exp(s01 - m1).astype(BF16)
                e11 = jnp.exp(s11 - m1).astype(BF16)
                et = jnp.concatenate(
                    [
                        jnp.concatenate([e00, e01], axis=1),
                        jnp.concatenate([jnp.zeros_like(e00), e11], axis=1),
                    ],
                    axis=0,
                )
                va = jnp.concatenate([vs[head * HEAD : (head + 1) * HEAD, cols[s]], ones], axis=0)
                full = dot(va, et)
                total = full[HEAD : HEAD + 1]
                parts[s].append((full[:HEAD] * (1.0 / total)).astype(BF16))
                sums[s].append(jnp.concatenate([m0, m1], axis=1) + jnp.log(total))
        outs = []
        for s in range(slots):
            ctx = jnp.concatenate(parts[s], axis=0)
            ctx_t[s] = ctx
            lse[s] = jnp.concatenate(sums[s], axis=0)
            outs.append(dot(ctx, wo[...], 0, 0))
        residual = source + jnp.concatenate(outs, axis=0)
        x1[...] = residual.reshape(slots, length, width)
        xhat2, _ = normalize(residual)
        h[...] = (xhat2 * g2 + b2).astype(BF16).reshape(slots, length, width)

    live = pl.program_id(0) * slots < count[0]
    pl.when(live)(one)

    @pl.when(jnp.logical_not(live))
    def _():
        h[...] = jnp.zeros((slots, length, width), BF16)


def forward(count, x, w_t, wk, wo, small, block=1):
    slots, length, width = x.shape
    per = lambda rows, cols: pl.BlockSpec((block, rows, cols), lambda i, c: (i, 0, 0))
    whole = lambda a: pl.BlockSpec(a.shape, lambda i, c: (0,) * a.ndim)
    shape = lambda rows, cols, kind: jax.ShapeDtypeStruct((slots, rows, cols), kind)
    return pl.pallas_call(
        forward_kernel,
        grid_spec=pltpu.PrefetchScalarGridSpec(
            num_scalar_prefetch=1,
            grid=(slots // block,),
            in_specs=[per(length, width)]
            + [whole(a) for a in (w_t, wk, wo, small)],
            out_specs=[
                per(width, length),
                per(length, width),
                per(width, length),
                per(width, length),
                per(length, width),
                per(length, width),
                per(HEADS, length),
            ],
        ),
        out_shape=[
            shape(width, length, BF16),
            shape(length, width, BF16),
            shape(width, length, BF16),
            shape(width, length, BF16),
            shape(length, width, F32),
            shape(length, width, BF16),
            shape(HEADS, length, F32),
        ],
        compiler_params=pltpu.CompilerParams(vmem_limit_bytes=VMEM_LIMIT),
        cost_estimate=pl.CostEstimate(
            flops=40_000_000_000, bytes_accessed=40 * MIB, transcendentals=8_000_000
        ),
        name="attention_forward",
    )(count, x, w_t, wk, wo, small)


def norm_back(grad, xhat, scale):
    return scale * (
        grad
        - jnp.mean(grad, axis=-1, keepdims=True)
        - xhat * jnp.mean(grad * xhat, axis=-1, keepdims=True)
    )


def backward_kernel(
    count, x, cot, x1, mix, dh, dc, q_t, k, v_t, ctx_t, lse, w_t, wo, small,
    lo, dx, grad_t, out_grad, vecs, back_t,
):
    slots, length, width = x.shape
    half = length // 2
    causal = lax.broadcasted_iota(jnp.int32, (half, half), 0) <= lax.broadcasted_iota(
        jnp.int32, (half, half), 1
    )
    step = pl.program_id(0)

    @pl.when(step == 0)
    def _():
        grad_t[...] = jnp.zeros_like(grad_t)
        out_grad[...] = jnp.zeros_like(out_grad)
        vecs[...] = jnp.zeros_like(vecs)

    g1, b1, g2, b2 = (small[i : i + 1] for i in range(4))
    router = small[8:16].astype(BF16)

    def one():
        tokens = slots * length
        cols = [slice(s * length, (s + 1) * length) for s in range(slots)]
        row = lax.broadcasted_iota(jnp.int32, (tokens, 1), 0) // length + step * slots
        live = row < count[0]
        keep = lambda v: v if slots == 1 else jnp.where(live, v, 0.0)
        residual = x1[...].reshape(tokens, width)
        xhat2, scale2 = normalize(residual)
        lo[...] = (
            keep(residual + mix[...].reshape(tokens, width).astype(F32))
            .astype(BF16)
            .reshape(slots, length, width)
        )
        hidden = (xhat2 * g2 + b2).astype(BF16)
        routed = []
        for s in range(slots):
            routed.append(dot(dc[s], router, 0, 0))
            vecs[8:16] += dot(dc[s], hidden[cols[s], :])
        grad_h = (
            (dh[...].reshape(tokens, width).astype(F32) + jnp.concatenate(routed, axis=0))
            .astype(BF16)
            .astype(F32)
        )
        vecs[0:1] += jnp.sum(grad_h * xhat2, axis=0, keepdims=True)
        vecs[1:2] += jnp.sum(grad_h, axis=0, keepdims=True)
        dx1 = keep(
            cot[...].reshape(tokens, width).astype(F32) + norm_back(grad_h * g2, xhat2, scale2)
        )
        datt = dx1.astype(BF16)
        dctx = dot(wo[...], datt, 1, 1).astype(BF16)
        partial = None
        for s in range(slots):
            term = dot(ctx_t[s], datt[cols[s], :])
            partial = term if partial is None else partial + term
        out_grad[...] += partial
        for s in range(slots):
            kt = jnp.transpose(k[s])
            vn = jnp.transpose(v_t[s])
            for head in range(HEADS):
                rows = slice(head * HEAD, (head + 1) * HEAD)
                pair = slice((head // 2) * 128, (head // 2) * 128 + 128)
                st = dot(k[s, :, pair], head_rows(q_t[s], head))
                stat = lse[s, head : head + 1, :]
                p00 = jnp.exp(jnp.where(causal, st[:half, :half], MASKED) - stat[:, :half])
                p01 = jnp.exp(st[:half, half:] - stat[:, half:])
                p11 = jnp.exp(jnp.where(causal, st[half:, half:], MASKED) - stat[:, half:])
                dctx_s = dctx[:, cols[s]]
                dp = dot(vn[:, pair], head_rows(dctx_s, head))
                inner = jnp.sum(
                    ctx_t[s, rows, :].astype(F32) * dctx_s[rows, :].astype(F32),
                    axis=0,
                    keepdims=True,
                )
                d00 = (p00 * (dp[:half, :half] - inner[:, :half])).astype(BF16)
                d01 = (p01 * (dp[:half, half:] - inner[:, half:])).astype(BF16)
                d11 = (p11 * (dp[half:, half:] - inner[:, half:])).astype(BF16)
                zero = jnp.zeros((half, half), BF16)

                def whole(c00, c01, c11):
                    return jnp.concatenate(
                        [
                            jnp.concatenate([c00, c01], axis=1),
                            jnp.concatenate([zero, c11], axis=1),
                        ],
                        axis=0,
                    )

                ds = whole(d00, d01, d11)
                pt = whole(p00.astype(BF16), p01.astype(BF16), p11.astype(BF16))
                dq = dot(kt[rows, :], ds) * 0.125
                dk = dot(q_t[s, rows, :], ds, 1, 1)
                dv = dot(dctx_s[rows, :], pt, 1, 1)
                back_t[rows, cols[s]] = dq.astype(BF16)
                back_t[width + head * HEAD : width + (head + 1) * HEAD, cols[s]] = dk.astype(BF16)
                back_t[2 * width + head * HEAD : 2 * width + (head + 1) * HEAD, cols[s]] = dv.astype(
                    BF16
                )
        source = x[...].reshape(tokens, width).astype(F32)
        xhat1, scale1 = normalize(source)
        a = (xhat1 * g1 + b1).astype(BF16)
        back = back_t[...]
        grad_t[...] += dot(back, a)
        da = dot(back, w_t[...], 0, 0)
        vecs[2:3] += jnp.sum(da * xhat1, axis=0, keepdims=True)
        vecs[3:4] += jnp.sum(da, axis=0, keepdims=True)
        dx[...] = (
            keep(dx1 + norm_back(da * g1, xhat1, scale1))
            .astype(BF16)
            .reshape(slots, length, width)
        )

    some = step * slots < count[0]
    pl.when(some)(one)

    @pl.when(jnp.logical_not(some))
    def _():
        dx[...] = jnp.zeros((slots, length, width), BF16)
        lo[...] = jnp.zeros((slots, length, width), BF16)


def backward(count, x, cot, x1, mix, dh, dc, q_t, k, v_t, ctx_t, lse, w_t, wo, small, block=1):
    slots, length, width = x.shape
    per = lambda a: pl.BlockSpec((block,) + a.shape[1:], lambda i, c: (i, 0, 0))
    whole = lambda a: pl.BlockSpec(a.shape, lambda i, c: (0,) * len(a.shape))
    outs = [
        jax.ShapeDtypeStruct((3 * width, width), F32),
        jax.ShapeDtypeStruct((width, width), F32),
        jax.ShapeDtypeStruct((16, width), F32),
    ]
    batched = (x, cot, x1, mix, dh, dc, q_t, k, v_t, ctx_t, lse)
    shared = (w_t, wo, small)
    return pl.pallas_call(
        backward_kernel,
        grid_spec=pltpu.PrefetchScalarGridSpec(
            num_scalar_prefetch=1,
            grid=(slots // block,),
            in_specs=[per(a) for a in batched] + [whole(a) for a in shared],
            out_specs=[per(x), per(x)] + [whole(a) for a in outs],
            scratch_shapes=[pltpu.VMEM((3 * width, block * length), BF16)],
        ),
        out_shape=[jax.ShapeDtypeStruct(x.shape, BF16)] * 2 + outs,
        compiler_params=pltpu.CompilerParams(vmem_limit_bytes=VMEM_LIMIT),
        cost_estimate=pl.CostEstimate(
            flops=100_000_000_000, bytes_accessed=60 * MIB, transcendentals=8_000_000
        ),
        name="attention_backward",
    )(count, *batched, *shared)


MESH = pl.DeviceIdType.MESH
TILE = 16


def bits_of(size):
    return size.bit_length() - 1


def orders(count):
    first = list(range(count))
    second = list(first)
    if count > 2:
        second[1], second[2] = second[2], second[1]
    return first, second


def greet(peers):
    barrier = pltpu.get_barrier_semaphore()
    for peer in peers:
        pl.semaphore_signal(barrier, inc=1, device_id=peer, device_id_type=MESH)
    pl.semaphore_wait(barrier, len(peers))


def my_bits(place, count):
    return [lax.rem(place // (1 << bit), 2) for bit in range(count)]


def across(place, bits, bit):
    return place + (1 - 2 * bits[bit]) * (1 << bit)


def pick(remaining, chosen):
    return tuple(chosen[bit] if bit in chosen else slice(None) for bit in remaining)


def remote(src, dst, send, recv, device):
    return pltpu.make_async_remote_copy(
        src_ref=src,
        dst_ref=dst,
        send_sem=send,
        recv_sem=recv,
        device_id=device,
        device_id_type=MESH,
    )


def gather_kernel(
    dp, pos, groups, slots,
    wq, wk, wv, wo, vectors, router, counts, ranks, ein, eout,
    w_t, wk_out, wo_out, vt, member, live, win, wout,
    held, zsend, zrecv, send, recv, esend, erecv, lsem,
):
    count = bits_of(pos)
    row, place = lax.axis_index("dp"), lax.axis_index("pos")
    bits = my_bits(place, count)
    others = [lax.rem(row + step, dp) for step in range(1, dp)]
    mates = [lax.rem(place + step, pos) for step in range(1, pos)]
    greet([(other, place) for other in others] + [(row, mate) for mate in mates])
    rows, width = wq.shape
    every = list(range(count))[::-1]
    here = pick(every, {bit: bits[bit] for bit in every})
    for index, weight in enumerate((wq, wk, wv, wo)):
        held[(row,) + here + (slice(None), slice(index * width, (index + 1) * width))] = weight[...]
    tall = jnp.concatenate(
        [
            vectors[...].astype(F32),
            jnp.zeros((8 - vectors.shape[0], rows), F32),
            router[...].astype(F32),
            jnp.zeros((120 - router.shape[0], rows), F32),
        ],
        axis=0,
    )
    square = jnp.concatenate([tall, jnp.zeros((128, 128 - rows), F32)], axis=1)
    held[(row,) + here + (slice(None), slice(4 * width, 4 * width + 128))] = jnp.transpose(square)[
        :rows
    ].astype(BF16)

    zcopies = []
    for step, other in enumerate(others):
        spot = held.at[(row,) + here]
        zcopies.append(remote(spot, spot, zsend.at[step], zrecv.at[step], (other, place)))
        zcopies[-1].start()

    first, second = orders(count)
    plans = (first[::-1], second[::-1])

    def push(block, stage):
        order = plans[block % 2]
        bit = order[stage]
        whose = lax.rem(row + dp - block, dp)
        spot = held.at[
            (whose,) + pick(every, {b: bits[b] for b in every if b not in order[:stage]})
        ]
        at = block * count + stage
        copy = remote(spot, spot, send.at[at], recv.at[at], (row, across(place, bits, bit)))
        copy.start()
        return copy

    flying = {0: push(0, 0)}
    copies = pos // ein.shape[0]
    ecopies = []
    for step, mate in enumerate(mates):
        for index, (src, dst) in enumerate(((ein, win), (eout, wout))):
            ecopies.append(
                remote(
                    src.at[mate // copies],
                    dst.at[place],
                    esend.at[2 * step + index],
                    erecv.at[2 * step + index],
                    (row, mate),
                )
            )
    local = [
        pltpu.make_async_copy(src.at[place // copies], dst.at[place], lsem.at[index])
        for index, (src, dst) in enumerate(((ein, win), (eout, wout)))
    ]
    for copy in local:
        copy.start()

    lanes = slots * TILE
    which = lax.broadcasted_iota(jnp.int32, (1, pos), 1)
    begin = jnp.sum(jnp.where(which < place, counts[...], 0), axis=1, keepdims=True)
    mine = jnp.sum(jnp.where(which == place, counts[...], 0), axis=1, keepdims=True)
    live[...] = jnp.broadcast_to(mine, live.shape)
    slot = lax.broadcasted_iota(jnp.int32, (1, lanes), 1) // TILE
    wanted = jnp.where(slot < mine, begin + slot, -1)
    table = (ranks[...] // 32).astype(F32) + 1.0
    size = table.shape[1]
    if size < 128:
        table = jnp.concatenate([table, jnp.zeros((1, 128 - size), F32)], axis=1)
    column = jnp.transpose(jnp.broadcast_to(table, (128, 128)))[:, :1]
    match = lax.broadcasted_iota(jnp.int32, (128, lanes), 0) == wanted
    ids = jnp.sum(jnp.where(match, column, 0.0), axis=0, keepdims=True)
    for g in range(groups):
        member[g : g + 1, :] = (ids == float(g + 1)).astype(F32)

    for block in range(1, dp):
        zcopies[block - 1].wait()
        flying[block] = push(block, 0)
    for stage in range(1, count):
        for block in range(dp):
            flying[block].wait()
            flying[block] = push(block, stage)
    for copy in ecopies:
        copy.start()
    for block in range(dp):
        flying[block].wait()
    full = held[...].reshape(dp * pos * rows, 4 * width + 128)
    for index in range(3):
        w_t[index * width : (index + 1) * width, :] = jnp.transpose(
            full[:, index * width : (index + 1) * width]
        )
    wk_out[...] = full[:, width : 2 * width]
    wo_out[...] = full[:, 3 * width : 4 * width]
    vt[...] = jnp.transpose(full[:, 4 * width :])[:16, :].astype(F32)
    for copy in local + ecopies:
        copy.wait()


def gather_weights(dp, pos, groups, slots, wq, wk, wv, wo, vectors, router, counts, ranks, ein, eout):
    rows, width = wq.shape
    whole = rows * dp * pos
    vmem = pl.BlockSpec(memory_space=pltpu.VMEM)
    hbm = pl.BlockSpec(memory_space=pl.ANY)
    count = bits_of(pos)
    dma = pltpu.SemaphoreType.DMA
    return pl.pallas_call(
        lambda *refs: gather_kernel(dp, pos, groups, slots, *refs),
        out_shape=[
            jax.ShapeDtypeStruct((3 * width, whole), BF16),
            jax.ShapeDtypeStruct((whole, width), BF16),
            jax.ShapeDtypeStruct((whole, width), BF16),
            jax.ShapeDtypeStruct((16, whole), F32),
            jax.ShapeDtypeStruct((groups, slots * TILE), F32),
            jax.ShapeDtypeStruct((1, 128), jnp.int32),
            jax.ShapeDtypeStruct((pos,) + ein.shape[1:], BF16),
            jax.ShapeDtypeStruct((pos,) + eout.shape[1:], BF16),
        ],
        in_specs=[vmem] * 8 + [hbm] * 2,
        out_specs=[vmem] * 6 + [hbm] * 2,
        scratch_shapes=[
            pltpu.VMEM((dp,) + (2,) * count + (rows, 4 * width + 128), BF16),
            dma((dp - 1,)),
            dma((dp - 1,)),
            dma((dp * count,)),
            dma((dp * count,)),
            dma((2 * (pos - 1),)),
            dma((2 * (pos - 1),)),
            dma((2,)),
        ],
        compiler_params=pltpu.CompilerParams(
            collective_id=0, has_side_effects=True, vmem_limit_bytes=VMEM_LIMIT
        ),
        name="gather_weights",
    )(wq, wk, wv, wo, vectors, router, counts, ranks, ein, eout)


def scatter_kernel(dp, pos, grad_t, out_grad, vecs, *rest):
    count = bits_of(pos)
    gins, gouts, rest = rest[:dp], rest[dp : 2 * dp], rest[2 * dp :]
    out, ein_out, eout_out, held, *rest = rest
    buffers, slots, rest = rest[: 2 * count], rest[2 * count], rest[2 * count + 1 :]
    send, recv, esend, erecv, ein_mine, ein_got, eout_mine, eout_got = rest
    row, place = lax.axis_index("dp"), lax.axis_index("pos")
    bits = my_bits(place, count)
    others = [lax.rem(row + step, dp) for step in range(1, dp)]
    mates = [lax.rem(place + step, pos) for step in range(1, pos)]
    greet([(other, place) for other in others] + [(row, mate) for mate in mates])
    width = out_grad.shape[1]
    ecopies = []
    for index, (parts, mine, got) in enumerate(
        ((gins, ein_mine, ein_got), (gouts, eout_mine, eout_got))
    ):
        total = parts[0][...].astype(F32)
        for part in parts[1:]:
            total = total + part[...].astype(F32)
        mine[...] = total.astype(BF16).reshape(mine.shape)
        for step, mate in enumerate(mates):
            at = index * (pos - 1) + step
            ecopies.append(
                remote(mine.at[mate], got.at[place], esend.at[at], erecv.at[at], (row, mate))
            )
            ecopies[-1].start()
        got[place] = mine[place]
    lead = held.shape[:-1]
    for index in range(3):
        held[..., index * width : (index + 1) * width] = (
            jnp.transpose(grad_t[index * width : (index + 1) * width, :])
            .astype(BF16)
            .reshape(lead + (width,))
        )
    held[..., 3 * width : 4 * width] = out_grad[...].astype(BF16).reshape(lead + (width,))
    tail = jnp.concatenate([vecs[...], jnp.zeros((112, vecs.shape[1]), F32)], axis=0)
    held[..., 4 * width :] = jnp.transpose(tail).astype(BF16).reshape(lead + (128,))
    used = 0
    halves = (slice(0, dp // 2), slice(dp // 2, dp))
    plans = orders(count)
    current = [held.at[half] for half in halves]
    remaining = [list(range(count))[::-1] for _ in halves]
    for stage in range(count):
        copies = []
        for side in range(2):
            bit = plans[side][stage]
            away = (slice(None),) + pick(remaining[side], {bit: 1 - bits[bit]})
            copies.append(
                remote(
                    current[side].at[away],
                    buffers[side * count + stage],
                    send.at[used],
                    recv.at[used],
                    (row, across(place, bits, bit)),
                )
            )
            used += 1
        for copy in copies:
            copy.start()
        for side in range(2):
            copies[side].wait()
            bit = plans[side][stage]
            near = (slice(None),) + pick(remaining[side], {bit: bits[bit]})
            target = buffers[side * count + stage]
            target[...] = (
                target[...].astype(F32) + current[side][near].astype(F32)
            ).astype(BF16)
            current[side] = target
            remaining[side] = [b for b in remaining[side] if b != bit]
    joined = jnp.concatenate([current[0][...], current[1][...]], axis=0)
    slots[1] = joined
    copies = []
    for step, other in enumerate(others):
        copies.append(
            remote(
                slots.at[1, other],
                slots.at[0, row],
                send.at[used],
                recv.at[used],
                (other, place),
            )
        )
        used += 1
        copies[-1].start()
    for copy in copies:
        copy.wait()
    total = slots[1, row].astype(F32)
    for other in others:
        total = total + slots[0, other].astype(F32)
    out[...] = total
    for copy in ecopies:
        copy.wait()
    for got, target in ((ein_got, ein_out), (eout_got, eout_out)):
        experts = target.shape[0]
        pieces = got[...].astype(F32).reshape((experts, pos // experts) + target.shape[1:])
        target[...] = jnp.sum(pieces, axis=1)


def scatter_weights(dp, pos, experts, grad_t, out_grad, vecs, gins, gouts):
    width = out_grad.shape[1]
    rows = out_grad.shape[0] // (dp * pos)
    wide = 4 * width + 128
    ein_shape = (gins[0].shape[0] // pos, gins[0].shape[1])
    eout_shape = (gouts[0].shape[0] // pos, gouts[0].shape[1])
    vmem = pl.BlockSpec(memory_space=pltpu.VMEM)
    count = bits_of(pos)
    total = dp - 1 + 2 * count
    return pl.pallas_call(
        lambda *refs: scatter_kernel(dp, pos, *refs),
        out_shape=[
            jax.ShapeDtypeStruct((rows, wide), F32),
            jax.ShapeDtypeStruct((experts,) + ein_shape, F32),
            jax.ShapeDtypeStruct((experts,) + eout_shape, F32),
        ],
        in_specs=[vmem] * (3 + 2 * dp),
        out_specs=[vmem] * 3,
        scratch_shapes=[pltpu.VMEM((dp,) + (2,) * count + (rows, wide), BF16)]
        + [
            pltpu.VMEM((dp // 2,) + (2,) * (count - 1 - stage) + (rows, wide), BF16)
            for _ in range(2)
            for stage in range(count)
        ]
        + [
            pltpu.VMEM((2, dp, rows, wide), BF16),
            pltpu.SemaphoreType.DMA((total,)),
            pltpu.SemaphoreType.DMA((total,)),
            pltpu.SemaphoreType.DMA((2 * (pos - 1),)),
            pltpu.SemaphoreType.DMA((2 * (pos - 1),)),
            pltpu.VMEM((pos,) + ein_shape, BF16),
            pltpu.VMEM((pos,) + ein_shape, BF16),
            pltpu.VMEM((pos,) + eout_shape, BF16),
            pltpu.VMEM((pos,) + eout_shape, BF16),
        ],
        compiler_params=pltpu.CompilerParams(
            collective_id=1, has_side_effects=True, vmem_limit_bytes=VMEM_LIMIT
        ),
        name="scatter_weights",
    )(grad_t, out_grad, vecs, *gins, *gouts)


def spread(packed, lane, block):
    chosen = jnp.where(lane // TILE == block, packed, 0.0)
    return fold(chosen, jnp.add)


def fold(values, combine):
    size = values.shape[-1]
    shift = TILE
    while shift < size:
        values = combine(values, pltpu.roll(values, shift, 1))
        shift *= 2
    return values


def block_weights(share, member, groups):
    experts, lanes = share.shape
    rounded = share.astype(BF16).astype(F32)
    spot = (
        lax.broadcasted_iota(jnp.int32, (TILE, lanes), 0)
        == lax.rem(lax.broadcasted_iota(jnp.int32, (TILE, lanes), 1), TILE)
    ).astype(F32)
    mask = jnp.stack([spot * member[g : g + 1, :] for g in range(groups)])
    full = rounded[:, None, None, :] * mask[None]
    return full.reshape(experts * groups * TILE, lanes).astype(BF16), mask


def exchange(local, gathered, send, recv, row, place, pos):
    copies = []
    for step in range(1, pos):
        copies.append(
            remote(
                local,
                gathered.at[step - 1],
                send.at[step - 1],
                recv.at[step - 1],
                (row, lax.rem(place + step, pos)),
            )
        )
        copies[-1].start()
    for copy in copies:
        copy.wait()


def expert_kernel(dp, pos, groups, h_in, cot_in, member, small, wout_in, *rest):
    count = bits_of(pos)
    wins, rest = rest[:dp], rest[dp:]
    share, y_all, dm_all, rest = rest[0], rest[1], rest[2], rest[3:]
    gins, gouts, rest = rest[:dp], rest[dp : 2 * dp], rest[2 * dp :]
    (h, cot, win, wout, logits, stats, gathered, m_part, dy_part, m_t, z, slope, du, own), rest = (
        rest[:14],
        rest[14:],
    )
    buffers, rest = rest[: 4 * count], rest[4 * count :]
    asend, arecv, bsend, brecv, csend, crecv, wsend, wrecv, lsem, isem = rest
    row, place = lax.axis_index("dp"), lax.axis_index("pos")
    bits = my_bits(place, count)
    slots, length, width = h.shape
    others = [lax.rem(row + step, dp) for step in range(1, dp)]

    loads = [
        pltpu.make_async_copy(h_in, h, isem.at[0]),
        pltpu.make_async_copy(cot_in, cot, isem.at[1]),
        pltpu.make_async_copy(wout_in, wout.at[row], isem.at[2]),
    ] + [
        pltpu.make_async_copy(part, win.at[lax.rem(row + dp - step, dp)], isem.at[3 + step])
        for step, part in enumerate(wins)
    ]
    for copy in loads:
        copy.start()
    greet(
        [(other, place) for other in others]
        + [(row, lax.rem(place + step, pos)) for step in range(1, pos)]
    )
    wcopies = [
        remote(wout_in, wout.at[row], wsend.at[step], wrecv.at[step], (other, place))
        for step, other in enumerate(others)
    ]
    for copy in wcopies:
        copy.start()

    blocks = length // TILE
    lanes = slots * TILE
    router = small[8:].astype(BF16)
    experts = router.shape[0]
    lane = lax.broadcasted_iota(jnp.int32, (experts, lanes), 1)
    stats[...] = jnp.zeros_like(stats)
    loads[0].wait()

    def first(block, carry):
        rows = h[:, pl.ds(pl.multiple_of(block * TILE, TILE), TILE), :].reshape(lanes, width)
        logit = dot(router, rows, 1, 1)
        logits[block] = logit
        for g in range(groups):
            inside = member[g : g + 1, :] > 0
            peak = fold(jnp.where(inside, logit, MASKED), jnp.maximum)
            total = fold(jnp.where(inside, jnp.exp(logit - peak), 0.0), jnp.add)
            here = lane // TILE == block
            stats[g] = jnp.where(here, peak, stats[g])
            stats[groups + g] = jnp.where(here, total, stats[groups + g])
        return carry

    lax.fori_loop(0, blocks, first, 0)
    exchange(stats, gathered, asend, arecv, row, place, pos)
    for g in range(groups):
        peak = stats[g]
        for step in range(pos - 1):
            peak = jnp.maximum(peak, gathered[step, g])
        total = stats[groups + g] * jnp.exp(stats[g] - peak)
        for step in range(pos - 1):
            total = total + gathered[step, groups + g] * jnp.exp(gathered[step, g] - peak)
        stats[g] = peak
        stats[groups + g] = 1.0 / total

    lead = (2,) * (count + 1)
    live = jnp.sum(member[...], axis=0, keepdims=True) > 0

    def mixture(block, carry):
        where = pl.ds(pl.multiple_of(block * TILE, TILE), TILE)
        rows = h[:, where, :].reshape(lanes, width)
        peak = jnp.zeros((experts, lanes), F32)
        scale = jnp.zeros((experts, lanes), F32)
        for g in range(groups):
            inside = member[g : g + 1, :]
            peak = peak + inside * spread(stats[g], lane, block)
            scale = scale + inside * spread(stats[groups + g], lane, block)
        part = jnp.exp(jnp.where(live, logits[block] - peak, MASKED)) * scale
        share[block] = part
        weights, _ = block_weights(part, member, groups)
        m_part[..., where, :] = dot(weights, rows).astype(BF16).reshape(lead + (TILE, width))
        return carry

    def gradient(block, carry):
        where = pl.ds(pl.multiple_of(block * TILE, TILE), TILE)
        grads = cot[:, where, :].reshape(lanes, width)
        weights, _ = block_weights(share[block], member, groups)
        dy_part[..., where, :] = (
            (32.0 * dot(weights, grads)).astype(BF16).reshape(lead + (TILE, width))
        )
        return carry

    plans = orders(count)
    every = list(range(count))[::-1]
    sources = (m_part, dy_part)
    targets = (y_all, dm_all)
    partner = lambda bit: (row, across(place, bits, bit))
    half = length // 2
    spans = (slice(0, half), slice(half, length))
    flying = {}

    def start(which, stage):
        for side in range(2):
            lane_of = 2 * which + side
            bit = plans[side][stage]
            left = [b for b in every if b not in plans[side][:stage]]
            away = pick(left, {bit: 1 - bits[bit]})
            src = (
                sources[which].at[away + (slice(None), spans[side])]
                if stage == 0
                else buffers[lane_of * count + stage - 1].at[away]
            )
            at = lane_of * count + stage
            flying[which, side] = remote(
                src, buffers[at], bsend.at[at], brecv.at[at], partner(bit)
            )

    def launch(which, side):
        flying[which, side].start()

    def finish(which, stage):
        for side in range(2):
            lane_of = 2 * which + side
            flying[which, side].wait()
            bit = plans[side][stage]
            left = [b for b in every if b not in plans[side][:stage]]
            near = pick(left, {bit: bits[bit]})
            target = buffers[lane_of * count + stage]
            if stage == 0:
                old = sources[which][near + (slice(None), spans[side])]
            else:
                old = buffers[lane_of * count + stage - 1][near]
            target[...] = (target[...].astype(F32) + old.astype(F32)).astype(BF16)

    def advance(which, stage):
        finish(which, stage)
        if stage + 1 < count:
            start(which, stage + 1)
            launch(which, 0)
            launch(which, 1)

    def final(which):
        return jnp.concatenate(
            [buffers[(2 * which + side) * count + count - 1][...] for side in range(2)], axis=1
        ).reshape(2 * length, width)

    lower, upper = blocks // 2, blocks
    start(0, 0)
    lax.fori_loop(0, lower, mixture, 0)
    launch(0, 0)
    lax.fori_loop(lower, upper, mixture, 0)
    launch(0, 1)
    loads[1].wait()
    start(1, 0)
    lax.fori_loop(0, lower, gradient, 0)
    launch(1, 0)
    lax.fori_loop(lower, upper, gradient, 0)
    launch(1, 1)

    mine = pick(every, {b: bits[b] for b in every})
    placed = {}

    def push(which, stage):
        for side in range(2):
            lane_of = 2 * which + side
            order = plans[side][::-1]
            bit = order[stage]
            spot = targets[which].at[
                pick(every, {b: bits[b] for b in every if b not in order[:stage]})
                + (slice(None), spans[side])
            ]
            at = lane_of * count + stage
            source = own.at[which, :, spans[side]] if stage == 0 else spot
            copy = remote(source, spot, csend.at[at], crecv.at[at], partner(bit))
            copy.start()
            flying[which, side] = copy

    def publish(which, value):
        own[which] = value.astype(BF16).reshape(2, length, width)
        copy = pltpu.make_async_copy(own.at[which], targets[which].at[mine], lsem.at[which])
        copy.start()
        placed[which] = copy
        push(which, 0)

    def relay(which, stage):
        for side in range(2):
            flying[which, side].wait()
        if stage == 0:
            placed[which].wait()
        if stage + 1 < count:
            push(which, stage + 1)

    for stage in range(count - 1):
        advance(0, stage)
    advance(1, 0)
    advance(0, count - 1)
    m = final(0)
    m_t[...] = jnp.transpose(m)
    for copy in loads[2:] + wcopies:
        copy.wait()
    hidden = win.shape[-1]
    up = win[...].reshape(width, hidden)
    down = wout.reshape(hidden, width)
    piece = hidden // dp
    y = jnp.zeros((2 * length, width), F32)
    root = math.sqrt(2 / math.pi)
    for c in range(0, hidden, piece):
        u = dot(m, up[:, c : c + piece])
        square = u * u
        t = jnp.tanh(u * (root + root * 0.044715 * square))
        gate = 0.5 * (1.0 + t)
        active = (u * gate).astype(BF16)
        z[:, c : c + piece] = active
        slope[:, c : c + piece] = gate + (u * gate) * (1.0 - t) * (
            root + 3 * root * 0.044715 * square
        )
        y = y + dot(active, down[c : c + piece, :])
    publish(0, y)
    for stage in range(1, count - 1):
        advance(1, stage)
    relay(0, 0)
    advance(1, count - 1)
    dy = final(1)
    dm = jnp.zeros((2 * length, width), F32)
    for c in range(0, hidden, piece):
        dz = dot(dy, down[c : c + piece, :], 1, 1).astype(BF16).astype(F32)
        grad = (dz * slope[:, c : c + piece]).astype(BF16)
        du[:, c : c + piece] = grad
        dm = dm + dot(grad, up[:, c : c + piece], 1, 1)
    publish(1, dm)
    for stage in range(1, count - 1):
        relay(0, stage)
    relay(1, 0)
    share_of = width // dp
    for step in range(dp):
        whose = lax.rem(row + step, dp)
        strip = m_t[pl.ds(pl.multiple_of(whose * share_of, share_of), share_of), :]
        for c in range(0, hidden, piece):
            gins[step][:, c : c + piece] = dot(strip, du[:, c : c + piece]).astype(BF16)
        gouts[step][...] = dot(
            z[:, pl.ds(pl.multiple_of(whose * piece, piece), piece)], dy, 0, 0
        ).astype(BF16)
    for stage in range(1, count - 1):
        relay(1, stage)
    relay(0, count - 1)
    relay(1, count - 1)


def mix_experts(dp, pos, groups, h, cot, member, small, wout_part, win_parts):
    slots, length, width = h.shape
    experts = small.shape[0] - 8
    lead = (2,) * (bits_of(pos) + 1)
    hidden = win_parts[0].shape[-1]
    blocks = length // TILE
    count = bits_of(pos)
    vmem = pl.BlockSpec(memory_space=pltpu.VMEM)
    hbm = pl.BlockSpec(memory_space=pl.ANY)
    rows = 2 * length
    dma = pltpu.SemaphoreType.DMA
    return pl.pallas_call(
        lambda *refs: expert_kernel(dp, pos, groups, *refs),
        out_shape=[
            jax.ShapeDtypeStruct((blocks, experts, slots * TILE), F32),
            jax.ShapeDtypeStruct(lead + (length, width), BF16),
            jax.ShapeDtypeStruct(lead + (length, width), BF16),
        ]
        + [jax.ShapeDtypeStruct((width // dp, hidden), BF16)] * dp
        + [jax.ShapeDtypeStruct((hidden // dp, width), BF16)] * dp,
        in_specs=[hbm, hbm, vmem, vmem, hbm] + [hbm] * dp,
        out_specs=[vmem, hbm, hbm] + [vmem] * (2 * dp),
        scratch_shapes=[
            pltpu.VMEM(h.shape, BF16),
            pltpu.VMEM(h.shape, BF16),
            pltpu.VMEM((dp,) + win_parts[0].shape, BF16),
            pltpu.VMEM((dp,) + wout_part.shape, BF16),
            pltpu.VMEM((blocks, experts, slots * TILE), F32),
            pltpu.VMEM((2 * groups, experts, slots * TILE), F32),
            pltpu.VMEM((pos - 1, 2 * groups, experts, slots * TILE), F32),
            pltpu.VMEM(lead + (length, width), BF16),
            pltpu.VMEM(lead + (length, width), BF16),
            pltpu.VMEM((width, rows), BF16),
            pltpu.VMEM((rows, hidden), BF16),
            pltpu.VMEM((rows, hidden), F32),
            pltpu.VMEM((rows, hidden), BF16),
            pltpu.VMEM((2, 2, length, width), BF16),
        ]
        + [
            pltpu.VMEM((2,) * (count - stage) + (length // 2, width), BF16)
            for _ in range(4)
            for stage in range(count)
        ]
        + [
            dma((pos - 1,)),
            dma((pos - 1,)),
            dma((4 * count,)),
            dma((4 * count,)),
            dma((4 * count,)),
            dma((4 * count,)),
            dma((dp - 1,)),
            dma((dp - 1,)),
            dma((2,)),
            dma((3 + dp,)),
        ],
        compiler_params=pltpu.CompilerParams(
            collective_id=2, has_side_effects=True, vmem_limit_bytes=VMEM_LIMIT
        ),
        name="mix_experts",
    )(h, cot, member, small, wout_part, *win_parts)


def routing_kernel(
    pos, groups, y, dm, h, cot, share, member, mix, dh, dc, dw, local, gathered, send, recv
):
    row, place = lax.axis_index("dp"), lax.axis_index("pos")
    block = pl.program_id(0)
    units, _, width = y.shape
    blocks, experts, lanes = share.shape
    slots = lanes // TILE
    lane = lax.broadcasted_iota(jnp.int32, (experts, lanes), 1)

    @pl.when(block == 0)
    def _():
        greet([(row, lax.rem(place + step, pos)) for step in range(1, pos)])
        local[...] = jnp.zeros_like(local)

    part = share[block]
    weights, mask = block_weights(part, member, groups)
    yb = y[...].reshape(units * TILE, width)
    dmb = dm[...].reshape(units * TILE, width)
    mix[...] = (32.0 * dot(weights, yb, 0, 0)).astype(BF16).reshape(slots, TILE, width)
    dh[...] = dot(weights, dmb, 0, 0).astype(BF16).reshape(slots, TILE, width)
    whole = 32.0 * dot(yb, cot[...].reshape(lanes, width), 1, 1) + dot(
        dmb, h[...].reshape(lanes, width), 1, 1
    )
    picked = whole.reshape(experts, groups, TILE, lanes) * mask[None]
    grad = jnp.sum(jnp.sum(picked, axis=1), axis=1)
    dw[block] = grad
    here = lane // TILE == block
    for g in range(groups):
        inside = member[g : g + 1, :]
        local[g] = jnp.where(here, fold(inside * part * grad, jnp.add), local[g])

    @pl.when(block == blocks - 1)
    def _():
        exchange(local, gathered, send, recv, row, place, pos)
        for g in range(groups):
            total = local[g]
            for step in range(pos - 1):
                total = total + gathered[step, g]
            local[g] = total

        def last(b, carry):
            inner = jnp.zeros((experts, lanes), F32)
            for g in range(groups):
                inner = inner + member[g : g + 1, :] * spread(local[g], lane, b)
            dc[b] = (share[b] * (dw[b] - inner)).astype(BF16)
            return carry

        lax.fori_loop(0, blocks, last, 0)


def route_back(pos, groups, y, dm, h, cot, share, member):
    slots, length, width = h.shape
    units = y.shape[0]
    blocks, experts, lanes = share.shape
    per = lambda rows: pl.BlockSpec((rows, TILE, width), lambda b: (0, b, 0))
    whole = lambda a: pl.BlockSpec(a.shape, lambda b: (0,) * len(a.shape))
    return pl.pallas_call(
        lambda *refs: routing_kernel(pos, groups, *refs),
        grid=(blocks,),
        out_shape=[
            jax.ShapeDtypeStruct(h.shape, BF16),
            jax.ShapeDtypeStruct(h.shape, BF16),
            jax.ShapeDtypeStruct(share.shape, BF16),
        ],
        in_specs=[per(units), per(units), per(slots), per(slots), whole(share), whole(member)],
        out_specs=[per(slots), per(slots), whole(share)],
        scratch_shapes=[
            pltpu.VMEM(share.shape, F32),
            pltpu.VMEM((groups, experts, lanes), F32),
            pltpu.VMEM((pos - 1, groups, experts, lanes), F32),
            pltpu.SemaphoreType.DMA((pos - 1,)),
            pltpu.SemaphoreType.DMA((pos - 1,)),
        ],
        compiler_params=pltpu.CompilerParams(
            collective_id=3, has_side_effects=True, vmem_limit_bytes=VMEM_LIMIT
        ),
        name="route_back",
    )(y, dm, h, cot, share, member)


from jax.sharding import PartitionSpec as P

MIXED_SEQUENCES = 32


def body(
    inputs,
    cotangent,
    counts,
    seq_rank,
    first_gain,
    first_bias,
    query_weight,
    key_weight,
    value_weight,
    output_weight,
    second_gain,
    second_bias,
    control_weight,
    expert_in,
    expert_out,
):
    capacity, length, features = inputs.shape
    dp, pos = lax.axis_size("dp"), lax.axis_size("pos")
    experts = control_weight.shape[1]
    groups = seq_rank.shape[1] // MIXED_SEQUENCES

    w_t, wk, wo, small, member, live, win, wout = gather_weights(
        dp,
        pos,
        groups,
        capacity,
        query_weight,
        key_weight,
        value_weight,
        output_weight,
        jnp.stack([first_gain, first_bias, second_gain, second_bias]),
        control_weight.T,
        counts,
        seq_rank,
        expert_in,
        expert_out,
    )
    count = live[0, :1]

    def send_rows(array, step):
        return lax.ppermute(array, "dp", [(i, (i + step) % dp) for i in range(dp)])

    wins = [win] + [send_rows(win, step) for step in range(1, dp)]
    q_t, k, v_t, ctx_t, x1, h, lse = forward(count, inputs, w_t, wk, wo, small)
    share, y_all, dm_all, *grads = mix_experts(
        dp, pos, groups, h, cotangent, member, small, wout, wins
    )
    grads = [
        [part if step == 0 else send_rows(part, step) for step, part in enumerate(parts)]
        for parts in (grads[:dp], grads[dp:])
    ]
    units = experts * groups
    y_all = y_all.reshape(units, length, features)
    dm_all = dm_all.reshape(units, length, features)
    mix, dh, dc = route_back(pos, groups, y_all, dm_all, h, cotangent, share, member)
    dc = (
        dc.reshape(length // TILE, experts, capacity, TILE)
        .transpose(2, 1, 0, 3)
        .reshape(capacity, experts, length)
    )

    layer_output, input_grad, grad_t, out_grad, vecs = backward(
        count, inputs, cotangent, x1, mix, dh, dc, q_t, k, v_t, ctx_t, lse, w_t, wo, small
    )
    shard, expert_in_grad, expert_out_grad = scatter_weights(
        dp, pos, experts, grad_t, out_grad, vecs, *grads
    )
    tail = shard[:, 4 * features :]
    return (
        layer_output,
        input_grad,
        tail[:, 2],
        tail[:, 3],
        shard[:, :features],
        shard[:, features : 2 * features],
        shard[:, 2 * features : 3 * features],
        shard[:, 3 * features : 4 * features],
        tail[:, 0],
        tail[:, 1],
        tail[:, 8 : 8 + experts],
        expert_in_grad,
        expert_out_grad,
    )


def solution(mesh):
    both = ("dp", "pos")
    vector, matrix, cube = P(both), P(both, None), P(both, None, None)
    middle = P(None, both, None)
    return jax.shard_map(
        body,
        mesh=mesh,
        in_specs=(
            cube,
            cube,
            P("dp", None),
            P("dp", None),
            vector,
            vector,
            matrix,
            matrix,
            matrix,
            matrix,
            vector,
            vector,
            matrix,
            middle,
            middle,
        ),
        out_specs=(
            cube,
            cube,
            vector,
            vector,
            matrix,
            matrix,
            matrix,
            matrix,
            vector,
            vector,
            matrix,
            middle,
            middle,
        ),
        check_vma=False,
    )
```

```python
import math
import jax
import jax.numpy as jnp
from jax import lax
from jax.experimental import pallas as pl
from jax.experimental.pallas import tpu as pltpu

HEADS = 8
HEAD = 64
NORM_EPS = 1e-05
MASKED = -1e30
F32 = jnp.float32
BF16 = jnp.bfloat16
MIB = 1 << 20
VMEM_LIMIT = 62 * MIB


def dot(a, b, ca=1, cb=0):
    return lax.dot_general(a, b, (((ca,), (cb,)), ((), ())), preferred_element_type=F32)


def normalize(v):
    center = v - jnp.mean(v, axis=-1, keepdims=True)
    spread = jnp.mean(center * center, axis=-1, keepdims=True)
    scale = lax.rsqrt(spread + NORM_EPS)
    return center * scale, scale


def spread_heads(parts):
    return jnp.concatenate(
        [
            jnp.concatenate(
                [part if i == j else jnp.zeros_like(part) for i in range(len(parts))], axis=0
            )
            for j, part in enumerate(parts)
        ],
        axis=1,
    )


def forward_kernel(count, x, w_t, wk, wo, small, q_t, k, v_t, ctx_t, x1, h, inverse, e_t, logits):
    g1, b1, g2, b2 = (small[i : i + 1] for i in range(4))
    slots, length, width = x.shape
    router = small[8:16].astype(BF16)
    wq_t, wv_t = w_t.at[:width], w_t.at[2 * width :]
    half = length // 2
    causal = lax.broadcasted_iota(jnp.int32, (half, half), 0) <= lax.broadcasted_iota(
        jnp.int32, (half, half), 1
    )

    def one():
        source = x[...].reshape(slots * length, width).astype(F32)
        xhat, _ = normalize(source)
        a = (xhat * g1 + b1).astype(BF16)
        qs = (dot(wq_t[...], a, 1, 1).astype(BF16) * 0.125).astype(BF16)
        ks = dot(a, wk[...]).astype(BF16)
        vs = dot(wv_t[...], a, 1, 1).astype(BF16)
        k[...] = ks.reshape(slots, length, width)
        ones = jnp.ones((16, length), BF16)
        parts = [[] for _ in range(slots)]
        sums = [[] for _ in range(slots)]
        cols = [slice(s * length, (s + 1) * length) for s in range(slots)]
        for s in range(slots):
            q_t[s] = qs[:, cols[s]]
            v_t[s] = vs[:, cols[s]]
        for base in range(0, HEADS, 4):
            for s in range(slots):
                four = slice(base * HEAD, (base + 4) * HEAD)
                spread_q = spread_heads(
                    [
                        qs[(base + i) * HEAD : (base + i + 1) * HEAD, cols[s]] for i in range(4)
                    ]
                )
                scores = dot(ks[cols[s], four], spread_q)
                exps = []
                for j in range(4):
                    st = scores[:, j * length : (j + 1) * length]
                    s00 = jnp.where(causal, st[:half, :half], MASKED)
                    s01 = st[:half, half:]
                    s11 = jnp.where(causal, st[half:, half:], MASKED)
                    m0 = jnp.max(s00, axis=0, keepdims=True)
                    m1 = jnp.maximum(
                        jnp.max(s01, axis=0, keepdims=True), jnp.max(s11, axis=0, keepdims=True)
                    )
                    e00 = jnp.exp(s00 - m0).astype(BF16)
                    e01 = jnp.exp(s01 - m1).astype(BF16)
                    e11 = jnp.exp(s11 - m1).astype(BF16)
                    et = jnp.concatenate(
                        [
                            jnp.concatenate([e00, e01], axis=1),
                            jnp.concatenate([jnp.zeros_like(e00), e11], axis=1),
                        ],
                        axis=0,
                    )
                    e_t[s, base + j] = et
                    exps.append(et)
                for j in range(0, 4, 2):
                    head = base + j
                    va = jnp.concatenate(
                        [
                            vs[head * HEAD : (head + 1) * HEAD, cols[s]],
                            ones,
                            vs[(head + 1) * HEAD : (head + 2) * HEAD, cols[s]],
                            ones,
                        ],
                        axis=0,
                    )
                    both = dot(va, jnp.concatenate(exps[j : j + 2], axis=1))
                    for i in range(2):
                        full = both[i * 80 : i * 80 + 80, i * length : (i + 1) * length]
                        total = full[HEAD : HEAD + 1]
                        scale = 1.0 / total
                        parts[s].append((full[:HEAD] * scale).astype(BF16))
                        sums[s].append(scale)
        outs = []
        for s in range(slots):
            ctx = jnp.concatenate(parts[s], axis=0)
            ctx_t[s] = ctx
            inverse[s] = jnp.concatenate(sums[s], axis=0)
            outs.append(dot(ctx, wo[...], 0, 0))
        residual = source + jnp.concatenate(outs, axis=0)
        x1[...] = residual.reshape(slots, length, width)
        xhat2, _ = normalize(residual)
        hidden = (xhat2 * g2 + b2).astype(BF16)
        h[...] = hidden.reshape(slots, length, width)
        for s in range(slots):
            logits[s] = dot(router, hidden[cols[s], :], 1, 1)

    live = pl.program_id(0) * slots < count[0]
    pl.when(live)(one)

    @pl.when(jnp.logical_not(live))
    def _():
        h[...] = jnp.zeros((slots, length, width), BF16)
        logits[...] = jnp.zeros_like(logits)


def forward(count, x, w_t, wk, wo, small, block=2):
    slots, length, width = x.shape
    per = lambda rows, cols: pl.BlockSpec((block, rows, cols), lambda i, c: (i, 0, 0))
    whole = lambda a: pl.BlockSpec(a.shape, lambda i, c: (0,) * a.ndim)
    shape = lambda rows, cols, kind: jax.ShapeDtypeStruct((slots, rows, cols), kind)
    return pl.pallas_call(
        forward_kernel,
        grid_spec=pltpu.PrefetchScalarGridSpec(
            num_scalar_prefetch=1,
            grid=(slots // block,),
            in_specs=[per(length, width)]
            + [whole(a) for a in (w_t, wk, wo, small)],
            out_specs=[
                per(width, length),
                per(length, width),
                per(width, length),
                per(width, length),
                per(length, width),
                per(length, width),
                per(HEADS, length),
            ]
            + [pl.BlockSpec((block, HEADS, length, length), lambda i, c: (i, 0, 0, 0)), per(HEADS, length)],
        ),
        out_shape=[
            shape(width, length, BF16),
            shape(length, width, BF16),
            shape(width, length, BF16),
            shape(width, length, BF16),
            shape(length, width, F32),
            shape(length, width, BF16),
            shape(HEADS, length, F32),
        ]
        + [jax.ShapeDtypeStruct((slots, HEADS, length, length), BF16), shape(8, length, F32)] ,
        compiler_params=pltpu.CompilerParams(vmem_limit_bytes=VMEM_LIMIT),
        cost_estimate=pl.CostEstimate(
            flops=40_000_000_000, bytes_accessed=40 * MIB, transcendentals=8_000_000
        ),
        name="attention_forward",
    )(count, x, w_t, wk, wo, small)


def norm_back(grad, xhat, scale):
    return scale * (
        grad
        - jnp.mean(grad, axis=-1, keepdims=True)
        - xhat * jnp.mean(grad * xhat, axis=-1, keepdims=True)
    )


def backward_kernel(
    count, x, cot, x1, mix, dh, dc, q_t, k, v_t, ctx_t, inverse, e_t, w_t, wo, small,
    lo, dx, grad_t, out_grad, vecs, back_t,
):
    slots, length, width = x.shape
    half = length // 2
    step = pl.program_id(0)

    @pl.when(step == 0)
    def _():
        grad_t[...] = jnp.zeros_like(grad_t)
        out_grad[...] = jnp.zeros_like(out_grad)
        vecs[...] = jnp.zeros_like(vecs)

    g1, b1, g2, b2 = (small[i : i + 1] for i in range(4))
    router = small[8:16].astype(BF16)

    def one():
        tokens = slots * length
        cols = [slice(s * length, (s + 1) * length) for s in range(slots)]
        row = lax.broadcasted_iota(jnp.int32, (tokens, 1), 0) // length + step * slots
        live = row < count[0]
        keep = lambda v: v if slots == 1 else jnp.where(live, v, 0.0)
        residual = x1[...].reshape(tokens, width)
        xhat2, scale2 = normalize(residual)
        lo[...] = (
            keep(residual + mix[...].reshape(tokens, width).astype(F32))
            .astype(BF16)
            .reshape(slots, length, width)
        )
        hidden = (xhat2 * g2 + b2).astype(BF16)
        routed = []
        for s in range(slots):
            routed.append(dot(dc[s], router, 0, 0))
            vecs[8:16] += dot(dc[s], hidden[cols[s], :])
        grad_h = (
            (dh[...].reshape(tokens, width).astype(F32) + jnp.concatenate(routed, axis=0))
            .astype(BF16)
            .astype(F32)
        )
        vecs[0:1] += jnp.sum(grad_h * xhat2, axis=0, keepdims=True)
        vecs[1:2] += jnp.sum(grad_h, axis=0, keepdims=True)
        dx1 = keep(
            cot[...].reshape(tokens, width).astype(F32) + norm_back(grad_h * g2, xhat2, scale2)
        )
        datt = dx1.astype(BF16)
        dctx = dot(wo[...], datt, 1, 1).astype(BF16)
        partial = None
        for s in range(slots):
            term = dot(ctx_t[s], datt[cols[s], :])
            partial = term if partial is None else partial + term
        out_grad[...] += partial
        zero = jnp.zeros((half, half), BF16)
        for s in range(slots):
            kt = jnp.transpose(k[s])
            vn = jnp.transpose(v_t[s])
            scaled = []
            inners = []
            for head in range(HEADS):
                rows = slice(head * HEAD, (head + 1) * HEAD)
                part = dctx[rows, cols[s]].astype(F32) * inverse[s, head : head + 1, :]
                scaled.append(part.astype(BF16))
                inners.append(jnp.sum(ctx_t[s, rows, :].astype(F32) * part, axis=0, keepdims=True))
            for base in range(0, HEADS, 4):
                four = slice(base * HEAD, (base + 4) * HEAD)
                dprobs = dot(vn[:, four], spread_heads(scaled[base : base + 4]))
                grads = []
                exps = []
                for j in range(4):
                    head = base + j
                    et = e_t[s, head]
                    dp = dprobs[:, j * length : (j + 1) * length]
                    inner = inners[head]
                    d00 = et[:half, :half].astype(F32) * (dp[:half, :half] - inner[:, :half])
                    d01 = et[:half, half:].astype(F32) * (dp[:half, half:] - inner[:, half:])
                    d11 = et[half:, half:].astype(F32) * (dp[half:, half:] - inner[:, half:])
                    grads.append(
                        jnp.concatenate(
                            [
                                jnp.concatenate([d00.astype(BF16), d01.astype(BF16)], axis=1),
                                jnp.concatenate([zero, d11.astype(BF16)], axis=1),
                            ],
                            axis=0,
                        )
                    )
                    exps.append(et)
                tall = jnp.concatenate(grads, axis=0)
                dk = dot(q_t[s, four, :], tall, 1, 1)
                dv = dot(
                    jnp.concatenate(scaled[base : base + 4], axis=0),
                    jnp.concatenate(exps, axis=0),
                    1,
                    1,
                )
                dq = [
                    dot(
                        kt[(base + j) * HEAD : (base + j + 2) * HEAD, :],
                        jnp.concatenate(grads[j : j + 2], axis=1),
                    )
                    * 0.125
                    for j in range(0, 4, 2)
                ]
                for j in range(4):
                    begin = (base + j) * HEAD
                    spot = slice(j * length, (j + 1) * length)
                    inside = slice(j * HEAD, (j + 1) * HEAD)
                    i = j % 2
                    back_t[begin : begin + HEAD, cols[s]] = dq[j // 2][
                        i * HEAD : (i + 1) * HEAD, i * length : (i + 1) * length
                    ].astype(BF16)
                    back_t[width + begin : width + begin + HEAD, cols[s]] = dk[inside, spot].astype(
                        BF16
                    )
                    back_t[2 * width + begin : 2 * width + begin + HEAD, cols[s]] = dv[
                        inside, spot
                    ].astype(BF16)
        source = x[...].reshape(tokens, width).astype(F32)
        xhat1, scale1 = normalize(source)
        a = (xhat1 * g1 + b1).astype(BF16)
        back = back_t[...]
        grad_t[...] += dot(back, a)
        da = dot(back, w_t[...], 0, 0)
        vecs[2:3] += jnp.sum(da * xhat1, axis=0, keepdims=True)
        vecs[3:4] += jnp.sum(da, axis=0, keepdims=True)
        dx[...] = (
            keep(dx1 + norm_back(da * g1, xhat1, scale1))
            .astype(BF16)
            .reshape(slots, length, width)
        )

    some = step * slots < count[0]
    pl.when(some)(one)

    @pl.when(jnp.logical_not(some))
    def _():
        dx[...] = jnp.zeros((slots, length, width), BF16)
        lo[...] = jnp.zeros((slots, length, width), BF16)


def backward(count, x, cot, x1, mix, dh, dc, q_t, k, v_t, ctx_t, inverse, e_t, w_t, wo, small, block=2):
    slots, length, width = x.shape
    per = lambda a: pl.BlockSpec(
        (block,) + a.shape[1:], lambda i, c: (i,) + (0,) * (len(a.shape) - 1)
    )
    whole = lambda a: pl.BlockSpec(a.shape, lambda i, c: (0,) * len(a.shape))
    outs = [
        jax.ShapeDtypeStruct((3 * width, width), F32),
        jax.ShapeDtypeStruct((width, width), F32),
        jax.ShapeDtypeStruct((16, width), F32),
    ]
    batched = (x, cot, x1, mix, dh, dc, q_t, k, v_t, ctx_t, inverse, e_t)
    shared = (w_t, wo, small)
    return pl.pallas_call(
        backward_kernel,
        grid_spec=pltpu.PrefetchScalarGridSpec(
            num_scalar_prefetch=1,
            grid=(slots // block,),
            in_specs=[per(a) for a in batched] + [whole(a) for a in shared],
            out_specs=[per(x), per(x)] + [whole(a) for a in outs],
            scratch_shapes=[pltpu.VMEM((3 * width, block * length), BF16)],
        ),
        out_shape=[jax.ShapeDtypeStruct(x.shape, BF16)] * 2 + outs,
        compiler_params=pltpu.CompilerParams(vmem_limit_bytes=VMEM_LIMIT),
        cost_estimate=pl.CostEstimate(
            flops=100_000_000_000, bytes_accessed=60 * MIB, transcendentals=8_000_000
        ),
        name="attention_backward",
    )(count, *batched, *shared)


MESH = pl.DeviceIdType.MESH
TILE = 16


def bits_of(size):
    return size.bit_length() - 1


def orders(count):
    first = list(range(count))
    second = list(first)
    if count > 2:
        second[1], second[2] = second[2], second[1]
    return first, second


def greet(peers):
    barrier = pltpu.get_barrier_semaphore()
    for peer in peers:
        pl.semaphore_signal(barrier, inc=1, device_id=peer, device_id_type=MESH)
    pl.semaphore_wait(barrier, len(peers))


def my_bits(place, count):
    return [lax.rem(place // (1 << bit), 2) for bit in range(count)]


def across(place, bits, bit):
    return place + (1 - 2 * bits[bit]) * (1 << bit)


def pick(remaining, chosen):
    return tuple(chosen[bit] if bit in chosen else slice(None) for bit in remaining)


def remote(src, dst, send, recv, device):
    return pltpu.make_async_remote_copy(
        src_ref=src,
        dst_ref=dst,
        send_sem=send,
        recv_sem=recv,
        device_id=device,
        device_id_type=MESH,
    )


def gather_kernel(
    dp, pos, groups, slots,
    wq, wk, wv, wo, vectors, router, counts, ranks, ein,
    w_t, wk_out, wo_out, vt, member, member_s, live, win,
    held, zsend, zrecv, send, recv, esend, erecv, lsem,
):
    count = bits_of(pos)
    row, place = lax.axis_index("dp"), lax.axis_index("pos")
    bits = my_bits(place, count)
    others = [lax.rem(row + step, dp) for step in range(1, dp)]
    mates = [lax.rem(place + step, pos) for step in range(1, pos)]
    greet([(other, place) for other in others] + [(row, mate) for mate in mates])
    rows, width = wq.shape
    every = list(range(count))[::-1]
    here = pick(every, {bit: bits[bit] for bit in every})
    for index, weight in enumerate((wq, wk, wv, wo)):
        held[(row,) + here + (slice(None), slice(index * width, (index + 1) * width))] = weight[...]
    tall = jnp.concatenate(
        [
            vectors[...].astype(F32),
            jnp.zeros((8 - vectors.shape[0], rows), F32),
            router[...].astype(F32),
            jnp.zeros((120 - router.shape[0], rows), F32),
        ],
        axis=0,
    )
    square = jnp.concatenate([tall, jnp.zeros((128, 128 - rows), F32)], axis=1)
    held[(row,) + here + (slice(None), slice(4 * width, 4 * width + 128))] = jnp.transpose(square)[
        :rows
    ].astype(BF16)

    copies = pos // ein.shape[0]
    local = pltpu.make_async_copy(ein.at[place // copies], win.at[place], lsem.at[0])
    local.start()
    zcopies = []
    for step, other in enumerate(others):
        spot = held.at[(row,) + here]
        zcopies.append(remote(spot, spot, zsend.at[step], zrecv.at[step], (other, place)))
        zcopies[-1].start()

    ecopies = []
    for step, mate in enumerate(mates):
        ecopies.append(
            remote(
                ein.at[mate // copies], win.at[place], esend.at[step], erecv.at[step], (row, mate)
            )
        )
        ecopies[-1].start()

    first, second = orders(count)
    plans = (first[::-1], second[::-1])

    def push(block, stage):
        order = plans[block % 2]
        bit = order[stage]
        whose = lax.rem(row + dp - block, dp)
        spot = held.at[
            (whose,) + pick(every, {b: bits[b] for b in every if b not in order[:stage]})
        ]
        at = block * count + stage
        copy = remote(spot, spot, send.at[at], recv.at[at], (row, across(place, bits, bit)))
        copy.start()
        return copy

    flying = {0: push(0, 0)}
    lanes = slots * TILE
    which = lax.broadcasted_iota(jnp.int32, (1, pos), 1)
    begin = jnp.sum(jnp.where(which < place, counts[...], 0), axis=1, keepdims=True)
    mine = jnp.sum(jnp.where(which == place, counts[...], 0), axis=1, keepdims=True)
    live[...] = jnp.broadcast_to(mine, live.shape)
    slot = lax.broadcasted_iota(jnp.int32, (1, lanes), 1) // TILE
    wanted = jnp.where(slot < mine, begin + slot, -1)
    table = (ranks[...] // 32).astype(F32) + 1.0
    size = table.shape[1]
    if size < 128:
        table = jnp.concatenate([table, jnp.zeros((1, 128 - size), F32)], axis=1)
    column = jnp.transpose(jnp.broadcast_to(table, (128, 128)))[:, :1]
    match = lax.broadcasted_iota(jnp.int32, (128, lanes), 0) == wanted
    ids = jnp.sum(jnp.where(match, column, 0.0), axis=0, keepdims=True)
    for g in range(groups):
        member[g : g + 1, :] = (ids == float(g + 1)).astype(F32)
    slot = lax.broadcasted_iota(jnp.int32, (slots, 1), 0)
    wanted = jnp.where(slot < mine, begin + slot, -1)
    match = lax.broadcasted_iota(jnp.int32, (slots, 128), 1) == wanted
    ids = jnp.sum(jnp.where(match, table, 0.0), axis=1, keepdims=True)
    for g in range(groups):
        member_s[g] = jnp.broadcast_to((ids == float(g + 1)).astype(F32), member_s.shape[1:])

    for block in range(1, dp):
        zcopies[block - 1].wait()
        flying[block] = push(block, 0)
    for stage in range(1, count):
        for block in range(dp):
            flying[block].wait()
            flying[block] = push(block, stage)
    for block in range(dp):
        flying[block].wait()
    full = held[...].reshape(dp * pos * rows, 4 * width + 128)
    for index in range(3):
        w_t[index * width : (index + 1) * width, :] = jnp.transpose(
            full[:, index * width : (index + 1) * width]
        )
    wk_out[...] = full[:, width : 2 * width]
    wo_out[...] = full[:, 3 * width : 4 * width]
    vt[...] = jnp.transpose(full[:, 4 * width :])[:16, :].astype(F32)
    for copy in [local] + ecopies:
        copy.wait()


def gather_weights(dp, pos, groups, slots, wq, wk, wv, wo, vectors, router, counts, ranks, ein):
    rows, width = wq.shape
    whole = rows * dp * pos
    vmem = pl.BlockSpec(memory_space=pltpu.VMEM)
    hbm = pl.BlockSpec(memory_space=pl.ANY)
    count = bits_of(pos)
    dma = pltpu.SemaphoreType.DMA
    return pl.pallas_call(
        lambda *refs: gather_kernel(dp, pos, groups, slots, *refs),
        out_shape=[
            jax.ShapeDtypeStruct((3 * width, whole), BF16),
            jax.ShapeDtypeStruct((whole, width), BF16),
            jax.ShapeDtypeStruct((whole, width), BF16),
            jax.ShapeDtypeStruct((16, whole), F32),
            jax.ShapeDtypeStruct((groups, slots * TILE), F32),
            jax.ShapeDtypeStruct((groups, slots, slots * TILE), F32),
            jax.ShapeDtypeStruct((1, 128), jnp.int32),
            jax.ShapeDtypeStruct((pos,) + ein.shape[1:], BF16),
        ],
        in_specs=[vmem] * 8 + [hbm],
        out_specs=[vmem] * 7 + [hbm],
        scratch_shapes=[
            pltpu.VMEM((dp,) + (2,) * count + (rows, 4 * width + 128), BF16),
            dma((dp - 1,)),
            dma((dp - 1,)),
            dma((dp * count,)),
            dma((dp * count,)),
            dma((pos - 1,)),
            dma((pos - 1,)),
            dma((1,)),
        ],
        compiler_params=pltpu.CompilerParams(
            collective_id=0, has_side_effects=True, vmem_limit_bytes=VMEM_LIMIT
        ),
        name="gather_weights",
    )(wq, wk, wv, wo, vectors, router, counts, ranks, ein)


def scatter_kernel(dp, pos, grad_t, out_grad, vecs, *rest):
    count = bits_of(pos)
    gins, gouts, rest = rest[:3], rest[3:6], rest[6:]
    out, ein_got, eout_got, held, *rest = rest
    buffers, slots, rest = rest[: 2 * count], rest[2 * count], rest[2 * count + 1 :]
    send, recv, esend, erecv, ein_mine, eout_mine = rest
    row, place = lax.axis_index("dp"), lax.axis_index("pos")
    bits = my_bits(place, count)
    others = [lax.rem(row + step, dp) for step in range(1, dp)]
    mates = [lax.rem(place + step, pos) for step in range(1, pos)]
    greet([(other, place) for other in others] + [(row, mate) for mate in mates])
    width = out_grad.shape[1]
    ecopies = []
    for index, (parts, mine, got) in enumerate(
        ((gins, ein_mine, ein_got), (gouts, eout_mine, eout_got))
    ):
        total = parts[0][...].astype(F32)
        for part in parts[1:]:
            total = total + part[...].astype(F32)
        mine[...] = total.astype(BF16).reshape(mine.shape)
        for step, mate in enumerate(mates):
            at = index * (pos - 1) + step
            ecopies.append(
                remote(mine.at[mate], got.at[place], esend.at[at], erecv.at[at], (row, mate))
            )
            ecopies[-1].start()
        got[place] = mine[place]
    lead = held.shape[:-1]
    for index in range(3):
        held[..., index * width : (index + 1) * width] = (
            jnp.transpose(grad_t[index * width : (index + 1) * width, :])
            .astype(BF16)
            .reshape(lead + (width,))
        )
    held[..., 3 * width : 4 * width] = out_grad[...].astype(BF16).reshape(lead + (width,))
    tail = jnp.concatenate([vecs[...], jnp.zeros((112, vecs.shape[1]), F32)], axis=0)
    held[..., 4 * width :] = jnp.transpose(tail).astype(BF16).reshape(lead + (128,))
    used = 0
    halves = (slice(0, dp // 2), slice(dp // 2, dp))
    plans = orders(count)
    current = [held.at[half] for half in halves]
    remaining = [list(range(count))[::-1] for _ in halves]
    for stage in range(count):
        copies = []
        for side in range(2):
            bit = plans[side][stage]
            away = (slice(None),) + pick(remaining[side], {bit: 1 - bits[bit]})
            copies.append(
                remote(
                    current[side].at[away],
                    buffers[side * count + stage],
                    send.at[used],
                    recv.at[used],
                    (row, across(place, bits, bit)),
                )
            )
            used += 1
        for copy in copies:
            copy.start()
        for side in range(2):
            copies[side].wait()
            bit = plans[side][stage]
            near = (slice(None),) + pick(remaining[side], {bit: bits[bit]})
            target = buffers[side * count + stage]
            target[...] = (
                target[...].astype(F32) + current[side][near].astype(F32)
            ).astype(BF16)
            current[side] = target
            remaining[side] = [b for b in remaining[side] if b != bit]
    joined = jnp.concatenate([current[0][...], current[1][...]], axis=0)
    slots[1] = joined
    copies = []
    for step, other in enumerate(others):
        copies.append(
            remote(
                slots.at[1, other],
                slots.at[0, row],
                send.at[used],
                recv.at[used],
                (other, place),
            )
        )
        used += 1
        copies[-1].start()
    for copy in copies:
        copy.wait()
    total = slots[1, row].astype(F32)
    for other in others:
        total = total + slots[0, other].astype(F32)
    out[...] = total
    for copy in ecopies:
        copy.wait()


def scatter_weights(dp, pos, grad_t, out_grad, vecs, gins, gouts):
    width = out_grad.shape[1]
    rows = out_grad.shape[0] // (dp * pos)
    wide = 4 * width + 128
    ein_shape = (gins[0].shape[0] // pos, gins[0].shape[1])
    eout_shape = (gouts[0].shape[0] // pos, gouts[0].shape[1])
    vmem = pl.BlockSpec(memory_space=pltpu.VMEM)
    count = bits_of(pos)
    total = dp - 1 + 2 * count
    return pl.pallas_call(
        lambda *refs: scatter_kernel(dp, pos, *refs),
        out_shape=[
            jax.ShapeDtypeStruct((rows, wide), F32),
            jax.ShapeDtypeStruct((pos,) + ein_shape, BF16),
            jax.ShapeDtypeStruct((pos,) + eout_shape, BF16),
        ],
        in_specs=[vmem] * 9,
        out_specs=[vmem] * 3,
        scratch_shapes=[pltpu.VMEM((dp,) + (2,) * count + (rows, wide), BF16)]
        + [
            pltpu.VMEM((dp // 2,) + (2,) * (count - 1 - stage) + (rows, wide), BF16)
            for _ in range(2)
            for stage in range(count)
        ]
        + [
            pltpu.VMEM((2, dp, rows, wide), BF16),
            pltpu.SemaphoreType.DMA((total,)),
            pltpu.SemaphoreType.DMA((total,)),
            pltpu.SemaphoreType.DMA((2 * (pos - 1),)),
            pltpu.SemaphoreType.DMA((2 * (pos - 1),)),
            pltpu.VMEM((pos,) + ein_shape, BF16),
            pltpu.VMEM((pos,) + eout_shape, BF16),
        ],
        compiler_params=pltpu.CompilerParams(
            collective_id=1, has_side_effects=True, vmem_limit_bytes=VMEM_LIMIT
        ),
        name="scatter_weights",
    )(grad_t, out_grad, vecs, *gins, *gouts)


def turn(parts):
    size = len(parts)
    lanes = parts[0].shape[1]
    tile = lax.broadcasted_iota(jnp.int32, parts[0].shape, 1) // TILE
    step = 1
    while step < size:
        low = lax.rem(tile // step, 2) == 0
        new = list(parts)
        for i in range(size):
            if i & step == 0:
                upper, lower = parts[i], parts[i | step]
                new[i] = jnp.where(low, upper, pltpu.roll(lower, step * TILE, 1))
                new[i | step] = jnp.where(low, pltpu.roll(upper, lanes - step * TILE, 1), lower)
        parts = new
        step *= 2
    return parts


def block_weights(share, member, groups):
    experts, lanes = share.shape
    rounded = share.astype(BF16).astype(F32)
    spot = (
        lax.broadcasted_iota(jnp.int32, (TILE, lanes), 0)
        == lax.rem(lax.broadcasted_iota(jnp.int32, (TILE, lanes), 1), TILE)
    ).astype(F32)
    mask = jnp.stack([spot * member[g : g + 1, :] for g in range(groups)])
    full = rounded[:, None, None, :] * mask[None]
    return full.reshape(experts * groups * TILE, lanes).astype(BF16), mask


def exchange(local, gathered, send, recv, row, place, pos):
    copies = []
    for step in range(1, pos):
        copies.append(
            remote(
                local,
                gathered.at[step - 1],
                send.at[step - 1],
                recv.at[step - 1],
                (row, lax.rem(place + step, pos)),
            )
        )
        copies[-1].start()
    for copy in copies:
        copy.wait()


def expert_kernel(dp, pos, groups, h_in, cot_in, logits, member, member_s, wout_in, *rest):
    count = bits_of(pos)
    wins, rest = rest[:3], rest[3:]
    share, share_s, y_all, dm_all, rest = rest[0], rest[1], rest[2], rest[3], rest[4:]
    gins, gouts, rest = rest[:dp], rest[dp : 2 * dp], rest[2 * dp :]
    (h, win, wout, stats, gathered, m_part, dy_part, m_t, z, slope, du, own), rest = (
        rest[:12],
        rest[12:],
    )
    ring_in, rest = rest[:2], rest[2:]
    buffers, rest = rest[: 4 * count], rest[4 * count :]
    asend, arecv, bsend, brecv, csend, crecv, psend, precv, wsend, wrecv, gsend, grecv, lsem, isem = (
        rest
    )
    row, place = lax.axis_index("dp"), lax.axis_index("pos")
    bits = my_bits(place, count)
    slots, length, width = h.shape
    right, left = lax.rem(row + 1, dp), lax.rem(row + dp - 1, dp)
    mates = [lax.rem(place + step, pos) for step in range(1, pos)]
    copies = pos // wout_in.shape[0]
    loads = [
        pltpu.make_async_copy(h_in, h, isem.at[0]),
        pltpu.make_async_copy(wout_in.at[place // copies], wout.at[row, place], isem.at[1]),
    ]
    middle = wout.shape[1] // 2
    halves = (slice(0, middle), slice(middle, 2 * middle))
    for step, part in enumerate(wins):
        loads.append(
            pltpu.make_async_copy(part, win.at[(row, left, right)[step]], isem.at[2 + step])
        )
    for copy in loads:
        copy.start()
    greet([(right, place), (left, place)] + [(row, mate) for mate in mates])
    pcopies = [
        remote(
            wout_in.at[mate // copies],
            wout.at[row, place],
            psend.at[step],
            precv.at[step],
            (row, mate),
        )
        for step, mate in enumerate(mates)
    ]

    for copy in pcopies:
        copy.start()

    def ring(which, distance):
        array = (win, wout)[which]
        sent = []
        for way, other in enumerate((right, left)):
            back = (distance - 1) * (1 - 2 * way)
            spot = (lax.rem(row + 2 * dp - back, dp),)
            if 2 * distance == dp:
                spot = spot + (halves[way],)
            at = (which * dp // 2 + distance - 1) * 2 + way
            sent.append(
                remote(array.at[spot], array.at[spot], wsend.at[at], wrecv.at[at], (other, place))
            )
            sent[-1].start()
        return sent

    def ring_on(which, first, passed):
        for distance in range(first, dp // 2 + 1):
            for copy in passed:
                copy.wait()
            passed = ring(which, distance)
        return passed

    win_ring = ring_on(0, 2, loads[2:])
    blocks = length // TILE
    lanes = slots * TILE
    experts = logits.shape[1]
    inside = [[member_s[g, s : s + 1, :] for s in range(slots)] for g in range(groups)]
    for g in range(groups):
        peak = jnp.full((experts, length), MASKED, F32)
        for s in range(slots):
            peak = jnp.maximum(peak, jnp.where(inside[g][s] > 0, logits[s], MASKED))
        total = jnp.zeros((experts, length), F32)
        for s in range(slots):
            total = total + jnp.where(inside[g][s] > 0, jnp.exp(logits[s] - peak), 0.0)
        stats[g] = peak
        stats[groups + g] = total
    exchange(stats, gathered, asend, arecv, row, place, pos)
    for copy in pcopies + loads[1:2]:
        copy.wait()
    wout_ring = ring(1, 1)
    for g in range(groups):
        peak = stats[g]
        for step in range(pos - 1):
            peak = jnp.maximum(peak, gathered[step, g])
        total = stats[groups + g] * jnp.exp(stats[g] - peak)
        for step in range(pos - 1):
            total = total + gathered[step, groups + g] * jnp.exp(gathered[step, g] - peak)
        stats[g] = peak
        stats[groups + g] = 1.0 / total
    parts = []
    for s in range(slots):
        peak = jnp.zeros((experts, length), F32)
        scale = jnp.zeros((experts, length), F32)
        some = jnp.zeros((1, length), F32)
        for g in range(groups):
            peak = peak + inside[g][s] * stats[g]
            scale = scale + inside[g][s] * stats[groups + g]
            some = some + inside[g][s]
        parts.append(jnp.exp(jnp.where(some > 0, logits[s] - peak, MASKED)) * scale)
        share_s[s] = parts[s]
    for block, part in enumerate(turn(parts)):
        share[block] = part

    lead = (2,) * (count + 1)
    loads[0].wait()

    def mixture(block, carry):
        where = pl.ds(pl.multiple_of(block * TILE, TILE), TILE)
        rows = h[:, where, :].reshape(lanes, width)
        weights, _ = block_weights(share[block], member, groups)
        m_part[..., where, :] = dot(weights, rows).astype(BF16).reshape(lead + (TILE, width))
        return carry

    def gradient(block, carry):
        where = pl.ds(pl.multiple_of(block * TILE, TILE), TILE)
        grads = h[:, where, :].reshape(lanes, width)
        weights, _ = block_weights(share[block], member, groups)
        dy_part[..., where, :] = (
            (32.0 * dot(weights, grads)).astype(BF16).reshape(lead + (TILE, width))
        )
        return carry

    plans = orders(count)
    every = list(range(count))[::-1]
    sources = (m_part, dy_part)
    targets = (y_all, dm_all)
    partner = lambda bit: (row, across(place, bits, bit))
    half = length // 2
    spans = (slice(0, half), slice(half, length))
    flying = {}

    def start(which, stage):
        for side in range(2):
            lane_of = 2 * which + side
            bit = plans[side][stage]
            left = [b for b in every if b not in plans[side][:stage]]
            away = pick(left, {bit: 1 - bits[bit]})
            src = (
                sources[which].at[away + (slice(None), spans[side])]
                if stage == 0
                else buffers[lane_of * count + stage - 1].at[away]
            )
            at = lane_of * count + stage
            flying[which, side] = remote(
                src, buffers[at], bsend.at[at], brecv.at[at], partner(bit)
            )

    def launch(which, side):
        flying[which, side].start()

    def finish(which, stage):
        for side in range(2):
            lane_of = 2 * which + side
            flying[which, side].wait()
            bit = plans[side][stage]
            left = [b for b in every if b not in plans[side][:stage]]
            near = pick(left, {bit: bits[bit]})
            target = buffers[lane_of * count + stage]
            if stage == 0:
                old = sources[which][near + (slice(None), spans[side])]
            else:
                old = buffers[lane_of * count + stage - 1][near]
            target[...] = (target[...].astype(F32) + old.astype(F32)).astype(BF16)

    def advance(which, stage):
        finish(which, stage)
        if stage + 1 < count:
            start(which, stage + 1)
            launch(which, 0)
            launch(which, 1)

    def final(which):
        return jnp.concatenate(
            [buffers[(2 * which + side) * count + count - 1][...] for side in range(2)], axis=1
        ).reshape(2 * length, width)

    lower, upper = blocks // 2, blocks
    start(0, 0)
    refill = [
        pltpu.make_async_copy(cot_in.at[:, span], h.at[:, span], isem.at[5 + side])
        for side, span in enumerate(spans)
    ]
    lax.fori_loop(0, lower, mixture, 0)
    launch(0, 0)
    refill[0].start()
    lax.fori_loop(lower, upper, mixture, 0)
    launch(0, 1)
    refill[1].start()
    refill[0].wait()
    start(1, 0)
    lax.fori_loop(0, lower, gradient, 0)
    launch(1, 0)
    advance(0, 0)
    refill[1].wait()
    lax.fori_loop(lower, upper, gradient, 0)
    launch(1, 1)

    mine = pick(every, {b: bits[b] for b in every})
    placed = {}

    def push(which, stage):
        for side in range(2):
            lane_of = 2 * which + side
            order = plans[side][::-1]
            bit = order[stage]
            spot = targets[which].at[
                pick(every, {b: bits[b] for b in every if b not in order[:stage]})
                + (slice(None), spans[side])
            ]
            at = lane_of * count + stage
            source = own.at[which, :, spans[side]] if stage == 0 else spot
            copy = remote(source, spot, csend.at[at], crecv.at[at], partner(bit))
            copy.start()
            flying[which, side] = copy

    def publish(which, value):
        own[which] = value.astype(BF16).reshape(2, length, width)
        copy = pltpu.make_async_copy(own.at[which], targets[which].at[mine], lsem.at[which])
        copy.start()
        placed[which] = copy
        push(which, 0)

    def relay(which, stage):
        for side in range(2):
            flying[which, side].wait()
        if stage == 0:
            placed[which].wait()
        if stage + 1 < count:
            push(which, stage + 1)

    for stage in range(1, count - 1):
        advance(0, stage)
    advance(1, 0)
    wout_ring = ring_on(1, 2, wout_ring)
    advance(0, count - 1)
    m = final(0)
    m_t[...] = jnp.transpose(m)
    for copy in (loads[2:] if dp < 4 else []) + win_ring + wout_ring:
        copy.wait()
    hidden = win.shape[-1]
    up = win[...].reshape(width, hidden)
    down = wout.reshape(hidden, width)
    piece = hidden // dp
    y = jnp.zeros((2 * length, width), F32)
    root = math.sqrt(2 / math.pi)
    for c in range(0, hidden, piece):
        u = dot(m, up[:, c : c + piece])
        square = u * u
        t = jnp.tanh(u * (root + root * 0.044715 * square))
        gate = 0.5 * (1.0 + t)
        active = (u * gate).astype(BF16)
        z[:, c : c + piece] = active
        slope[:, c : c + piece] = gate + (u * gate) * (1.0 - t) * (
            root + 3 * root * 0.044715 * square
        )
        y = y + dot(active, down[c : c + piece, :])
    publish(0, y)
    for stage in range(1, count - 1):
        advance(1, stage)
    relay(0, 0)
    advance(1, count - 1)
    dy = final(1)
    dm = jnp.zeros((2 * length, width), F32)
    for c in range(0, hidden, piece):
        dz = dot(dy, down[c : c + piece, :], 1, 1).astype(BF16).astype(F32)
        grad = (dz * slope[:, c : c + piece]).astype(BF16)
        du[:, c : c + piece] = grad
        dm = dm + dot(grad, up[:, c : c + piece], 1, 1)
    publish(1, dm)
    share_of = width // dp

    def weights_of(step):
        whose = lax.rem(row + step, dp)
        strip = m_t[pl.ds(pl.multiple_of(whose * share_of, share_of), share_of), :]
        for c in range(0, hidden, piece):
            gins[step][:, c : c + piece] = dot(strip, du[:, c : c + piece]).astype(BF16)
        gouts[step][...] = dot(
            z[:, pl.ds(pl.multiple_of(whose * piece, piece), piece)], dy, 0, 0
        ).astype(BF16)

    def pass_sums(distance):
        sent = []
        for way, other in enumerate((right, left)):
            step = distance if way == 0 else dp - distance
            for index, grads in enumerate((gins, gouts)):
                rows = grads[step].shape[0]
                span = slice(0, rows)
                if 2 * distance == dp:
                    span = (slice(0, rows // 2), slice(rows // 2, rows))[way]
                at = 4 * (distance - 2) + 2 * way + index
                sent.append(
                    (
                        remote(
                            grads[step].at[span],
                            ring_in[index].at[distance - 2, way, span],
                            gsend.at[at],
                            grecv.at[at],
                            (other, place),
                        ),
                        grads[step - 1 if way == 0 else step + 1],
                        ring_in[index].at[distance - 2, way, span],
                        span,
                    )
                )
                sent[-1][0].start()
        return sent

    weights_of(dp // 2)
    passed = pass_sums(dp // 2)
    relay(1, 0)
    for distance in range(dp // 2 - 1, 0, -1):
        weights_of(distance)
        weights_of(dp - distance)
        if distance == 1:
            weights_of(0)
            for stage in range(1, count - 1):
                relay(0, stage)
                relay(1, stage)
        for copy, target, arrived, span in passed:
            copy.wait()
            target[span, :] = (target[span, :].astype(F32) + arrived[...].astype(F32)).astype(BF16)
        passed = pass_sums(distance) if distance > 1 else []
    relay(0, count - 1)
    relay(1, count - 1)


def mix_experts(dp, pos, groups, h, cot, logits, member, member_s, expert_out, win_parts):
    slots, length, width = h.shape
    experts = logits.shape[1]
    part = expert_out.shape[1:]
    lead = (2,) * (bits_of(pos) + 1)
    hidden = win_parts[0].shape[-1]
    blocks = length // TILE
    count = bits_of(pos)
    vmem = pl.BlockSpec(memory_space=pltpu.VMEM)
    hbm = pl.BlockSpec(memory_space=pl.ANY)
    rows = 2 * length
    dma = pltpu.SemaphoreType.DMA
    return pl.pallas_call(
        lambda *refs: expert_kernel(dp, pos, groups, *refs),
        out_shape=[
            jax.ShapeDtypeStruct((blocks, experts, slots * TILE), F32),
            jax.ShapeDtypeStruct(logits.shape, F32),
            jax.ShapeDtypeStruct(lead + (length, width), BF16),
            jax.ShapeDtypeStruct(lead + (length, width), BF16),
        ]
        + [jax.ShapeDtypeStruct((width // dp, hidden), BF16)] * dp
        + [jax.ShapeDtypeStruct((hidden // dp, width), BF16)] * dp,
        in_specs=[hbm, hbm, vmem, vmem, vmem, hbm] + [hbm] * 3,
        out_specs=[vmem, vmem, hbm, hbm] + [vmem] * (2 * dp),
        scratch_shapes=[
            pltpu.VMEM(h.shape, BF16),
            pltpu.VMEM((dp,) + win_parts[0].shape, BF16),
            pltpu.VMEM((dp, pos) + part, BF16),
            pltpu.VMEM((2 * groups, experts, slots * TILE), F32),
            pltpu.VMEM((pos - 1, 2 * groups, experts, slots * TILE), F32),
            pltpu.VMEM(lead + (length, width), BF16),
            pltpu.VMEM(lead + (length, width), BF16),
            pltpu.VMEM((width, rows), BF16),
            pltpu.VMEM((rows, hidden), BF16),
            pltpu.VMEM((rows, hidden), F32),
            pltpu.VMEM((rows, hidden), BF16),
            pltpu.VMEM((2, 2, length, width), BF16),
            pltpu.VMEM((dp // 2 - 1, 2, width // dp, hidden), BF16),
            pltpu.VMEM((dp // 2 - 1, 2, hidden // dp, width), BF16),
        ]
        + [
            pltpu.VMEM((2,) * (count - stage) + (length // 2, width), BF16)
            for _ in range(4)
            for stage in range(count)
        ]
        + [
            dma((pos - 1,)),
            dma((pos - 1,)),
            dma((4 * count,)),
            dma((4 * count,)),
            dma((4 * count,)),
            dma((4 * count,)),
            dma((pos - 1,)),
            dma((pos - 1,)),
            dma((2 * dp,)),
            dma((2 * dp,)),
            dma((4 * (dp // 2 - 1),)),
            dma((4 * (dp // 2 - 1),)),
            dma((2,)),
            dma((7,)),
        ],
        compiler_params=pltpu.CompilerParams(
            collective_id=2, has_side_effects=True, vmem_limit_bytes=VMEM_LIMIT
        ),
        name="mix_experts",
    )(h, cot, logits, member, member_s, expert_out, *win_parts)


def routing_kernel(
    pos, groups, y, dm, h, cot, share, share_s, member, member_s,
    mix, dh, dc, dw, local, gathered, send, recv,
):
    row, place = lax.axis_index("dp"), lax.axis_index("pos")
    step = pl.program_id(0)
    units, span, width = y.shape
    blocks, experts, lanes = share.shape
    slots = lanes // TILE
    several = span // TILE

    @pl.when(step == 0)
    def _():
        greet([(row, lax.rem(place + other, pos)) for other in range(1, pos)])

    for i in range(several):
        block = step * several + i
        where = slice(i * TILE, (i + 1) * TILE)
        weights, mask = block_weights(share[block], member, groups)
        yb = y[:, where, :].reshape(units * TILE, width)
        dmb = dm[:, where, :].reshape(units * TILE, width)
        whole = 32.0 * dot(yb, cot[:, where, :].reshape(lanes, width), 1, 1) + dot(
            dmb, h[:, where, :].reshape(lanes, width), 1, 1
        )
        mix[:, where, :] = (32.0 * dot(weights, yb, 0, 0)).astype(BF16).reshape(slots, TILE, width)
        dh[:, where, :] = dot(weights, dmb, 0, 0).astype(BF16).reshape(slots, TILE, width)
        picked = whole.reshape(experts, groups, TILE, lanes) * mask[None]
        dw[block] = jnp.sum(jnp.sum(picked, axis=1), axis=1)

    @pl.when(step == blocks // several - 1)
    def _():
        grads = turn([dw[b] for b in range(blocks)])
        for g in range(groups):
            total = jnp.zeros(local.shape[1:], F32)
            for s in range(slots):
                total = total + member_s[g, s : s + 1, :] * share_s[s] * grads[s]
            local[g] = total
        exchange(local, gathered, send, recv, row, place, pos)
        sums = []
        for g in range(groups):
            total = local[g]
            for other in range(pos - 1):
                total = total + gathered[other, g]
            sums.append(total)
        for s in range(slots):
            inner = jnp.zeros(local.shape[1:], F32)
            for g in range(groups):
                inner = inner + member_s[g, s : s + 1, :] * sums[g]
            dc[s] = (share_s[s] * (grads[s] - inner)).astype(BF16)


def route_back(pos, groups, y, dm, h, cot, share, share_s, member, member_s, several=2):
    slots, length, width = h.shape
    units = y.shape[0]
    blocks, experts, lanes = share.shape
    per = lambda rows: pl.BlockSpec((rows, several * TILE, width), lambda b: (0, b, 0))
    whole = lambda a: pl.BlockSpec(a.shape, lambda b: (0,) * len(a.shape))
    return pl.pallas_call(
        lambda *refs: routing_kernel(pos, groups, *refs),
        grid=(blocks // several,),
        out_shape=[
            jax.ShapeDtypeStruct(h.shape, BF16),
            jax.ShapeDtypeStruct(h.shape, BF16),
            jax.ShapeDtypeStruct(share_s.shape, BF16),
        ],
        in_specs=[per(units), per(units), per(slots), per(slots)]
        + [whole(a) for a in (share, share_s, member, member_s)],
        out_specs=[per(slots), per(slots), whole(share_s)],
        scratch_shapes=[
            pltpu.VMEM(share.shape, F32),
            pltpu.VMEM((groups, experts, length), F32),
            pltpu.VMEM((pos - 1, groups, experts, length), F32),
            pltpu.SemaphoreType.DMA((pos - 1,)),
            pltpu.SemaphoreType.DMA((pos - 1,)),
        ],
        compiler_params=pltpu.CompilerParams(
            collective_id=3, has_side_effects=True, vmem_limit_bytes=VMEM_LIMIT
        ),
        name="route_back",
    )(y, dm, h, cot, share, share_s, member, member_s)


from jax.sharding import PartitionSpec as P

MIXED_SEQUENCES = 32


def body(
    inputs,
    cotangent,
    counts,
    seq_rank,
    first_gain,
    first_bias,
    query_weight,
    key_weight,
    value_weight,
    output_weight,
    second_gain,
    second_bias,
    control_weight,
    expert_in,
    expert_out,
):
    capacity, length, features = inputs.shape
    dp, pos = lax.axis_size("dp"), lax.axis_size("pos")
    experts = control_weight.shape[1]
    groups = seq_rank.shape[1] // MIXED_SEQUENCES

    w_t, wk, wo, small, member, member_s, live, win = gather_weights(
        dp,
        pos,
        groups,
        capacity,
        query_weight,
        key_weight,
        value_weight,
        output_weight,
        jnp.stack([first_gain, first_bias, second_gain, second_bias]),
        control_weight.T,
        counts,
        seq_rank,
        expert_in,
    )
    count = live[0, :1]

    def send_rows(array, step):
        return lax.ppermute(array, "dp", [(i, (i + step) % dp) for i in range(dp)])

    wins = (win, send_rows(win, 1), send_rows(win, -1))

    q_t, k, v_t, ctx_t, x1, h, inverse, e_t, logits = forward(count, inputs, w_t, wk, wo, small)
    share, share_s, y_all, dm_all, *grads = mix_experts(
        dp, pos, groups, h, cotangent, logits, member, member_s, expert_out, wins
    )
    grads = [
        (parts[0], send_rows(parts[1], 1), send_rows(parts[dp - 1], -1))
        for parts in (grads[:dp], grads[dp:])
    ]
    units = experts * groups
    y_all = y_all.reshape(units, length, features)
    dm_all = dm_all.reshape(units, length, features)
    mix, dh, dc = route_back(
        pos, groups, y_all, dm_all, h, cotangent, share, share_s, member, member_s
    )

    layer_output, input_grad, grad_t, out_grad, vecs = backward(
        count, inputs, cotangent, x1, mix, dh, dc, q_t, k, v_t, ctx_t, inverse, e_t, w_t, wo, small
    )
    shard, *grads = scatter_weights(
        dp, pos, grad_t, out_grad, vecs, *grads
    )
    expert_in_grad, expert_out_grad = (
        jnp.sum(part.astype(F32).reshape((experts, pos // experts) + part.shape[1:]), axis=1)
        for part in grads
    )
    tail = shard[:, 4 * features :]
    return (
        layer_output,
        input_grad,
        tail[:, 2],
        tail[:, 3],
        shard[:, :features],
        shard[:, features : 2 * features],
        shard[:, 2 * features : 3 * features],
        shard[:, 3 * features : 4 * features],
        tail[:, 0],
        tail[:, 1],
        tail[:, 8 : 8 + experts],
        expert_in_grad,
        expert_out_grad,
    )


def solution(mesh):
    both = ("dp", "pos")
    vector, matrix, cube = P(both), P(both, None), P(both, None, None)
    middle = P(None, both, None)
    return jax.shard_map(
        body,
        mesh=mesh,
        in_specs=(
            cube,
            cube,
            P("dp", None),
            P("dp", None),
            vector,
            vector,
            matrix,
            matrix,
            matrix,
            matrix,
            vector,
            vector,
            matrix,
            middle,
            middle,
        ),
        out_specs=(
            cube,
            cube,
            vector,
            vector,
            matrix,
            matrix,
            matrix,
            matrix,
            vector,
            vector,
            matrix,
            middle,
            middle,
        ),
        check_vma=False,
    )
```

```python
import math
import jax
import jax.numpy as jnp
from jax import lax
from jax.experimental import pallas as pl
from jax.experimental.pallas import tpu as pltpu

HEADS = 8
HEAD = 64
NORM_EPS = 1e-05
MASKED = -1e30
F32 = jnp.float32
BF16 = jnp.bfloat16
MIB = 1 << 20
VMEM_LIMIT = 62 * MIB


def dot(a, b, ca=1, cb=0):
    return lax.dot_general(a, b, (((ca,), (cb,)), ((), ())), preferred_element_type=F32)


def normalize(v):
    center = v - jnp.mean(v, axis=-1, keepdims=True)
    spread = jnp.mean(center * center, axis=-1, keepdims=True)
    scale = lax.rsqrt(spread + NORM_EPS)
    return center * scale, scale


def spread_heads(parts):
    return jnp.concatenate(
        [
            jnp.concatenate(
                [part if i == j else jnp.zeros_like(part) for i in range(len(parts))], axis=0
            )
            for j, part in enumerate(parts)
        ],
        axis=1,
    )


def forward_kernel(count, x, w_t, wk, wo, small, q_t, k, v_t, ctx_t, x1, h, inverse, e_t, logits):
    g1, b1, g2, b2 = (small[i : i + 1] for i in range(4))
    slots, length, width = x.shape
    router = small[8:16].astype(BF16)
    wq_t, wv_t = w_t.at[:width], w_t.at[2 * width :]
    half = length // 2
    causal = lax.broadcasted_iota(jnp.int32, (half, half), 0) <= lax.broadcasted_iota(
        jnp.int32, (half, half), 1
    )

    def one():
        source = x[...].reshape(slots * length, width).astype(F32)
        xhat, _ = normalize(source)
        a = (xhat * g1 + b1).astype(BF16)
        qs = (dot(wq_t[...], a, 1, 1).astype(BF16) * 0.125).astype(BF16)
        ks = dot(a, wk[...]).astype(BF16)
        vs = dot(wv_t[...], a, 1, 1).astype(BF16)
        k[...] = ks.reshape(slots, length, width)
        ones = jnp.ones((16, length), BF16)
        parts = [[] for _ in range(slots)]
        sums = [[] for _ in range(slots)]
        cols = [slice(s * length, (s + 1) * length) for s in range(slots)]
        for s in range(slots):
            q_t[s] = qs[:, cols[s]]
            v_t[s] = vs[:, cols[s]]
        for base in range(0, HEADS, 4):
            for s in range(slots):
                four = slice(base * HEAD, (base + 4) * HEAD)
                spread_q = spread_heads(
                    [
                        qs[(base + i) * HEAD : (base + i + 1) * HEAD, cols[s]] for i in range(4)
                    ]
                )
                scores = dot(ks[cols[s], four], spread_q)
                exps = []
                for j in range(4):
                    st = scores[:, j * length : (j + 1) * length]
                    s00 = jnp.where(causal, st[:half, :half], MASKED)
                    s01 = st[:half, half:]
                    s11 = jnp.where(causal, st[half:, half:], MASKED)
                    m0 = jnp.max(s00, axis=0, keepdims=True)
                    m1 = jnp.maximum(
                        jnp.max(s01, axis=0, keepdims=True), jnp.max(s11, axis=0, keepdims=True)
                    )
                    e00 = jnp.exp(s00 - m0).astype(BF16)
                    e01 = jnp.exp(s01 - m1).astype(BF16)
                    e11 = jnp.exp(s11 - m1).astype(BF16)
                    et = jnp.concatenate(
                        [
                            jnp.concatenate([e00, e01], axis=1),
                            jnp.concatenate([jnp.zeros_like(e00), e11], axis=1),
                        ],
                        axis=0,
                    )
                    e_t[s, base + j] = et
                    exps.append(et)
                for j in range(0, 4, 2):
                    head = base + j
                    va = jnp.concatenate(
                        [
                            vs[head * HEAD : (head + 1) * HEAD, cols[s]],
                            ones,
                            vs[(head + 1) * HEAD : (head + 2) * HEAD, cols[s]],
                            ones,
                        ],
                        axis=0,
                    )
                    both = dot(va, jnp.concatenate(exps[j : j + 2], axis=1))
                    for i in range(2):
                        full = both[i * 80 : i * 80 + 80, i * length : (i + 1) * length]
                        total = full[HEAD : HEAD + 1]
                        scale = 1.0 / total
                        parts[s].append((full[:HEAD] * scale).astype(BF16))
                        sums[s].append(scale)
        outs = []
        for s in range(slots):
            ctx = jnp.concatenate(parts[s], axis=0)
            ctx_t[s] = ctx
            inverse[s] = jnp.concatenate(sums[s], axis=0)
            outs.append(ctx)
        residual = source + dot(jnp.concatenate(outs, axis=1), wo[...], 0, 0)
        x1[...] = residual.reshape(slots, length, width)
        xhat2, _ = normalize(residual)
        hidden = (xhat2 * g2 + b2).astype(BF16)
        h[...] = hidden.reshape(slots, length, width)
        for s in range(slots):
            logits[s] = dot(router, hidden[cols[s], :], 1, 1)

    live = pl.program_id(0) * slots < count[0]
    pl.when(live)(one)

    @pl.when(jnp.logical_not(live))
    def _():
        h[...] = jnp.zeros((slots, length, width), BF16)
        logits[...] = jnp.zeros_like(logits)


def forward(count, x, w_t, wk, wo, small, block=2):
    slots, length, width = x.shape
    per = lambda rows, cols: pl.BlockSpec((block, rows, cols), lambda i, c: (i, 0, 0))
    whole = lambda a: pl.BlockSpec(a.shape, lambda i, c: (0,) * a.ndim)
    shape = lambda rows, cols, kind: jax.ShapeDtypeStruct((slots, rows, cols), kind)
    return pl.pallas_call(
        forward_kernel,
        grid_spec=pltpu.PrefetchScalarGridSpec(
            num_scalar_prefetch=1,
            grid=(slots // block,),
            in_specs=[per(length, width)]
            + [whole(a) for a in (w_t, wk, wo, small)],
            out_specs=[
                per(width, length),
                per(length, width),
                per(width, length),
                per(width, length),
                per(length, width),
                per(length, width),
                per(HEADS, length),
            ]
            + [pl.BlockSpec((block, HEADS, length, length), lambda i, c: (i, 0, 0, 0)), per(HEADS, length)],
        ),
        out_shape=[
            shape(width, length, BF16),
            shape(length, width, BF16),
            shape(width, length, BF16),
            shape(width, length, BF16),
            shape(length, width, F32),
            shape(length, width, BF16),
            shape(HEADS, length, F32),
        ]
        + [jax.ShapeDtypeStruct((slots, HEADS, length, length), BF16), shape(8, length, F32)] ,
        compiler_params=pltpu.CompilerParams(vmem_limit_bytes=VMEM_LIMIT),
        cost_estimate=pl.CostEstimate(
            flops=40_000_000_000, bytes_accessed=40 * MIB, transcendentals=8_000_000
        ),
        name="attention_forward",
    )(count, x, w_t, wk, wo, small)


def norm_back(grad, xhat, scale):
    return scale * (
        grad
        - jnp.mean(grad, axis=-1, keepdims=True)
        - xhat * jnp.mean(grad * xhat, axis=-1, keepdims=True)
    )


def backward_kernel(
    count, x, cot, x1, mix, dh, dc, q_t, k, v_t, ctx_t, inverse, e_t, w_t, wo, small,
    lo, dx, grad_t, out_grad, vecs, back_t,
):
    slots, length, width = x.shape
    half = length // 2
    step = pl.program_id(0)

    @pl.when(step == 0)
    def _():
        grad_t[...] = jnp.zeros_like(grad_t)
        out_grad[...] = jnp.zeros_like(out_grad)
        vecs[...] = jnp.zeros_like(vecs)

    g1, b1, g2, b2 = (small[i : i + 1] for i in range(4))
    router = small[8:16].astype(BF16)

    def one():
        tokens = slots * length
        cols = [slice(s * length, (s + 1) * length) for s in range(slots)]
        row = lax.broadcasted_iota(jnp.int32, (tokens, 1), 0) // length + step * slots
        live = row < count[0]
        keep = lambda v: v if slots == 1 else jnp.where(live, v, 0.0)
        residual = x1[...].reshape(tokens, width)
        xhat2, scale2 = normalize(residual)
        lo[...] = (
            keep(residual + mix[...].reshape(tokens, width).astype(F32))
            .astype(BF16)
            .reshape(slots, length, width)
        )
        hidden = (xhat2 * g2 + b2).astype(BF16)
        routed = []
        for s in range(slots):
            routed.append(dot(dc[s], router, 0, 0))
            vecs[8:16] += dot(dc[s], hidden[cols[s], :])
        grad_h = (
            (dh[...].reshape(tokens, width).astype(F32) + jnp.concatenate(routed, axis=0))
            .astype(BF16)
            .astype(F32)
        )
        vecs[0:1] += jnp.sum(grad_h * xhat2, axis=0, keepdims=True)
        vecs[1:2] += jnp.sum(grad_h, axis=0, keepdims=True)
        dx1 = keep(
            cot[...].reshape(tokens, width).astype(F32) + norm_back(grad_h * g2, xhat2, scale2)
        )
        datt = dx1.astype(BF16)
        dctx = dot(wo[...], datt, 1, 1).astype(BF16)
        out_grad[...] += dot(jnp.concatenate([ctx_t[s] for s in range(slots)], axis=1), datt)
        zero = jnp.zeros((half, half), BF16)
        for s in range(slots):
            kt = jnp.transpose(k[s])
            vn = jnp.transpose(v_t[s])
            scaled = []
            inners = []
            for head in range(HEADS):
                rows = slice(head * HEAD, (head + 1) * HEAD)
                part = dctx[rows, cols[s]].astype(F32) * inverse[s, head : head + 1, :]
                scaled.append(part.astype(BF16))
                inners.append(jnp.sum(ctx_t[s, rows, :].astype(F32) * part, axis=0, keepdims=True))
            for base in range(0, HEADS, 4):
                four = slice(base * HEAD, (base + 4) * HEAD)
                dprobs = dot(vn[:, four], spread_heads(scaled[base : base + 4]))
                grads = []
                exps = []
                for j in range(4):
                    head = base + j
                    et = e_t[s, head]
                    dp = dprobs[:, j * length : (j + 1) * length]
                    inner = inners[head]
                    d00 = et[:half, :half].astype(F32) * (dp[:half, :half] - inner[:, :half])
                    d01 = et[:half, half:].astype(F32) * (dp[:half, half:] - inner[:, half:])
                    d11 = et[half:, half:].astype(F32) * (dp[half:, half:] - inner[:, half:])
                    grads.append(
                        jnp.concatenate(
                            [
                                jnp.concatenate([d00.astype(BF16), d01.astype(BF16)], axis=1),
                                jnp.concatenate([zero, d11.astype(BF16)], axis=1),
                            ],
                            axis=0,
                        )
                    )
                    exps.append(et)
                tall = jnp.concatenate(grads, axis=0)
                dk = dot(q_t[s, four, :], tall, 1, 1)
                dv = dot(
                    jnp.concatenate(scaled[base : base + 4], axis=0),
                    jnp.concatenate(exps, axis=0),
                    1,
                    1,
                )
                dq = [
                    dot(
                        kt[(base + j) * HEAD : (base + j + 2) * HEAD, :],
                        jnp.concatenate(grads[j : j + 2], axis=1),
                    )
                    * 0.125
                    for j in range(0, 4, 2)
                ]
                for j in range(4):
                    begin = (base + j) * HEAD
                    spot = slice(j * length, (j + 1) * length)
                    inside = slice(j * HEAD, (j + 1) * HEAD)
                    i = j % 2
                    back_t[begin : begin + HEAD, cols[s]] = dq[j // 2][
                        i * HEAD : (i + 1) * HEAD, i * length : (i + 1) * length
                    ].astype(BF16)
                    back_t[width + begin : width + begin + HEAD, cols[s]] = dk[inside, spot].astype(
                        BF16
                    )
                    back_t[2 * width + begin : 2 * width + begin + HEAD, cols[s]] = dv[
                        inside, spot
                    ].astype(BF16)
        source = x[...].reshape(tokens, width).astype(F32)
        xhat1, scale1 = normalize(source)
        a = (xhat1 * g1 + b1).astype(BF16)
        back = back_t[...]
        grad_t[...] += dot(back, a)
        da = dot(back, w_t[...], 0, 0)
        vecs[2:3] += jnp.sum(da * xhat1, axis=0, keepdims=True)
        vecs[3:4] += jnp.sum(da, axis=0, keepdims=True)
        dx[...] = (
            keep(dx1 + norm_back(da * g1, xhat1, scale1))
            .astype(BF16)
            .reshape(slots, length, width)
        )

    some = step * slots < count[0]
    pl.when(some)(one)

    @pl.when(jnp.logical_not(some))
    def _():
        dx[...] = jnp.zeros((slots, length, width), BF16)
        lo[...] = jnp.zeros((slots, length, width), BF16)


def backward(count, x, cot, x1, mix, dh, dc, q_t, k, v_t, ctx_t, inverse, e_t, w_t, wo, small, block=2):
    slots, length, width = x.shape
    per = lambda a: pl.BlockSpec(
        (block,) + a.shape[1:], lambda i, c: (i,) + (0,) * (len(a.shape) - 1)
    )
    whole = lambda a: pl.BlockSpec(a.shape, lambda i, c: (0,) * len(a.shape))
    outs = [
        jax.ShapeDtypeStruct((3 * width, width), F32),
        jax.ShapeDtypeStruct((width, width), F32),
        jax.ShapeDtypeStruct((16, width), F32),
    ]
    batched = (x, cot, x1, mix, dh, dc, q_t, k, v_t, ctx_t, inverse, e_t)
    shared = (w_t, wo, small)
    return pl.pallas_call(
        backward_kernel,
        grid_spec=pltpu.PrefetchScalarGridSpec(
            num_scalar_prefetch=1,
            grid=(slots // block,),
            in_specs=[per(a) for a in batched] + [whole(a) for a in shared],
            out_specs=[per(x), per(x)] + [whole(a) for a in outs],
            scratch_shapes=[pltpu.VMEM((3 * width, block * length), BF16)],
        ),
        out_shape=[jax.ShapeDtypeStruct(x.shape, BF16)] * 2 + outs,
        compiler_params=pltpu.CompilerParams(vmem_limit_bytes=VMEM_LIMIT),
        cost_estimate=pl.CostEstimate(
            flops=100_000_000_000, bytes_accessed=60 * MIB, transcendentals=8_000_000
        ),
        name="attention_backward",
    )(count, *batched, *shared)


MESH = pl.DeviceIdType.MESH
TILE = 16


def bits_of(size):
    return size.bit_length() - 1


def orders(count):
    first = list(range(count))
    second = list(first)
    if count > 2:
        second[1], second[2] = second[2], second[1]
    return first, second


def greet(peers):
    barrier = pltpu.get_barrier_semaphore()
    for peer in peers:
        pl.semaphore_signal(barrier, inc=1, device_id=peer, device_id_type=MESH)
    pl.semaphore_wait(barrier, len(peers))


def my_bits(place, count):
    return [lax.rem(place // (1 << bit), 2) for bit in range(count)]


def across(place, bits, bit):
    return place + (1 - 2 * bits[bit]) * (1 << bit)


def pick(remaining, chosen):
    return tuple(chosen[bit] if bit in chosen else slice(None) for bit in remaining)


def remote(src, dst, send, recv, device):
    return pltpu.make_async_remote_copy(
        src_ref=src,
        dst_ref=dst,
        send_sem=send,
        recv_sem=recv,
        device_id=device,
        device_id_type=MESH,
    )


def gather_kernel(
    dp, pos, groups, slots,
    wq, wk, wv, wo, vectors, router, counts, ranks, ein,
    w_t, wk_out, wo_out, vt, member, member_s, live, win,
    held, zsend, zrecv, send, recv, esend, erecv, lsem,
):
    count = bits_of(pos)
    row, place = lax.axis_index("dp"), lax.axis_index("pos")
    bits = my_bits(place, count)
    others = [lax.rem(row + step, dp) for step in range(1, dp)]
    mates = [lax.rem(place + step, pos) for step in range(1, pos)]
    greet([(other, place) for other in others] + [(row, mate) for mate in mates])
    rows, width = wq.shape
    every = list(range(count))[::-1]
    here = pick(every, {bit: bits[bit] for bit in every})
    for index, weight in enumerate((wq, wk, wv, wo)):
        held[(row,) + here + (slice(None), slice(index * width, (index + 1) * width))] = weight[...]
    tall = jnp.concatenate(
        [
            vectors[...].astype(F32),
            jnp.zeros((8 - vectors.shape[0], rows), F32),
            router[...].astype(F32),
            jnp.zeros((120 - router.shape[0], rows), F32),
        ],
        axis=0,
    )
    square = jnp.concatenate([tall, jnp.zeros((128, 128 - rows), F32)], axis=1)
    held[(row,) + here + (slice(None), slice(4 * width, 4 * width + 128))] = jnp.transpose(square)[
        :rows
    ].astype(BF16)

    copies = pos // ein.shape[0]
    local = pltpu.make_async_copy(ein.at[place // copies], win.at[place], lsem.at[0])
    local.start()
    zcopies = []
    for step, other in enumerate(others):
        spot = held.at[(row,) + here]
        zcopies.append(remote(spot, spot, zsend.at[step], zrecv.at[step], (other, place)))
        zcopies[-1].start()

    ecopies = []
    for step, mate in enumerate(mates):
        ecopies.append(
            remote(
                ein.at[mate // copies], win.at[place], esend.at[step], erecv.at[step], (row, mate)
            )
        )
        ecopies[-1].start()

    first, second = orders(count)
    plans = (first[::-1], second[::-1])

    def push(block, stage):
        order = plans[block % 2]
        bit = order[stage]
        whose = lax.rem(row + dp - block, dp)
        spot = held.at[
            (whose,) + pick(every, {b: bits[b] for b in every if b not in order[:stage]})
        ]
        at = block * count + stage
        copy = remote(spot, spot, send.at[at], recv.at[at], (row, across(place, bits, bit)))
        copy.start()
        return copy

    flying = {0: push(0, 0)}
    lanes = slots * TILE
    which = lax.broadcasted_iota(jnp.int32, (1, pos), 1)
    begin = jnp.sum(jnp.where(which < place, counts[...], 0), axis=1, keepdims=True)
    mine = jnp.sum(jnp.where(which == place, counts[...], 0), axis=1, keepdims=True)
    live[...] = jnp.broadcast_to(mine, live.shape)
    slot = lax.broadcasted_iota(jnp.int32, (1, lanes), 1) // TILE
    wanted = jnp.where(slot < mine, begin + slot, -1)
    table = (ranks[...] // 32).astype(F32) + 1.0
    size = table.shape[1]
    if size < 128:
        table = jnp.concatenate([table, jnp.zeros((1, 128 - size), F32)], axis=1)
    column = jnp.transpose(jnp.broadcast_to(table, (128, 128)))[:, :1]
    match = lax.broadcasted_iota(jnp.int32, (128, lanes), 0) == wanted
    ids = jnp.sum(jnp.where(match, column, 0.0), axis=0, keepdims=True)
    for g in range(groups):
        member[g : g + 1, :] = (ids == float(g + 1)).astype(F32)
    slot = lax.broadcasted_iota(jnp.int32, (slots, 1), 0)
    wanted = jnp.where(slot < mine, begin + slot, -1)
    match = lax.broadcasted_iota(jnp.int32, (slots, 128), 1) == wanted
    ids = jnp.sum(jnp.where(match, table, 0.0), axis=1, keepdims=True)
    for g in range(groups):
        member_s[g] = jnp.broadcast_to((ids == float(g + 1)).astype(F32), member_s.shape[1:])

    for block in range(1, dp):
        zcopies[block - 1].wait()
        flying[block] = push(block, 0)
    for stage in range(1, count):
        for block in range(dp):
            flying[block].wait()
            flying[block] = push(block, stage)
    for block in range(dp):
        flying[block].wait()
    full = held[...].reshape(dp * pos * rows, 4 * width + 128)
    for index in range(3):
        w_t[index * width : (index + 1) * width, :] = jnp.transpose(
            full[:, index * width : (index + 1) * width]
        )
    wk_out[...] = full[:, width : 2 * width]
    wo_out[...] = full[:, 3 * width : 4 * width]
    vt[...] = jnp.transpose(full[:, 4 * width :])[:16, :].astype(F32)
    for copy in [local] + ecopies:
        copy.wait()


def gather_weights(dp, pos, groups, slots, wq, wk, wv, wo, vectors, router, counts, ranks, ein):
    rows, width = wq.shape
    whole = rows * dp * pos
    vmem = pl.BlockSpec(memory_space=pltpu.VMEM)
    hbm = pl.BlockSpec(memory_space=pl.ANY)
    count = bits_of(pos)
    dma = pltpu.SemaphoreType.DMA
    return pl.pallas_call(
        lambda *refs: gather_kernel(dp, pos, groups, slots, *refs),
        out_shape=[
            jax.ShapeDtypeStruct((3 * width, whole), BF16),
            jax.ShapeDtypeStruct((whole, width), BF16),
            jax.ShapeDtypeStruct((whole, width), BF16),
            jax.ShapeDtypeStruct((16, whole), F32),
            jax.ShapeDtypeStruct((groups, slots * TILE), F32),
            jax.ShapeDtypeStruct((groups, slots, slots * TILE), F32),
            jax.ShapeDtypeStruct((1, 128), jnp.int32),
            jax.ShapeDtypeStruct((pos,) + ein.shape[1:], BF16),
        ],
        in_specs=[vmem] * 8 + [hbm],
        out_specs=[vmem] * 7 + [hbm],
        scratch_shapes=[
            pltpu.VMEM((dp,) + (2,) * count + (rows, 4 * width + 128), BF16),
            dma((dp - 1,)),
            dma((dp - 1,)),
            dma((dp * count,)),
            dma((dp * count,)),
            dma((pos - 1,)),
            dma((pos - 1,)),
            dma((1,)),
        ],
        compiler_params=pltpu.CompilerParams(
            collective_id=0, has_side_effects=True, vmem_limit_bytes=VMEM_LIMIT
        ),
        name="gather_weights",
    )(wq, wk, wv, wo, vectors, router, counts, ranks, ein)


def scatter_kernel(dp, pos, grad_t, out_grad, vecs, *rest):
    count = bits_of(pos)
    grads, rest = rest[:3], rest[3:]
    out, ein_got, eout_got, held, *rest = rest
    buffers, slots, rest = rest[: 2 * count], rest[2 * count], rest[2 * count + 1 :]
    send, recv, esend, erecv, ein_mine, eout_mine = rest
    row, place = lax.axis_index("dp"), lax.axis_index("pos")
    bits = my_bits(place, count)
    others = [lax.rem(row + step, dp) for step in range(1, dp)]
    mates = [lax.rem(place + step, pos) for step in range(1, pos)]
    greet([(other, place) for other in others] + [(row, mate) for mate in mates])
    width = out_grad.shape[1]
    ecopies = []
    for index, (mine, got) in enumerate(((ein_mine, ein_got), (eout_mine, eout_got))):
        total = grads[0][index].astype(F32)
        for part in grads[1:]:
            total = total + part[index].astype(F32)
        total = total.astype(BF16)
        if index == 0:
            strip = width // dp
            for c in range(0, mine.shape[2], width):
                at = c // width * strip
                mine[:, :, c : c + width] = total[at : at + strip].reshape(
                    mine.shape[:2] + (width,)
                )
        else:
            mine[...] = total.reshape(mine.shape)
        for step, mate in enumerate(mates):
            at = index * (pos - 1) + step
            ecopies.append(
                remote(mine.at[mate], got.at[place], esend.at[at], erecv.at[at], (row, mate))
            )
            ecopies[-1].start()
        got[place] = mine[place]
    lead = held.shape[:-1]
    for index in range(3):
        held[..., index * width : (index + 1) * width] = (
            jnp.transpose(grad_t[index * width : (index + 1) * width, :])
            .astype(BF16)
            .reshape(lead + (width,))
        )
    held[..., 3 * width : 4 * width] = out_grad[...].astype(BF16).reshape(lead + (width,))
    tail = jnp.concatenate([vecs[...], jnp.zeros((112, vecs.shape[1]), F32)], axis=0)
    held[..., 4 * width :] = jnp.transpose(tail).astype(BF16).reshape(lead + (128,))
    used = 0
    halves = (slice(0, dp // 2), slice(dp // 2, dp))
    plans = orders(count)
    current = [held.at[half] for half in halves]
    remaining = [list(range(count))[::-1] for _ in halves]
    for stage in range(count):
        copies = []
        for side in range(2):
            bit = plans[side][stage]
            away = (slice(None),) + pick(remaining[side], {bit: 1 - bits[bit]})
            copies.append(
                remote(
                    current[side].at[away],
                    buffers[side * count + stage],
                    send.at[used],
                    recv.at[used],
                    (row, across(place, bits, bit)),
                )
            )
            used += 1
        for copy in copies:
            copy.start()
        for side in range(2):
            copies[side].wait()
            bit = plans[side][stage]
            near = (slice(None),) + pick(remaining[side], {bit: bits[bit]})
            target = buffers[side * count + stage]
            target[...] = (
                target[...].astype(F32) + current[side][near].astype(F32)
            ).astype(BF16)
            current[side] = target
            remaining[side] = [b for b in remaining[side] if b != bit]
    joined = jnp.concatenate([current[0][...], current[1][...]], axis=0)
    slots[1] = joined
    copies = []
    for step, other in enumerate(others):
        copies.append(
            remote(
                slots.at[1, other],
                slots.at[0, row],
                send.at[used],
                recv.at[used],
                (other, place),
            )
        )
        used += 1
        copies[-1].start()
    for copy in copies:
        copy.wait()
    total = slots[1, row].astype(F32)
    for other in others:
        total = total + slots[0, other].astype(F32)
    out[...] = total
    for copy in ecopies:
        copy.wait()


def scatter_weights(dp, pos, grad_t, out_grad, vecs, *grads):
    width = out_grad.shape[1]
    rows = out_grad.shape[0] // (dp * pos)
    wide = 4 * width + 128
    hidden = grads[0].shape[1] * dp
    ein_shape = (width // (dp * pos), hidden)
    eout_shape = (hidden // (dp * pos), width)
    vmem = pl.BlockSpec(memory_space=pltpu.VMEM)
    count = bits_of(pos)
    total = dp - 1 + 2 * count
    return pl.pallas_call(
        lambda *refs: scatter_kernel(dp, pos, *refs),
        out_shape=[
            jax.ShapeDtypeStruct((rows, wide), F32),
            jax.ShapeDtypeStruct((pos,) + ein_shape, BF16),
            jax.ShapeDtypeStruct((pos,) + eout_shape, BF16),
        ],
        in_specs=[vmem] * 6,
        out_specs=[vmem] * 3,
        scratch_shapes=[pltpu.VMEM((dp,) + (2,) * count + (rows, wide), BF16)]
        + [
            pltpu.VMEM((dp // 2,) + (2,) * (count - 1 - stage) + (rows, wide), BF16)
            for _ in range(2)
            for stage in range(count)
        ]
        + [
            pltpu.VMEM((2, dp, rows, wide), BF16),
            pltpu.SemaphoreType.DMA((total,)),
            pltpu.SemaphoreType.DMA((total,)),
            pltpu.SemaphoreType.DMA((2 * (pos - 1),)),
            pltpu.SemaphoreType.DMA((2 * (pos - 1),)),
            pltpu.VMEM((pos,) + ein_shape, BF16),
            pltpu.VMEM((pos,) + eout_shape, BF16),
        ],
        compiler_params=pltpu.CompilerParams(
            collective_id=1, has_side_effects=True, vmem_limit_bytes=VMEM_LIMIT
        ),
        name="scatter_weights",
    )(grad_t, out_grad, vecs, *grads)


def turn(parts):
    size = len(parts)
    lanes = parts[0].shape[1]
    tile = lax.broadcasted_iota(jnp.int32, parts[0].shape, 1) // TILE
    step = 1
    while step < size:
        low = lax.rem(tile // step, 2) == 0
        new = list(parts)
        for i in range(size):
            if i & step == 0:
                upper, lower = parts[i], parts[i | step]
                new[i] = jnp.where(low, upper, pltpu.roll(lower, step * TILE, 1))
                new[i | step] = jnp.where(low, pltpu.roll(upper, lanes - step * TILE, 1), lower)
        parts = new
        step *= 2
    return parts


def block_weights(share, member, groups):
    experts, lanes = share.shape
    rounded = share.astype(BF16).astype(F32)
    spot = (
        lax.broadcasted_iota(jnp.int32, (TILE, lanes), 0)
        == lax.rem(lax.broadcasted_iota(jnp.int32, (TILE, lanes), 1), TILE)
    ).astype(F32)
    mask = jnp.stack([spot * member[g : g + 1, :] for g in range(groups)])
    full = rounded[:, None, None, :] * mask[None]
    return full.reshape(experts * groups * TILE, lanes).astype(BF16), mask


def exchange(local, gathered, send, recv, row, place, pos):
    copies = []
    for step in range(1, pos):
        copies.append(
            remote(
                local,
                gathered.at[step - 1],
                send.at[step - 1],
                recv.at[step - 1],
                (row, lax.rem(place + step, pos)),
            )
        )
        copies[-1].start()
    for copy in copies:
        copy.wait()


def expert_kernel(dp, pos, groups, h_in, cot_in, logits, member, member_s, wout_in, *rest):
    count = bits_of(pos)
    wins, rest = rest[:3], rest[3:]
    mix, dh, dc, rest = rest[0], rest[1], rest[2], rest[3:]
    grads, rest = rest[:dp], rest[dp:]
    (share, share_s, dw, h, win, wout, stats, gathered, inner, gathered_inner), rest = (
        rest[:10],
        rest[10:],
    )
    (m_part, dy_part, m_t, z, slope, du), rest = rest[:6], rest[6:]
    ring_in, rest = rest[0], rest[1:]
    buffers, rest = rest[: 4 * count], rest[4 * count :]
    asend, arecv, bsend, brecv, csend, crecv, psend, precv, wsend, wrecv, gsend, grecv, dsend, drecv, osem, isem = (
        rest
    )
    row, place = lax.axis_index("dp"), lax.axis_index("pos")
    bits = my_bits(place, count)
    slots, length, width = h.shape
    right, left = lax.rem(row + 1, dp), lax.rem(row + dp - 1, dp)
    mates = [lax.rem(place + step, pos) for step in range(1, pos)]
    copies = pos // wout_in.shape[0]
    loads = [
        pltpu.make_async_copy(h_in, h, isem.at[0]),
        pltpu.make_async_copy(wout_in.at[place // copies], wout.at[row, place], isem.at[1]),
    ]
    middle = wout.shape[1] // 2
    halves = (slice(0, middle), slice(middle, 2 * middle))
    for step, part in enumerate(wins):
        loads.append(
            pltpu.make_async_copy(part, win.at[(row, left, right)[step]], isem.at[2 + step])
        )
    for copy in loads:
        copy.start()
    greet([(right, place), (left, place)] + [(row, mate) for mate in mates])
    pcopies = [
        remote(
            wout_in.at[mate // copies],
            wout.at[row, place],
            psend.at[step],
            precv.at[step],
            (row, mate),
        )
        for step, mate in enumerate(mates)
    ]

    for copy in pcopies:
        copy.start()

    def ring(which, distance):
        array = (win, wout)[which]
        sent = []
        for way, other in enumerate((right, left)):
            back = (distance - 1) * (1 - 2 * way)
            spot = (lax.rem(row + 2 * dp - back, dp),)
            if 2 * distance == dp:
                spot = spot + (halves[way],)
            at = (which * dp // 2 + distance - 1) * 2 + way
            sent.append(
                remote(array.at[spot], array.at[spot], wsend.at[at], wrecv.at[at], (other, place))
            )
            sent[-1].start()
        return sent

    def ring_on(which, first, passed):
        for distance in range(first, dp // 2 + 1):
            for copy in passed:
                copy.wait()
            passed = ring(which, distance)
        return passed

    win_ring = ring_on(0, 2, loads[2:])
    blocks = length // TILE
    lanes = slots * TILE
    experts = logits.shape[1]
    inside = [[member_s[g, s : s + 1, :] for s in range(slots)] for g in range(groups)]
    for g in range(groups):
        peak = jnp.full((experts, length), MASKED, F32)
        for s in range(slots):
            peak = jnp.maximum(peak, jnp.where(inside[g][s] > 0, logits[s], MASKED))
        total = jnp.zeros((experts, length), F32)
        for s in range(slots):
            total = total + jnp.where(inside[g][s] > 0, jnp.exp(logits[s] - peak), 0.0)
        stats[g] = peak
        stats[groups + g] = total
    exchange(stats, gathered, asend, arecv, row, place, pos)
    for copy in pcopies + loads[1:2]:
        copy.wait()
    wout_ring = ring(1, 1)
    for g in range(groups):
        peak = stats[g]
        for step in range(pos - 1):
            peak = jnp.maximum(peak, gathered[step, g])
        total = stats[groups + g] * jnp.exp(stats[g] - peak)
        for step in range(pos - 1):
            total = total + gathered[step, groups + g] * jnp.exp(gathered[step, g] - peak)
        stats[g] = peak
        stats[groups + g] = 1.0 / total
    parts = []
    for s in range(slots):
        peak = jnp.zeros((experts, length), F32)
        scale = jnp.zeros((experts, length), F32)
        some = jnp.zeros((1, length), F32)
        for g in range(groups):
            peak = peak + inside[g][s] * stats[g]
            scale = scale + inside[g][s] * stats[groups + g]
            some = some + inside[g][s]
        parts.append(jnp.exp(jnp.where(some > 0, logits[s] - peak, MASKED)) * scale)
        share_s[s] = parts[s]
    for block, part in enumerate(turn(parts)):
        share[block] = part

    lead = (2,) * (count + 1)
    loads[0].wait()

    def mixture(block, carry):
        where = pl.ds(pl.multiple_of(block * TILE, TILE), TILE)
        rows = h[:, where, :].reshape(lanes, width)
        weights, _ = block_weights(share[block], member, groups)
        m_part[..., where, :] = dot(weights, rows).astype(BF16).reshape(lead + (TILE, width))
        return carry

    def gradient(block, carry):
        where = pl.ds(pl.multiple_of(block * TILE, TILE), TILE)
        grads = h[:, where, :].reshape(lanes, width)
        weights, _ = block_weights(share[block], member, groups)
        dy_part[..., where, :] = (
            (32.0 * dot(weights, grads)).astype(BF16).reshape(lead + (TILE, width))
        )
        return carry

    plans = orders(count)
    every = list(range(count))[::-1]
    sources = (m_part, dy_part)
    targets = sources
    partner = lambda bit: (row, across(place, bits, bit))
    half = length // 2
    spans = (slice(0, half), slice(half, length))
    flying = {}

    def start(which, stage, sides=(0, 1)):
        for side in sides:
            lane_of = 2 * which + side
            bit = plans[side][stage]
            left = [b for b in every if b not in plans[side][:stage]]
            away = pick(left, {bit: 1 - bits[bit]})
            src = (
                sources[which].at[away + (slice(None), spans[side])]
                if stage == 0
                else buffers[lane_of * count + stage - 1].at[away]
            )
            at = lane_of * count + stage
            flying[which, side] = remote(
                src, buffers[at], bsend.at[at], brecv.at[at], partner(bit)
            )

    def launch(which, side):
        flying[which, side].start()

    def finish(which, stage, sides=(0, 1)):
        for side in sides:
            lane_of = 2 * which + side
            flying[which, side].wait()
            bit = plans[side][stage]
            left = [b for b in every if b not in plans[side][:stage]]
            near = pick(left, {bit: bits[bit]})
            target = buffers[lane_of * count + stage]
            if stage == 0:
                old = sources[which][near + (slice(None), spans[side])]
            else:
                old = buffers[lane_of * count + stage - 1][near]
            target[...] = (target[...].astype(F32) + old.astype(F32)).astype(BF16)

    def advance(which, stage, sides=(0, 1)):
        finish(which, stage, sides)
        if stage + 1 < count:
            start(which, stage + 1, sides)
            for side in sides:
                launch(which, side)

    def final(which):
        return jnp.concatenate(
            [buffers[(2 * which + side) * count + count - 1][...] for side in range(2)], axis=1
        ).reshape(2 * length, width)

    lower, upper = blocks // 2, blocks
    start(0, 0)
    refill = [
        pltpu.make_async_copy(cot_in.at[:, span], h.at[:, span], isem.at[5 + side])
        for side, span in enumerate(spans)
    ]
    lax.fori_loop(0, lower, mixture, 0)
    launch(0, 0)
    refill[0].start()
    lax.fori_loop(lower, upper, mixture, 0)
    launch(0, 1)
    refill[1].start()
    refill[0].wait()
    start(1, 0)
    advance(0, 0, (0,))
    lax.fori_loop(0, lower // 2, gradient, 0)
    advance(0, 0, (1,))
    lax.fori_loop(lower // 2, lower, gradient, 0)
    launch(1, 0)
    refill[1].wait()
    lax.fori_loop(lower, upper, gradient, 0)
    launch(1, 1)

    mine = pick(every, {b: bits[b] for b in every})

    def push(which, stage):
        for side in range(2):
            lane_of = 2 * which + side
            order = plans[side][::-1]
            bit = order[stage]
            spot = targets[which].at[
                pick(every, {b: bits[b] for b in every if b not in order[:stage]})
                + (slice(None), spans[side])
            ]
            at = lane_of * count + stage
            copy = remote(spot, spot, csend.at[at], crecv.at[at], partner(bit))
            copy.start()
            flying[which, side] = copy

    def publish(which, value):
        targets[which][mine] = value.astype(BF16).reshape(2, length, width)
        push(which, 0)

    def relay(which, stage):
        for side in range(2):
            flying[which, side].wait()
        if stage + 1 < count:
            push(which, stage + 1)

    for stage in range(1, count - 1):
        advance(0, stage)
    advance(1, 0)
    wout_ring = ring_on(1, 2, wout_ring)
    advance(0, count - 1)
    m = final(0)
    m_t[...] = jnp.transpose(m)
    for copy in (loads[2:] if dp < 4 else []) + win_ring:
        copy.wait()
    hidden = win.shape[-1]
    up = win[...].reshape(width, hidden)
    down = wout.reshape(hidden, width)
    piece = hidden // dp
    root = math.sqrt(2 / math.pi)
    for c in range(0, hidden, piece):
        u = dot(m, up[:, c : c + piece])
        square = u * u
        t = jnp.tanh(u * (root + root * 0.044715 * square))
        gate = 0.5 * (1.0 + t)
        active = (u * gate).astype(BF16)
        z[:, c : c + piece] = active
        slope[:, c : c + piece] = gate + (u * gate) * (1.0 - t) * (
            root + 3 * root * 0.044715 * square
        )
    for copy in wout_ring:
        copy.wait()
    y = dot(z[...], down[...])
    publish(0, y)
    for stage in range(1, count - 1):
        advance(1, stage)
    relay(0, 0)
    advance(1, count - 1)
    dy = final(1)
    dm = jnp.zeros((2 * length, width), F32)
    for c in range(0, hidden, piece):
        dz = dot(dy, down[c : c + piece, :], 1, 1).astype(BF16).astype(F32)
        grad = (dz * slope[:, c : c + piece]).astype(BF16)
        du[:, c : c + piece] = grad
        dm = dm + dot(grad, up[:, c : c + piece], 1, 1)
    publish(1, dm)
    share_of = width // dp

    def weights_of(step):
        whose = lax.rem(row + step, dp)
        strip = m_t[pl.ds(pl.multiple_of(whose * share_of, share_of), share_of), :]
        for c in range(0, hidden, width):
            at = c // width * share_of
            grads[step][0, at : at + share_of, :] = dot(strip, du[:, c : c + width]).astype(BF16)
        grads[step][1] = dot(
            z[:, pl.ds(pl.multiple_of(whose * piece, piece), piece)], dy, 0, 0
        ).astype(BF16)

    def pass_sums(distance):
        sent = []
        for way, other in enumerate((right, left)):
            step = distance if way == 0 else dp - distance
            span = slice(0, 2) if 2 * distance < dp else slice(way, way + 1)
            at = 2 * (distance - 2) + way
            arrived = ring_in.at[distance - 2, way, span]
            sent.append(
                (
                    remote(
                        grads[step].at[span], arrived, gsend.at[at], grecv.at[at], (other, place)
                    ),
                    grads[step - 1 if way == 0 else step + 1],
                    arrived,
                    span,
                )
            )
            sent[-1][0].start()
        return sent

    columns = hidden // width
    seats = [
        ((z, du)[s * 2 // slots], s % (slots // 2) // columns * length, s % columns * width)
        for s in range(slots)
    ]
    seat = lambda s: seats[s][0].at[
        seats[s][1] : seats[s][1] + length, seats[s][2] : seats[s][2] + width
    ]
    again = [
        pltpu.make_async_copy(h_in.at[s], seat(s), osem.at[1 + s]) for s in range(slots)
    ]
    mix_out = pltpu.make_async_copy(h, mix, osem.at[0])
    dh_out = [
        pltpu.make_async_copy(seat(s), dh.at[s], osem.at[1 + slots + s]) for s in range(slots)
    ]

    def chosen(block):
        return pl.ds(pl.multiple_of(block * TILE, TILE), TILE)

    def picked(whole, mask):
        products = whole.reshape(experts, groups, TILE, lanes) * mask[None]
        return jnp.sum(jnp.sum(products, axis=1), axis=1)

    def first_part(block, carry):
        where = chosen(block)
        weights, mask = block_weights(share[block], member, groups)
        rows = targets[0][..., where, :].reshape(experts * groups * TILE, width)
        grads = h[:, where, :].reshape(lanes, width)
        dw[block] = 32.0 * picked(dot(rows, grads, 1, 1), mask)
        h[:, where, :] = (
            (32.0 * dot(weights, rows, 0, 0)).astype(BF16).reshape(slots, TILE, width)
        )
        return carry

    def second_part(block, carry):
        weights, mask = block_weights(share[block], member, groups)
        rows = targets[1][..., chosen(block), :].reshape(experts * groups * TILE, width)
        places = [
            (
                ref,
                pl.ds(pl.multiple_of(top + block * TILE, TILE), TILE),
                slice(left_edge, left_edge + width),
            )
            for ref, top, left_edge in seats
        ]
        tokens = jnp.concatenate([ref[span, cols] for ref, span, cols in places], axis=0)
        dw[block] = dw[block] + picked(dot(rows, tokens, 1, 1), mask)
        back = dot(weights, rows, 0, 0).astype(BF16)
        for s, (ref, span, cols) in enumerate(places):
            ref[span, cols] = back[s * TILE : (s + 1) * TILE]
        return carry

    weights_of(dp // 2)
    passed = pass_sums(dp // 2)
    relay(1, 0)
    for distance in range(dp // 2 - 1, 0, -1):
        weights_of(distance)
        weights_of(dp - distance)
        if distance == 1:
            weights_of(0)
            for stage in range(1, count):
                relay(0, stage)
            for copy in again:
                copy.start()
            lax.fori_loop(0, blocks, first_part, 0)
            mix_out.start()
            for stage in range(1, count - 1):
                relay(1, stage)
        for copy, target, arrived, span in passed:
            copy.wait()
            target[span] = (target[span].astype(F32) + arrived[...].astype(F32)).astype(BF16)
        passed = pass_sums(distance) if distance > 1 else []
    for copy in again:
        copy.wait()
    flying[1, 0].wait()
    lax.fori_loop(0, lower, second_part, 0)
    flying[1, 1].wait()
    lax.fori_loop(lower, upper, second_part, 0)
    for copy in dh_out:
        copy.start()
    grads_s = turn([dw[b] for b in range(blocks)])
    for g in range(groups):
        total = jnp.zeros((experts, length), F32)
        for s in range(slots):
            total = total + inside[g][s] * share_s[s] * grads_s[s]
        inner[g] = total
    exchange(inner, gathered_inner, dsend, drecv, row, place, pos)
    sums = []
    for g in range(groups):
        total = inner[g]
        for step in range(pos - 1):
            total = total + gathered_inner[step, g]
        sums.append(total)
    for s in range(slots):
        mean = jnp.zeros((experts, length), F32)
        for g in range(groups):
            mean = mean + inside[g][s] * sums[g]
        dc[s] = (share_s[s] * (grads_s[s] - mean)).astype(BF16)
    for copy in [mix_out] + dh_out:
        copy.wait()


def mix_experts(dp, pos, groups, h, cot, logits, member, member_s, expert_out, win_parts):
    slots, length, width = h.shape
    experts = logits.shape[1]
    part = expert_out.shape[1:]
    lead = (2,) * (bits_of(pos) + 1)
    hidden = win_parts[0].shape[-1]
    blocks = length // TILE
    count = bits_of(pos)
    vmem = pl.BlockSpec(memory_space=pltpu.VMEM)
    hbm = pl.BlockSpec(memory_space=pl.ANY)
    rows = 2 * length
    dma = pltpu.SemaphoreType.DMA
    return pl.pallas_call(
        lambda *refs: expert_kernel(dp, pos, groups, *refs),
        out_shape=[
            jax.ShapeDtypeStruct(h.shape, BF16),
            jax.ShapeDtypeStruct(h.shape, BF16),
            jax.ShapeDtypeStruct(logits.shape, BF16),
        ]
        + [jax.ShapeDtypeStruct((2, hidden // dp, width), BF16)] * dp,
        in_specs=[hbm, hbm, vmem, vmem, vmem, hbm] + [hbm] * 3,
        out_specs=[hbm, hbm, vmem] + [vmem] * dp,
        scratch_shapes=[
            pltpu.VMEM((blocks, experts, slots * TILE), F32),
            pltpu.VMEM(logits.shape, F32),
            pltpu.VMEM((blocks, experts, slots * TILE), F32),
            pltpu.VMEM(h.shape, BF16),
            pltpu.VMEM((dp,) + win_parts[0].shape, BF16),
            pltpu.VMEM((dp, pos) + part, BF16),
            pltpu.VMEM((2 * groups, experts, slots * TILE), F32),
            pltpu.VMEM((pos - 1, 2 * groups, experts, slots * TILE), F32),
            pltpu.VMEM((groups, experts, length), F32),
            pltpu.VMEM((pos - 1, groups, experts, length), F32),
            pltpu.VMEM(lead + (length, width), BF16),
            pltpu.VMEM(lead + (length, width), BF16),
            pltpu.VMEM((width, rows), BF16),
            pltpu.VMEM((rows, hidden), BF16),
            pltpu.VMEM((rows, hidden), F32),
            pltpu.VMEM((rows, hidden), BF16),
            pltpu.VMEM((dp // 2 - 1, 2, 2, hidden // dp, width), BF16),
        ]
        + [
            pltpu.VMEM((2,) * (count - stage) + (length // 2, width), BF16)
            for _ in range(4)
            for stage in range(count)
        ]
        + [
            dma((pos - 1,)),
            dma((pos - 1,)),
            dma((4 * count,)),
            dma((4 * count,)),
            dma((4 * count,)),
            dma((4 * count,)),
            dma((pos - 1,)),
            dma((pos - 1,)),
            dma((2 * dp,)),
            dma((2 * dp,)),
            dma((2 * (dp // 2 - 1),)),
            dma((2 * (dp // 2 - 1),)),
            dma((pos - 1,)),
            dma((pos - 1,)),
            dma((1 + 2 * slots,)),
            dma((7,)),
        ],
        compiler_params=pltpu.CompilerParams(
            collective_id=2, has_side_effects=True, vmem_limit_bytes=VMEM_LIMIT
        ),
        name="mix_experts",
    )(h, cot, logits, member, member_s, expert_out, *win_parts)


from jax.sharding import PartitionSpec as P

MIXED_SEQUENCES = 32


def body(
    inputs,
    cotangent,
    counts,
    seq_rank,
    first_gain,
    first_bias,
    query_weight,
    key_weight,
    value_weight,
    output_weight,
    second_gain,
    second_bias,
    control_weight,
    expert_in,
    expert_out,
):
    capacity, length, features = inputs.shape
    dp, pos = lax.axis_size("dp"), lax.axis_size("pos")
    experts = control_weight.shape[1]
    groups = seq_rank.shape[1] // MIXED_SEQUENCES

    w_t, wk, wo, small, member, member_s, live, win = gather_weights(
        dp,
        pos,
        groups,
        capacity,
        query_weight,
        key_weight,
        value_weight,
        output_weight,
        jnp.stack([first_gain, first_bias, second_gain, second_bias]),
        control_weight.T,
        counts,
        seq_rank,
        expert_in,
    )
    count = live[0, :1]

    def send_rows(array, step):
        return lax.ppermute(array, "dp", [(i, (i + step) % dp) for i in range(dp)])

    wins = (win, send_rows(win, 1), send_rows(win, -1))

    q_t, k, v_t, ctx_t, x1, h, inverse, e_t, logits = forward(count, inputs, w_t, wk, wo, small)
    mix, dh, dc, *grads = mix_experts(
        dp, pos, groups, h, cotangent, logits, member, member_s, expert_out, wins
    )
    grads = (grads[0], send_rows(grads[1], 1), send_rows(grads[dp - 1], -1))
    layer_output, input_grad, grad_t, out_grad, vecs = backward(
        count, inputs, cotangent, x1, mix, dh, dc, q_t, k, v_t, ctx_t, inverse, e_t, w_t, wo, small
    )
    shard, *grads = scatter_weights(
        dp, pos, grad_t, out_grad, vecs, *grads
    )
    if pos > experts:
        grads = [
            jnp.sum(part.astype(F32).reshape((experts, pos // experts) + part.shape[1:]), axis=1)
            for part in grads
        ]
    expert_in_grad, expert_out_grad = (part.astype(F32) for part in grads)
    tail = shard[:, 4 * features :]
    return (
        layer_output,
        input_grad,
        tail[:, 2],
        tail[:, 3],
        shard[:, :features],
        shard[:, features : 2 * features],
        shard[:, 2 * features : 3 * features],
        shard[:, 3 * features : 4 * features],
        tail[:, 0],
        tail[:, 1],
        tail[:, 8 : 8 + experts],
        expert_in_grad,
        expert_out_grad,
    )


def solution(mesh):
    both = ("dp", "pos")
    vector, matrix, cube = P(both), P(both, None), P(both, None, None)
    middle = P(None, both, None)
    return jax.shard_map(
        body,
        mesh=mesh,
        in_specs=(
            cube,
            cube,
            P("dp", None),
            P("dp", None),
            vector,
            vector,
            matrix,
            matrix,
            matrix,
            matrix,
            vector,
            vector,
            matrix,
            middle,
            middle,
        ),
        out_specs=(
            cube,
            cube,
            vector,
            vector,
            matrix,
            matrix,
            matrix,
            matrix,
            vector,
            vector,
            matrix,
            middle,
            middle,
        ),
        check_vma=False,
    )
```

```python
import math
import jax
import jax.numpy as jnp
from jax import lax
from jax.experimental import pallas as pl
from jax.experimental.pallas import tpu as pltpu

HEADS = 8
HEAD = 64
NORM_EPS = 1e-05
MASKED = -1e30
F32 = jnp.float32
BF16 = jnp.bfloat16
MIB = 1 << 20
VMEM_LIMIT = 62 * MIB


def dot(a, b, ca=1, cb=0):
    return lax.dot_general(a, b, (((ca,), (cb,)), ((), ())), preferred_element_type=F32)


def normalize(v):
    center = v - jnp.mean(v, axis=-1, keepdims=True)
    spread = jnp.mean(center * center, axis=-1, keepdims=True)
    scale = lax.rsqrt(spread + NORM_EPS)
    return center * scale, scale


def spread_heads(parts):
    return jnp.concatenate(
        [
            jnp.concatenate(
                [part if i == j else jnp.zeros_like(part) for i in range(len(parts))], axis=0
            )
            for j, part in enumerate(parts)
        ],
        axis=1,
    )


def forward_kernel(count, x, w_t, wk, wo, small, q_t, k, v_t, ctx_t, x1, h, inverse, e_t, logits):
    g1, b1, g2, b2 = (small[i : i + 1] for i in range(4))
    slots, length, width = x.shape
    router = small[8:16].astype(BF16)
    wq_t, wv_t = w_t.at[:width], w_t.at[2 * width :]
    half = length // 2
    causal = lax.broadcasted_iota(jnp.int32, (half, half), 0) <= lax.broadcasted_iota(
        jnp.int32, (half, half), 1
    )

    def one():
        source = x[...].reshape(slots * length, width).astype(F32)
        xhat, _ = normalize(source)
        a = (xhat * g1 + b1).astype(BF16)
        qs = (dot(wq_t[...], a, 1, 1).astype(BF16) * 0.125).astype(BF16)
        ks = dot(a, wk[...]).astype(BF16)
        vs = dot(wv_t[...], a, 1, 1).astype(BF16)
        k[...] = ks.reshape(slots, length, width)
        ones = jnp.ones((16, length), BF16)
        parts = [[] for _ in range(slots)]
        sums = [[] for _ in range(slots)]
        cols = [slice(s * length, (s + 1) * length) for s in range(slots)]
        for s in range(slots):
            q_t[s] = qs[:, cols[s]]
            v_t[s] = vs[:, cols[s]]
        for base in range(0, HEADS, 4):
            for s in range(slots):
                four = slice(base * HEAD, (base + 4) * HEAD)
                spread_q = spread_heads(
                    [
                        qs[(base + i) * HEAD : (base + i + 1) * HEAD, cols[s]] for i in range(4)
                    ]
                )
                scores = dot(ks[cols[s], four], spread_q)
                exps = []
                for j in range(4):
                    st = scores[:, j * length : (j + 1) * length]
                    s00 = jnp.where(causal, st[:half, :half], MASKED)
                    s01 = st[:half, half:]
                    s11 = jnp.where(causal, st[half:, half:], MASKED)
                    m0 = jnp.max(s00, axis=0, keepdims=True)
                    m1 = jnp.maximum(
                        jnp.max(s01, axis=0, keepdims=True), jnp.max(s11, axis=0, keepdims=True)
                    )
                    e00 = jnp.exp(s00 - m0).astype(BF16)
                    e01 = jnp.exp(s01 - m1).astype(BF16)
                    e11 = jnp.exp(s11 - m1).astype(BF16)
                    et = jnp.concatenate(
                        [
                            jnp.concatenate([e00, e01], axis=1),
                            jnp.concatenate([jnp.zeros_like(e00), e11], axis=1),
                        ],
                        axis=0,
                    )
                    e_t[s, base + j] = et
                    exps.append(et)
                for j in range(0, 4, 2):
                    head = base + j
                    va = jnp.concatenate(
                        [
                            vs[head * HEAD : (head + 1) * HEAD, cols[s]],
                            ones,
                            vs[(head + 1) * HEAD : (head + 2) * HEAD, cols[s]],
                            ones,
                        ],
                        axis=0,
                    )
                    both = dot(va, jnp.concatenate(exps[j : j + 2], axis=1))
                    for i in range(2):
                        full = both[i * 80 : i * 80 + 80, i * length : (i + 1) * length]
                        total = full[HEAD : HEAD + 1]
                        scale = 1.0 / total
                        parts[s].append((full[:HEAD] * scale).astype(BF16))
                        sums[s].append(scale)
        outs = []
        for s in range(slots):
            ctx = jnp.concatenate(parts[s], axis=0)
            ctx_t[s] = ctx
            inverse[s] = jnp.concatenate(sums[s], axis=0)
            outs.append(ctx)
        residual = source + dot(jnp.concatenate(outs, axis=1), wo[...], 0, 0)
        x1[...] = residual.reshape(slots, length, width)
        xhat2, _ = normalize(residual)
        hidden = (xhat2 * g2 + b2).astype(BF16)
        h[...] = hidden.reshape(slots, length, width)
        for s in range(slots):
            logits[s] = dot(router, hidden[cols[s], :], 1, 1)

    live = pl.program_id(0) * slots < count[0]
    pl.when(live)(one)

    @pl.when(jnp.logical_not(live))
    def _():
        h[...] = jnp.zeros((slots, length, width), BF16)
        logits[...] = jnp.zeros_like(logits)


def forward(count, x, w_t, wk, wo, small, block=2):
    slots, length, width = x.shape
    per = lambda rows, cols: pl.BlockSpec((block, rows, cols), lambda i, c: (i, 0, 0))
    whole = lambda a: pl.BlockSpec(a.shape, lambda i, c: (0,) * a.ndim)
    shape = lambda rows, cols, kind: jax.ShapeDtypeStruct((slots, rows, cols), kind)
    return pl.pallas_call(
        forward_kernel,
        grid_spec=pltpu.PrefetchScalarGridSpec(
            num_scalar_prefetch=1,
            grid=(slots // block,),
            in_specs=[per(length, width)]
            + [whole(a) for a in (w_t, wk, wo, small)],
            out_specs=[
                per(width, length),
                per(length, width),
                per(width, length),
                per(width, length),
                per(length, width),
                per(length, width),
                per(HEADS, length),
            ]
            + [pl.BlockSpec((block, HEADS, length, length), lambda i, c: (i, 0, 0, 0)), per(HEADS, length)],
        ),
        out_shape=[
            shape(width, length, BF16),
            shape(length, width, BF16),
            shape(width, length, BF16),
            shape(width, length, BF16),
            shape(length, width, F32),
            shape(length, width, BF16),
            shape(HEADS, length, F32),
        ]
        + [jax.ShapeDtypeStruct((slots, HEADS, length, length), BF16), shape(8, length, F32)] ,
        compiler_params=pltpu.CompilerParams(vmem_limit_bytes=VMEM_LIMIT),
        cost_estimate=pl.CostEstimate(
            flops=40_000_000_000, bytes_accessed=40 * MIB, transcendentals=8_000_000
        ),
        name="attention_forward",
    )(count, x, w_t, wk, wo, small)


def norm_back(grad, xhat, scale):
    return scale * (
        grad
        - jnp.mean(grad, axis=-1, keepdims=True)
        - xhat * jnp.mean(grad * xhat, axis=-1, keepdims=True)
    )


def backward_kernel(
    count, x, cot, x1, mix, dh, dc, q_t, k, v_t, ctx_t, inverse, e_t, w_t, wo, small,
    lo, dx, grad_t, out_grad, vecs, back_t,
):
    slots, length, width = x.shape
    half = length // 2
    step = pl.program_id(0)

    @pl.when(step == 0)
    def _():
        grad_t[...] = jnp.zeros_like(grad_t)
        out_grad[...] = jnp.zeros_like(out_grad)
        vecs[...] = jnp.zeros_like(vecs)

    g1, b1, g2, b2 = (small[i : i + 1] for i in range(4))
    router = small[8:16].astype(BF16)

    def one():
        tokens = slots * length
        cols = [slice(s * length, (s + 1) * length) for s in range(slots)]
        row = lax.broadcasted_iota(jnp.int32, (tokens, 1), 0) // length + step * slots
        live = row < count[0]
        keep = lambda v: v if slots == 1 else jnp.where(live, v, 0.0)
        residual = x1[...].reshape(tokens, width)
        xhat2, scale2 = normalize(residual)
        lo[...] = (
            keep(residual + mix[...].reshape(tokens, width).astype(F32))
            .astype(BF16)
            .reshape(slots, length, width)
        )
        hidden = (xhat2 * g2 + b2).astype(BF16)
        routed = []
        for s in range(slots):
            routed.append(dot(dc[s], router, 0, 0))
            vecs[8:16] += dot(dc[s], hidden[cols[s], :])
        grad_h = (
            (dh[...].reshape(tokens, width).astype(F32) + jnp.concatenate(routed, axis=0))
            .astype(BF16)
            .astype(F32)
        )
        vecs[0:1] += jnp.sum(grad_h * xhat2, axis=0, keepdims=True)
        vecs[1:2] += jnp.sum(grad_h, axis=0, keepdims=True)
        dx1 = keep(
            cot[...].reshape(tokens, width).astype(F32) + norm_back(grad_h * g2, xhat2, scale2)
        )
        datt = dx1.astype(BF16)
        dctx = dot(wo[...], datt, 1, 1).astype(BF16)
        out_grad[...] += dot(jnp.concatenate([ctx_t[s] for s in range(slots)], axis=1), datt)
        zero = jnp.zeros((half, half), BF16)
        for s in range(slots):
            kt = jnp.transpose(k[s])
            vn = jnp.transpose(v_t[s])
            scaled = []
            inners = []
            for head in range(HEADS):
                rows = slice(head * HEAD, (head + 1) * HEAD)
                part = dctx[rows, cols[s]].astype(F32) * inverse[s, head : head + 1, :]
                scaled.append(part.astype(BF16))
                inners.append(jnp.sum(ctx_t[s, rows, :].astype(F32) * part, axis=0, keepdims=True))
            for base in range(0, HEADS, 4):
                four = slice(base * HEAD, (base + 4) * HEAD)
                dprobs = dot(vn[:, four], spread_heads(scaled[base : base + 4]))
                grads = []
                exps = []
                for j in range(4):
                    head = base + j
                    et = e_t[s, head]
                    dp = dprobs[:, j * length : (j + 1) * length]
                    inner = inners[head]
                    d00 = et[:half, :half].astype(F32) * (dp[:half, :half] - inner[:, :half])
                    d01 = et[:half, half:].astype(F32) * (dp[:half, half:] - inner[:, half:])
                    d11 = et[half:, half:].astype(F32) * (dp[half:, half:] - inner[:, half:])
                    grads.append(
                        jnp.concatenate(
                            [
                                jnp.concatenate([d00.astype(BF16), d01.astype(BF16)], axis=1),
                                jnp.concatenate([zero, d11.astype(BF16)], axis=1),
                            ],
                            axis=0,
                        )
                    )
                    exps.append(et)
                tall = jnp.concatenate(grads, axis=0)
                dk = dot(q_t[s, four, :], tall, 1, 1)
                dv = dot(
                    jnp.concatenate(scaled[base : base + 4], axis=0),
                    jnp.concatenate(exps, axis=0),
                    1,
                    1,
                )
                dq = [
                    dot(
                        kt[(base + j) * HEAD : (base + j + 2) * HEAD, :],
                        jnp.concatenate(grads[j : j + 2], axis=1),
                    )
                    * 0.125
                    for j in range(0, 4, 2)
                ]
                for j in range(4):
                    begin = (base + j) * HEAD
                    spot = slice(j * length, (j + 1) * length)
                    inside = slice(j * HEAD, (j + 1) * HEAD)
                    i = j % 2
                    back_t[begin : begin + HEAD, cols[s]] = dq[j // 2][
                        i * HEAD : (i + 1) * HEAD, i * length : (i + 1) * length
                    ].astype(BF16)
                    back_t[width + begin : width + begin + HEAD, cols[s]] = dk[inside, spot].astype(
                        BF16
                    )
                    back_t[2 * width + begin : 2 * width + begin + HEAD, cols[s]] = dv[
                        inside, spot
                    ].astype(BF16)
        source = x[...].reshape(tokens, width).astype(F32)
        xhat1, scale1 = normalize(source)
        a = (xhat1 * g1 + b1).astype(BF16)
        back = back_t[...]
        grad_t[...] += dot(back, a)
        da = dot(back, w_t[...], 0, 0)
        vecs[2:3] += jnp.sum(da * xhat1, axis=0, keepdims=True)
        vecs[3:4] += jnp.sum(da, axis=0, keepdims=True)
        dx[...] = (
            keep(dx1 + norm_back(da * g1, xhat1, scale1))
            .astype(BF16)
            .reshape(slots, length, width)
        )

    some = step * slots < count[0]
    pl.when(some)(one)

    @pl.when(jnp.logical_not(some))
    def _():
        dx[...] = jnp.zeros((slots, length, width), BF16)
        lo[...] = jnp.zeros((slots, length, width), BF16)


def backward(count, x, cot, x1, mix, dh, dc, q_t, k, v_t, ctx_t, inverse, e_t, w_t, wo, small, block=2):
    slots, length, width = x.shape
    per = lambda a: pl.BlockSpec(
        (block,) + a.shape[1:], lambda i, c: (i,) + (0,) * (len(a.shape) - 1)
    )
    whole = lambda a: pl.BlockSpec(a.shape, lambda i, c: (0,) * len(a.shape))
    outs = [
        jax.ShapeDtypeStruct((3 * width, width), F32),
        jax.ShapeDtypeStruct((width, width), F32),
        jax.ShapeDtypeStruct((16, width), F32),
    ]
    batched = (x, cot, x1, mix, dh, dc, q_t, k, v_t, ctx_t, inverse, e_t)
    shared = (w_t, wo, small)
    return pl.pallas_call(
        backward_kernel,
        grid_spec=pltpu.PrefetchScalarGridSpec(
            num_scalar_prefetch=1,
            grid=(slots // block,),
            in_specs=[per(a) for a in batched] + [whole(a) for a in shared],
            out_specs=[per(x), per(x)] + [whole(a) for a in outs],
            scratch_shapes=[pltpu.VMEM((3 * width, block * length), BF16)],
        ),
        out_shape=[jax.ShapeDtypeStruct(x.shape, BF16)] * 2 + outs,
        compiler_params=pltpu.CompilerParams(vmem_limit_bytes=VMEM_LIMIT),
        cost_estimate=pl.CostEstimate(
            flops=100_000_000_000, bytes_accessed=60 * MIB, transcendentals=8_000_000
        ),
        name="attention_backward",
    )(count, *batched, *shared)


MESH = pl.DeviceIdType.MESH
TILE = 16


def bits_of(size):
    return size.bit_length() - 1


def orders(count):
    first = list(range(count))
    second = list(first)
    if count > 2:
        second[1], second[2] = second[2], second[1]
    return first, second


def greet(peers):
    barrier = pltpu.get_barrier_semaphore()
    for peer in peers:
        pl.semaphore_signal(barrier, inc=1, device_id=peer, device_id_type=MESH)
    pl.semaphore_wait(barrier, len(peers))


def my_bits(place, count):
    return [lax.rem(place // (1 << bit), 2) for bit in range(count)]


def across(place, bits, bit):
    return place + (1 - 2 * bits[bit]) * (1 << bit)


def pick(remaining, chosen):
    return tuple(chosen[bit] if bit in chosen else slice(None) for bit in remaining)


def remote(src, dst, send, recv, device):
    return pltpu.make_async_remote_copy(
        src_ref=src,
        dst_ref=dst,
        send_sem=send,
        recv_sem=recv,
        device_id=device,
        device_id_type=MESH,
    )


def gather_kernel(
    dp, pos, groups, slots,
    wq, wk, wv, wo, vectors, router, counts, ranks, ein,
    w_t, wk_out, wo_out, vt, member, member_s, live, win,
    held, zsend, zrecv, send, recv, esend, erecv, lsem,
):
    count = bits_of(pos)
    row, place = lax.axis_index("dp"), lax.axis_index("pos")
    bits = my_bits(place, count)
    others = [lax.rem(row + step, dp) for step in range(1, dp)]
    mates = [lax.rem(place + step, pos) for step in range(1, pos)]
    greet([(other, place) for other in others] + [(row, mate) for mate in mates])
    rows, width = wq.shape
    every = list(range(count))[::-1]
    here = pick(every, {bit: bits[bit] for bit in every})
    for index, weight in enumerate((wq, wk, wv, wo)):
        held[(row,) + here + (slice(None), slice(index * width, (index + 1) * width))] = weight[...]
    tall = jnp.concatenate(
        [
            vectors[...].astype(F32),
            jnp.zeros((8 - vectors.shape[0], rows), F32),
            router[...].astype(F32),
            jnp.zeros((120 - router.shape[0], rows), F32),
        ],
        axis=0,
    )
    square = jnp.concatenate([tall, jnp.zeros((128, 128 - rows), F32)], axis=1)
    held[(row,) + here + (slice(None), slice(4 * width, 4 * width + 128))] = jnp.transpose(square)[
        :rows
    ].astype(BF16)

    copies = pos // ein.shape[0]
    local = pltpu.make_async_copy(ein.at[place // copies], win.at[place], lsem.at[0])
    local.start()
    zcopies = []
    for step, other in enumerate(others):
        spot = held.at[(row,) + here]
        zcopies.append(remote(spot, spot, zsend.at[step], zrecv.at[step], (other, place)))
        zcopies[-1].start()

    ecopies = []
    for step, mate in enumerate(mates):
        ecopies.append(
            remote(
                ein.at[mate // copies], win.at[place], esend.at[step], erecv.at[step], (row, mate)
            )
        )
        ecopies[-1].start()

    first, second = orders(count)
    plans = (first[::-1], second[::-1])

    def push(block, stage):
        order = plans[block % 2]
        bit = order[stage]
        whose = lax.rem(row + dp - block, dp)
        spot = held.at[
            (whose,) + pick(every, {b: bits[b] for b in every if b not in order[:stage]})
        ]
        at = block * count + stage
        copy = remote(spot, spot, send.at[at], recv.at[at], (row, across(place, bits, bit)))
        copy.start()
        return copy

    flying = {0: push(0, 0)}
    lanes = slots * TILE
    which = lax.broadcasted_iota(jnp.int32, (1, pos), 1)
    begin = jnp.sum(jnp.where(which < place, counts[...], 0), axis=1, keepdims=True)
    mine = jnp.sum(jnp.where(which == place, counts[...], 0), axis=1, keepdims=True)
    live[...] = jnp.broadcast_to(mine, live.shape)
    slot = lax.broadcasted_iota(jnp.int32, (1, lanes), 1) // TILE
    wanted = jnp.where(slot < mine, begin + slot, -1)
    table = (ranks[...] // 32).astype(F32) + 1.0
    size = table.shape[1]
    if size < 128:
        table = jnp.concatenate([table, jnp.zeros((1, 128 - size), F32)], axis=1)
    column = jnp.transpose(jnp.broadcast_to(table, (128, 128)))[:, :1]
    match = lax.broadcasted_iota(jnp.int32, (128, lanes), 0) == wanted
    ids = jnp.sum(jnp.where(match, column, 0.0), axis=0, keepdims=True)
    for g in range(groups):
        member[g : g + 1, :] = (ids == float(g + 1)).astype(F32)
    slot = lax.broadcasted_iota(jnp.int32, (slots, 1), 0)
    wanted = jnp.where(slot < mine, begin + slot, -1)
    match = lax.broadcasted_iota(jnp.int32, (slots, 128), 1) == wanted
    ids = jnp.sum(jnp.where(match, table, 0.0), axis=1, keepdims=True)
    for g in range(groups):
        member_s[g] = jnp.broadcast_to((ids == float(g + 1)).astype(F32), member_s.shape[1:])

    for block in range(1, dp):
        zcopies[block - 1].wait()
        flying[block] = push(block, 0)
    for stage in range(1, count):
        for block in range(dp):
            flying[block].wait()
            flying[block] = push(block, stage)
    for block in range(dp):
        flying[block].wait()
    full = held[...].reshape(dp * pos * rows, 4 * width + 128)
    for index in range(3):
        w_t[index * width : (index + 1) * width, :] = jnp.transpose(
            full[:, index * width : (index + 1) * width]
        )
    wk_out[...] = full[:, width : 2 * width]
    wo_out[...] = full[:, 3 * width : 4 * width]
    vt[...] = jnp.transpose(full[:, 4 * width :])[:16, :].astype(F32)
    for copy in [local] + ecopies:
        copy.wait()


def gather_weights(dp, pos, groups, slots, wq, wk, wv, wo, vectors, router, counts, ranks, ein):
    rows, width = wq.shape
    whole = rows * dp * pos
    vmem = pl.BlockSpec(memory_space=pltpu.VMEM)
    hbm = pl.BlockSpec(memory_space=pl.ANY)
    count = bits_of(pos)
    dma = pltpu.SemaphoreType.DMA
    return pl.pallas_call(
        lambda *refs: gather_kernel(dp, pos, groups, slots, *refs),
        out_shape=[
            jax.ShapeDtypeStruct((3 * width, whole), BF16),
            jax.ShapeDtypeStruct((whole, width), BF16),
            jax.ShapeDtypeStruct((whole, width), BF16),
            jax.ShapeDtypeStruct((16, whole), F32),
            jax.ShapeDtypeStruct((groups, slots * TILE), F32),
            jax.ShapeDtypeStruct((groups, slots, slots * TILE), F32),
            jax.ShapeDtypeStruct((1, 128), jnp.int32),
            jax.ShapeDtypeStruct((pos,) + ein.shape[1:], BF16),
        ],
        in_specs=[vmem] * 8 + [hbm],
        out_specs=[vmem] * 7 + [hbm],
        scratch_shapes=[
            pltpu.VMEM((dp,) + (2,) * count + (rows, 4 * width + 128), BF16),
            dma((dp - 1,)),
            dma((dp - 1,)),
            dma((dp * count,)),
            dma((dp * count,)),
            dma((pos - 1,)),
            dma((pos - 1,)),
            dma((1,)),
        ],
        compiler_params=pltpu.CompilerParams(
            collective_id=0, has_side_effects=True, vmem_limit_bytes=VMEM_LIMIT
        ),
        name="gather_weights",
    )(wq, wk, wv, wo, vectors, router, counts, ranks, ein)


def scatter_kernel(dp, pos, grad_in, out_in, vecs, *rest):
    count = bits_of(pos)
    parts, rest = rest[:3], rest[3:]
    out, ein_got, eout_got, held, grad_t, out_grad, grads, isem, *rest = rest
    loads = [pltpu.make_async_copy(part, grads.at[i], isem.at[i]) for i, part in enumerate(parts)]
    loads.append(pltpu.make_async_copy(grad_in, grad_t, isem.at[3]))
    loads.append(pltpu.make_async_copy(out_in, out_grad, isem.at[4]))
    for copy in loads:
        copy.start()
    buffers, slots, rest = rest[: 2 * count], rest[2 * count], rest[2 * count + 1 :]
    send, recv, esend, erecv, ein_mine, eout_mine = rest
    row, place = lax.axis_index("dp"), lax.axis_index("pos")
    bits = my_bits(place, count)
    others = [lax.rem(row + step, dp) for step in range(1, dp)]
    mates = [lax.rem(place + step, pos) for step in range(1, pos)]
    greet([(other, place) for other in others] + [(row, mate) for mate in mates])
    width = out_grad.shape[1]
    ecopies = []
    for copy in loads[:3]:
        copy.wait()
    for index, (mine, got) in enumerate(((ein_mine, ein_got), (eout_mine, eout_got))):
        total = grads[0, index].astype(F32)
        for i in range(1, 3):
            total = total + grads[i, index].astype(F32)
        total = total.astype(BF16)
        if index == 0:
            strip = width // dp
            for c in range(0, mine.shape[2], width):
                at = c // width * strip
                mine[:, :, c : c + width] = total[at : at + strip].reshape(
                    mine.shape[:2] + (width,)
                )
        else:
            mine[...] = total.reshape(mine.shape)
        for step, mate in enumerate(mates):
            at = index * (pos - 1) + step
            ecopies.append(
                remote(mine.at[mate], got.at[place], esend.at[at], erecv.at[at], (row, mate))
            )
            if index == 0:
                ecopies[-1].start()
        got[place] = mine[place]
    for copy in loads[3:]:
        copy.wait()
    lead = held.shape[:-1]
    for index in range(3):
        held[..., index * width : (index + 1) * width] = (
            jnp.transpose(grad_t[index * width : (index + 1) * width, :].astype(BF16)).reshape(
                lead + (width,)
            )
        )
    held[..., 3 * width : 4 * width] = out_grad[...].astype(BF16).reshape(lead + (width,))
    tail = jnp.concatenate([vecs[...], jnp.zeros((112, vecs.shape[1]), F32)], axis=0)
    held[..., 4 * width :] = jnp.transpose(tail).astype(BF16).reshape(lead + (128,))
    used = 0
    halves = (slice(0, dp // 2), slice(dp // 2, dp))
    plans = orders(count)
    current = [held.at[half] for half in halves]
    remaining = [list(range(count))[::-1] for _ in halves]
    for stage in range(count):
        copies = []
        for side in range(2):
            bit = plans[side][stage]
            away = (slice(None),) + pick(remaining[side], {bit: 1 - bits[bit]})
            copies.append(
                remote(
                    current[side].at[away],
                    buffers[side * count + stage],
                    send.at[used],
                    recv.at[used],
                    (row, across(place, bits, bit)),
                )
            )
            used += 1
        for copy in copies:
            copy.start()
        if stage == count - 1:
            for copy in ecopies[len(mates) :]:
                copy.start()
        for side in range(2):
            copies[side].wait()
            bit = plans[side][stage]
            near = (slice(None),) + pick(remaining[side], {bit: bits[bit]})
            target = buffers[side * count + stage]
            target[...] = (
                target[...].astype(F32) + current[side][near].astype(F32)
            ).astype(BF16)
            current[side] = target
            remaining[side] = [b for b in remaining[side] if b != bit]
    joined = jnp.concatenate([current[0][...], current[1][...]], axis=0)
    slots[1] = joined
    copies = []
    for step, other in enumerate(others):
        copies.append(
            remote(
                slots.at[1, other],
                slots.at[0, row],
                send.at[used],
                recv.at[used],
                (other, place),
            )
        )
        used += 1
        copies[-1].start()
    for copy in copies:
        copy.wait()
    total = slots[1, row].astype(F32)
    for other in others:
        total = total + slots[0, other].astype(F32)
    out[...] = total
    for copy in ecopies:
        copy.wait()


def scatter_weights(dp, pos, grad_t, out_grad, vecs, *grads):
    width = out_grad.shape[1]
    rows = out_grad.shape[0] // (dp * pos)
    wide = 4 * width + 128
    hidden = grads[0].shape[1] * dp
    hbm = pl.BlockSpec(memory_space=pl.ANY)
    ein_shape = (width // (dp * pos), hidden)
    eout_shape = (hidden // (dp * pos), width)
    vmem = pl.BlockSpec(memory_space=pltpu.VMEM)
    count = bits_of(pos)
    total = dp - 1 + 2 * count
    return pl.pallas_call(
        lambda *refs: scatter_kernel(dp, pos, *refs),
        out_shape=[
            jax.ShapeDtypeStruct((rows, wide), F32),
            jax.ShapeDtypeStruct((pos,) + ein_shape, BF16),
            jax.ShapeDtypeStruct((pos,) + eout_shape, BF16),
        ],
        in_specs=[hbm, hbm, vmem] + [hbm] * 3,
        out_specs=[vmem] * 3,
        scratch_shapes=[
            pltpu.VMEM((dp,) + (2,) * count + (rows, wide), BF16),
            pltpu.VMEM(grad_t.shape, F32),
            pltpu.VMEM(out_grad.shape, F32),
            pltpu.VMEM((3,) + grads[0].shape, BF16),
            pltpu.SemaphoreType.DMA((5,)),
        ]
        + [
            pltpu.VMEM((dp // 2,) + (2,) * (count - 1 - stage) + (rows, wide), BF16)
            for _ in range(2)
            for stage in range(count)
        ]
        + [
            pltpu.VMEM((2, dp, rows, wide), BF16),
            pltpu.SemaphoreType.DMA((total,)),
            pltpu.SemaphoreType.DMA((total,)),
            pltpu.SemaphoreType.DMA((2 * (pos - 1),)),
            pltpu.SemaphoreType.DMA((2 * (pos - 1),)),
            pltpu.VMEM((pos,) + ein_shape, BF16),
            pltpu.VMEM((pos,) + eout_shape, BF16),
        ],
        compiler_params=pltpu.CompilerParams(
            collective_id=1, has_side_effects=True, vmem_limit_bytes=VMEM_LIMIT
        ),
        name="scatter_weights",
    )(grad_t, out_grad, vecs, *grads)


def finish_kernel(shard, ein_got, eout_got, *outs):
    width = outs[0].shape[1]
    rows = shard.shape[0]
    for index in range(4):
        outs[index][...] = shard[:, index * width : (index + 1) * width]
    tail = jnp.transpose(
        jnp.concatenate([shard[:, 4 * width :], jnp.zeros((128 - rows, 128), F32)], axis=0)
    )
    outs[4][...] = tail[:8, :rows]
    outs[5][...] = tail[8:16, :rows]
    for got, target in ((ein_got, outs[6]), (eout_got, outs[7])):
        experts = target.shape[0]
        copies = got.shape[0] // experts
        for expert in range(experts):
            total = got[expert * copies].astype(F32)
            for copy in range(1, copies):
                total = total + got[expert * copies + copy].astype(F32)
            target[expert] = total


def finish(experts, shard, ein_got, eout_got):
    rows = shard.shape[0]
    width = (shard.shape[1] - 128) // 4
    vmem = pl.BlockSpec(memory_space=pltpu.VMEM)
    return pl.pallas_call(
        finish_kernel,
        out_shape=[jax.ShapeDtypeStruct((rows, width), F32)] * 4
        + [jax.ShapeDtypeStruct((8, rows), F32)] * 2
        + [
            jax.ShapeDtypeStruct((experts,) + ein_got.shape[1:], F32),
            jax.ShapeDtypeStruct((experts,) + eout_got.shape[1:], F32),
        ],
        in_specs=[vmem] * 3,
        out_specs=[vmem] * 8,
        compiler_params=pltpu.CompilerParams(vmem_limit_bytes=VMEM_LIMIT),
        name="finish",
    )(shard, ein_got, eout_got)


def turn(parts):
    size = len(parts)
    lanes = parts[0].shape[1]
    tile = lax.broadcasted_iota(jnp.int32, parts[0].shape, 1) // TILE
    step = 1
    while step < size:
        low = lax.rem(tile // step, 2) == 0
        new = list(parts)
        for i in range(size):
            if i & step == 0:
                upper, lower = parts[i], parts[i | step]
                new[i] = jnp.where(low, upper, pltpu.roll(lower, step * TILE, 1))
                new[i | step] = jnp.where(low, pltpu.roll(upper, lanes - step * TILE, 1), lower)
        parts = new
        step *= 2
    return parts


def block_weights(share, member, groups):
    experts, lanes = share.shape
    rounded = share.astype(BF16).astype(F32)
    spot = (
        lax.broadcasted_iota(jnp.int32, (TILE, lanes), 0)
        == lax.rem(lax.broadcasted_iota(jnp.int32, (TILE, lanes), 1), TILE)
    ).astype(F32)
    mask = jnp.stack([spot * member[g : g + 1, :] for g in range(groups)])
    full = rounded[:, None, None, :] * mask[None]
    return full.reshape(experts * groups * TILE, lanes).astype(BF16), mask


def exchange(local, gathered, send, recv, row, place, pos):
    copies = []
    for step in range(1, pos):
        copies.append(
            remote(
                local,
                gathered.at[step - 1],
                send.at[step - 1],
                recv.at[step - 1],
                (row, lax.rem(place + step, pos)),
            )
        )
        copies[-1].start()
    for copy in copies:
        copy.wait()


def expert_kernel(dp, pos, groups, h_in, cot_in, logits, member, member_s, wout_in, *rest):
    count = bits_of(pos)
    wins, rest = rest[:3], rest[3:]
    mix, dh, dc, rest = rest[0], rest[1], rest[2], rest[3:]
    grads, rest = rest[:dp], rest[dp:]
    (share, share_s, dw, h, win, wout, stats, gathered, inner, gathered_inner), rest = (
        rest[:10],
        rest[10:],
    )
    (m_part, dy_part, m_t, z, slope, du), rest = rest[:6], rest[6:]
    ring_in, rest = rest[0], rest[1:]
    buffers, rest = rest[: 4 * count], rest[4 * count :]
    asend, arecv, bsend, brecv, csend, crecv, psend, precv, wsend, wrecv, gsend, grecv, dsend, drecv, osem, isem = (
        rest
    )
    row, place = lax.axis_index("dp"), lax.axis_index("pos")
    bits = my_bits(place, count)
    slots, length, width = h.shape
    right, left = lax.rem(row + 1, dp), lax.rem(row + dp - 1, dp)
    mates = [lax.rem(place + step, pos) for step in range(1, pos)]
    copies = pos // wout_in.shape[0]
    loads = [
        pltpu.make_async_copy(h_in, h, isem.at[0]),
        pltpu.make_async_copy(wout_in.at[place // copies], wout.at[row, place], isem.at[1]),
    ]
    middle = wout.shape[1] // 2
    halves = (slice(0, middle), slice(middle, 2 * middle))
    for step, part in enumerate(wins):
        loads.append(
            pltpu.make_async_copy(part, win.at[(row, left, right)[step]], isem.at[2 + step])
        )
    for copy in loads:
        copy.start()
    greet([(right, place), (left, place)] + [(row, mate) for mate in mates])
    pcopies = [
        remote(
            wout_in.at[mate // copies],
            wout.at[row, place],
            psend.at[step],
            precv.at[step],
            (row, mate),
        )
        for step, mate in enumerate(mates)
    ]

    for copy in pcopies:
        copy.start()

    def ring(which, distance):
        array = (win, wout)[which]
        sent = []
        for way, other in enumerate((right, left)):
            back = (distance - 1) * (1 - 2 * way)
            spot = (lax.rem(row + 2 * dp - back, dp),)
            if 2 * distance == dp:
                spot = spot + (halves[way],)
            at = (which * dp // 2 + distance - 1) * 2 + way
            sent.append(
                remote(array.at[spot], array.at[spot], wsend.at[at], wrecv.at[at], (other, place))
            )
            sent[-1].start()
        return sent

    def ring_on(which, first, passed):
        for distance in range(first, dp // 2 + 1):
            for copy in passed:
                copy.wait()
            passed = ring(which, distance)
        return passed

    win_ring = ring_on(0, 2, loads[2:])
    blocks = length // TILE
    lanes = slots * TILE
    experts = logits.shape[1]
    inside = [[member_s[g, s : s + 1, :] for s in range(slots)] for g in range(groups)]
    for g in range(groups):
        peak = jnp.full((experts, length), MASKED, F32)
        for s in range(slots):
            peak = jnp.maximum(peak, jnp.where(inside[g][s] > 0, logits[s], MASKED))
        total = jnp.zeros((experts, length), F32)
        for s in range(slots):
            total = total + jnp.where(inside[g][s] > 0, jnp.exp(logits[s] - peak), 0.0)
        stats[g] = peak
        stats[groups + g] = total
    exchange(stats, gathered, asend, arecv, row, place, pos)
    for copy in pcopies + loads[1:2]:
        copy.wait()
    wout_ring = ring(1, 1)
    for g in range(groups):
        peak = stats[g]
        for step in range(pos - 1):
            peak = jnp.maximum(peak, gathered[step, g])
        total = stats[groups + g] * jnp.exp(stats[g] - peak)
        for step in range(pos - 1):
            total = total + gathered[step, groups + g] * jnp.exp(gathered[step, g] - peak)
        stats[g] = peak
        stats[groups + g] = 1.0 / total
    parts = []
    for s in range(slots):
        peak = jnp.zeros((experts, length), F32)
        scale = jnp.zeros((experts, length), F32)
        some = jnp.zeros((1, length), F32)
        for g in range(groups):
            peak = peak + inside[g][s] * stats[g]
            scale = scale + inside[g][s] * stats[groups + g]
            some = some + inside[g][s]
        parts.append(jnp.exp(jnp.where(some > 0, logits[s] - peak, MASKED)) * scale)
        share_s[s] = parts[s]
    for block, part in enumerate(turn(parts)):
        share[block] = part

    lead = (2,) * (count + 1)
    loads[0].wait()

    def mixture(block, carry):
        where = pl.ds(pl.multiple_of(block * TILE, TILE), TILE)
        rows = h[:, where, :].reshape(lanes, width)
        weights, _ = block_weights(share[block], member, groups)
        m_part[..., where, :] = dot(weights, rows).astype(BF16).reshape(lead + (TILE, width))
        return carry

    def gradient(block, carry):
        where = pl.ds(pl.multiple_of(block * TILE, TILE), TILE)
        grads = h[:, where, :].reshape(lanes, width)
        weights, _ = block_weights(share[block], member, groups)
        dy_part[..., where, :] = (
            (32.0 * dot(weights, grads)).astype(BF16).reshape(lead + (TILE, width))
        )
        return carry

    plans = orders(count)
    every = list(range(count))[::-1]
    sources = (m_part, dy_part)
    targets = sources
    partner = lambda bit: (row, across(place, bits, bit))
    half = length // 2
    spans = (slice(0, half), slice(half, length))
    flying = {}

    def start(which, stage, sides=(0, 1)):
        for side in sides:
            lane_of = 2 * which + side
            bit = plans[side][stage]
            left = [b for b in every if b not in plans[side][:stage]]
            away = pick(left, {bit: 1 - bits[bit]})
            src = (
                sources[which].at[away + (slice(None), spans[side])]
                if stage == 0
                else buffers[lane_of * count + stage - 1].at[away]
            )
            at = lane_of * count + stage
            flying[which, side] = remote(
                src, buffers[at], bsend.at[at], brecv.at[at], partner(bit)
            )

    def launch(which, side):
        flying[which, side].start()

    def finish(which, stage, sides=(0, 1)):
        for side in sides:
            lane_of = 2 * which + side
            flying[which, side].wait()
            bit = plans[side][stage]
            left = [b for b in every if b not in plans[side][:stage]]
            near = pick(left, {bit: bits[bit]})
            target = buffers[lane_of * count + stage]
            if stage == 0:
                old = sources[which][near + (slice(None), spans[side])]
            else:
                old = buffers[lane_of * count + stage - 1][near]
            target[...] = (target[...].astype(F32) + old.astype(F32)).astype(BF16)

    def advance(which, stage, sides=(0, 1)):
        finish(which, stage, sides)
        if stage + 1 < count:
            start(which, stage + 1, sides)
            for side in sides:
                launch(which, side)

    def final(which):
        return jnp.concatenate(
            [buffers[(2 * which + side) * count + count - 1][...] for side in range(2)], axis=1
        ).reshape(2 * length, width)

    lower, upper = blocks // 2, blocks
    start(0, 0)
    refill = [
        pltpu.make_async_copy(cot_in.at[:, span], h.at[:, span], isem.at[5 + side])
        for side, span in enumerate(spans)
    ]
    lax.fori_loop(0, lower, mixture, 0)
    launch(0, 0)
    refill[0].start()
    lax.fori_loop(lower, upper, mixture, 0)
    launch(0, 1)
    refill[1].start()
    refill[0].wait()
    start(1, 0)
    advance(0, 0, (0,))
    lax.fori_loop(0, lower // 2, gradient, 0)
    advance(0, 0, (1,))
    lax.fori_loop(lower // 2, lower, gradient, 0)
    launch(1, 0)
    refill[1].wait()
    lax.fori_loop(lower, upper, gradient, 0)
    launch(1, 1)

    mine = pick(every, {b: bits[b] for b in every})

    def push(which, stage):
        for side in range(2):
            lane_of = 2 * which + side
            order = plans[side][::-1]
            bit = order[stage]
            spot = targets[which].at[
                pick(every, {b: bits[b] for b in every if b not in order[:stage]})
                + (slice(None), spans[side])
            ]
            at = lane_of * count + stage
            copy = remote(spot, spot, csend.at[at], crecv.at[at], partner(bit))
            copy.start()
            flying[which, side] = copy

    def publish(which, value):
        targets[which][mine] = value.astype(BF16).reshape(2, length, width)
        push(which, 0)

    def relay(which, stage):
        for side in range(2):
            flying[which, side].wait()
        if stage + 1 < count:
            push(which, stage + 1)

    for stage in range(1, count - 1):
        advance(0, stage)
    advance(1, 0)
    advance(0, count - 1)
    wout_ring = ring_on(1, 2, wout_ring)
    m = final(0)
    m_t[...] = jnp.transpose(m)
    for copy in (loads[2:] if dp < 4 else []) + win_ring:
        copy.wait()
    hidden = win.shape[-1]
    up = win[...].reshape(width, hidden)
    down = wout.reshape(hidden, width)
    piece = hidden // dp
    root = math.sqrt(2 / math.pi)
    for c in range(0, hidden, piece):
        u = dot(m, up[:, c : c + piece])
        square = u * u
        t = jnp.tanh(u * (root + root * 0.044715 * square))
        gate = 0.5 * (1.0 + t)
        active = (u * gate).astype(BF16)
        z[:, c : c + piece] = active
        slope[:, c : c + piece] = gate + (u * gate) * (1.0 - t) * (
            root + 3 * root * 0.044715 * square
        )
    for copy in wout_ring:
        copy.wait()
    y = dot(z[...], down[...])
    for stage in range(1, count - 1):
        advance(1, stage)
    publish(0, y)
    advance(1, count - 1)
    dy = final(1)
    share_of = width // dp

    def out_of(step):
        whose = lax.rem(row + step, dp)
        grads[step][1] = dot(
            z[:, pl.ds(pl.multiple_of(whose * piece, piece), piece)], dy, 0, 0
        ).astype(BF16)

    def in_of(step):
        whose = lax.rem(row + step, dp)
        strip = m_t[pl.ds(pl.multiple_of(whose * share_of, share_of), share_of), :]
        for c in range(0, hidden, width):
            at = c // width * share_of
            grads[step][0, at : at + share_of, :] = dot(strip, du[:, c : c + width]).astype(BF16)

    def weights_of(step):
        in_of(step)
        out_of(step)

    def pass_sums(distance, ways=(0, 1)):
        sent = []
        for way in ways:
            other = (right, left)[way]
            step = distance if way == 0 else dp - distance
            span = slice(0, 2) if 2 * distance < dp else slice(way, way + 1)
            at = 2 * (distance - 2) + way
            arrived = ring_in.at[distance - 2, way, span]
            sent.append(
                (
                    remote(
                        grads[step].at[span], arrived, gsend.at[at], grecv.at[at], (other, place)
                    ),
                    grads[step - 1 if way == 0 else step + 1],
                    arrived,
                    span,
                )
            )
            sent[-1][0].start()
        return sent

    out_of(dp // 2)
    passed = pass_sums(dp // 2, (1,))
    dm = jnp.zeros((2 * length, width), F32)
    for c in range(0, hidden, piece):
        dz = dot(dy, down[c : c + piece, :], 1, 1).astype(BF16).astype(F32)
        grad = (dz * slope[:, c : c + piece]).astype(BF16)
        du[:, c : c + piece] = grad
        dm = dm + dot(grad, up[:, c : c + piece], 1, 1)
    publish(1, dm)
    relay(0, 0)
    columns = hidden // width
    seats = [
        ((z, du)[s * 2 // slots], s % (slots // 2) // columns * length, s % columns * width)
        for s in range(slots)
    ]
    seat = lambda s: seats[s][0].at[
        seats[s][1] : seats[s][1] + length, seats[s][2] : seats[s][2] + width
    ]
    again = [
        pltpu.make_async_copy(h_in.at[s], seat(s), osem.at[1 + s]) for s in range(slots)
    ]
    mix_out = pltpu.make_async_copy(h, mix, osem.at[0])
    dh_out = [
        pltpu.make_async_copy(seat(s), dh.at[s], osem.at[1 + slots + s]) for s in range(slots)
    ]

    def chosen(block):
        return pl.ds(pl.multiple_of(block * TILE, TILE), TILE)

    def picked(whole, mask):
        products = whole.reshape(experts, groups, TILE, lanes) * mask[None]
        return jnp.sum(jnp.sum(products, axis=1), axis=1)

    def first_part(block, carry):
        where = chosen(block)
        weights, mask = block_weights(share[block], member, groups)
        rows = targets[0][..., where, :].reshape(experts * groups * TILE, width)
        grads = h[:, where, :].reshape(lanes, width)
        dw[block] = 32.0 * picked(dot(rows, grads, 1, 1), mask)
        h[:, where, :] = (
            (32.0 * dot(weights, rows, 0, 0)).astype(BF16).reshape(slots, TILE, width)
        )
        return carry

    def second_part(block, carry):
        weights, mask = block_weights(share[block], member, groups)
        rows = targets[1][..., chosen(block), :].reshape(experts * groups * TILE, width)
        places = [
            (
                ref,
                pl.ds(pl.multiple_of(top + block * TILE, TILE), TILE),
                slice(left_edge, left_edge + width),
            )
            for ref, top, left_edge in seats
        ]
        tokens = jnp.concatenate([ref[span, cols] for ref, span, cols in places], axis=0)
        dw[block] = dw[block] + picked(dot(rows, tokens, 1, 1), mask)
        back = dot(weights, rows, 0, 0).astype(BF16)
        for s, (ref, span, cols) in enumerate(places):
            ref[span, cols] = back[s * TILE : (s + 1) * TILE]
        return carry

    in_of(dp // 2)
    passed = passed + pass_sums(dp // 2, (0,))
    relay(1, 0)
    for distance in range(dp // 2 - 1, 0, -1):
        weights_of(distance)
        weights_of(dp - distance)
        if distance == 1:
            weights_of(0)
            for stage in range(1, count):
                relay(0, stage)
            for copy in again:
                copy.start()
            lax.fori_loop(0, blocks, first_part, 0)
            mix_out.start()
            for stage in range(1, count - 1):
                relay(1, stage)
        for copy, target, arrived, span in passed:
            copy.wait()
            target[span] = (target[span].astype(F32) + arrived[...].astype(F32)).astype(BF16)
        passed = pass_sums(distance) if distance > 1 else []
    for copy in again:
        copy.wait()
    flying[1, 0].wait()
    lax.fori_loop(0, lower, second_part, 0)
    flying[1, 1].wait()
    lax.fori_loop(lower, upper, second_part, 0)
    for copy in dh_out:
        copy.start()
    grads_s = turn([dw[b] for b in range(blocks)])
    for g in range(groups):
        total = jnp.zeros((experts, length), F32)
        for s in range(slots):
            total = total + inside[g][s] * share_s[s] * grads_s[s]
        inner[g] = total
    exchange(inner, gathered_inner, dsend, drecv, row, place, pos)
    sums = []
    for g in range(groups):
        total = inner[g]
        for step in range(pos - 1):
            total = total + gathered_inner[step, g]
        sums.append(total)
    for s in range(slots):
        mean = jnp.zeros((experts, length), F32)
        for g in range(groups):
            mean = mean + inside[g][s] * sums[g]
        dc[s] = (share_s[s] * (grads_s[s] - mean)).astype(BF16)
    for copy in [mix_out] + dh_out:
        copy.wait()


def mix_experts(dp, pos, groups, h, cot, logits, member, member_s, expert_out, win_parts):
    slots, length, width = h.shape
    experts = logits.shape[1]
    part = expert_out.shape[1:]
    lead = (2,) * (bits_of(pos) + 1)
    hidden = win_parts[0].shape[-1]
    blocks = length // TILE
    count = bits_of(pos)
    vmem = pl.BlockSpec(memory_space=pltpu.VMEM)
    hbm = pl.BlockSpec(memory_space=pl.ANY)
    rows = 2 * length
    dma = pltpu.SemaphoreType.DMA
    return pl.pallas_call(
        lambda *refs: expert_kernel(dp, pos, groups, *refs),
        out_shape=[
            jax.ShapeDtypeStruct(h.shape, BF16),
            jax.ShapeDtypeStruct(h.shape, BF16),
            jax.ShapeDtypeStruct(logits.shape, BF16),
        ]
        + [jax.ShapeDtypeStruct((2, hidden // dp, width), BF16)] * dp,
        in_specs=[hbm, hbm, vmem, vmem, vmem, hbm] + [hbm] * 3,
        out_specs=[hbm, hbm, vmem] + [vmem] * dp,
        scratch_shapes=[
            pltpu.VMEM((blocks, experts, slots * TILE), F32),
            pltpu.VMEM(logits.shape, F32),
            pltpu.VMEM((blocks, experts, slots * TILE), F32),
            pltpu.VMEM(h.shape, BF16),
            pltpu.VMEM((dp,) + win_parts[0].shape, BF16),
            pltpu.VMEM((dp, pos) + part, BF16),
            pltpu.VMEM((2 * groups, experts, slots * TILE), F32),
            pltpu.VMEM((pos - 1, 2 * groups, experts, slots * TILE), F32),
            pltpu.VMEM((groups, experts, length), F32),
            pltpu.VMEM((pos - 1, groups, experts, length), F32),
            pltpu.VMEM(lead + (length, width), BF16),
            pltpu.VMEM(lead + (length, width), BF16),
            pltpu.VMEM((width, rows), BF16),
            pltpu.VMEM((rows, hidden), BF16),
            pltpu.VMEM((rows, hidden), F32),
            pltpu.VMEM((rows, hidden), BF16),
            pltpu.VMEM((dp // 2 - 1, 2, 2, hidden // dp, width), BF16),
        ]
        + [
            pltpu.VMEM((2,) * (count - stage) + (length // 2, width), BF16)
            for _ in range(4)
            for stage in range(count)
        ]
        + [
            dma((pos - 1,)),
            dma((pos - 1,)),
            dma((4 * count,)),
            dma((4 * count,)),
            dma((4 * count,)),
            dma((4 * count,)),
            dma((pos - 1,)),
            dma((pos - 1,)),
            dma((2 * dp,)),
            dma((2 * dp,)),
            dma((2 * (dp // 2 - 1),)),
            dma((2 * (dp // 2 - 1),)),
            dma((pos - 1,)),
            dma((pos - 1,)),
            dma((1 + 2 * slots,)),
            dma((7,)),
        ],
        compiler_params=pltpu.CompilerParams(
            collective_id=2, has_side_effects=True, vmem_limit_bytes=VMEM_LIMIT
        ),
        name="mix_experts",
    )(h, cot, logits, member, member_s, expert_out, *win_parts)


from jax.sharding import PartitionSpec as P

MIXED_SEQUENCES = 32


def body(
    inputs,
    cotangent,
    counts,
    seq_rank,
    first_gain,
    first_bias,
    query_weight,
    key_weight,
    value_weight,
    output_weight,
    second_gain,
    second_bias,
    control_weight,
    expert_in,
    expert_out,
):
    capacity, length, features = inputs.shape
    dp, pos = lax.axis_size("dp"), lax.axis_size("pos")
    experts = control_weight.shape[1]
    groups = seq_rank.shape[1] // MIXED_SEQUENCES

    w_t, wk, wo, small, member, member_s, live, win = gather_weights(
        dp,
        pos,
        groups,
        capacity,
        query_weight,
        key_weight,
        value_weight,
        output_weight,
        jnp.stack([first_gain, first_bias, second_gain, second_bias]),
        control_weight.T,
        counts,
        seq_rank,
        expert_in,
    )
    count = live[0, :1]

    def send_rows(array, step):
        return lax.ppermute(array, "dp", [(i, (i + step) % dp) for i in range(dp)])

    wins = (win, send_rows(win, 1), send_rows(win, -1))

    q_t, k, v_t, ctx_t, x1, h, inverse, e_t, logits = forward(count, inputs, w_t, wk, wo, small)
    mix, dh, dc, *grads = mix_experts(
        dp, pos, groups, h, cotangent, logits, member, member_s, expert_out, wins
    )
    grads = (grads[0], send_rows(grads[1], 1), send_rows(grads[dp - 1], -1))
    layer_output, input_grad, grad_t, out_grad, vecs = backward(
        count, inputs, cotangent, x1, mix, dh, dc, q_t, k, v_t, ctx_t, inverse, e_t, w_t, wo, small
    )
    shard, *grads = scatter_weights(
        dp, pos, grad_t, out_grad, vecs, *grads
    )
    query_grad, key_grad, value_grad, output_grad, vectors, control, ein_grad, eout_grad = finish(
        experts, shard, *grads
    )
    return (
        layer_output,
        input_grad,
        vectors[2],
        vectors[3],
        query_grad,
        key_grad,
        value_grad,
        output_grad,
        vectors[0],
        vectors[1],
        control.T,
        ein_grad,
        eout_grad,
    )


def solution(mesh):
    both = ("dp", "pos")
    vector, matrix, cube = P(both), P(both, None), P(both, None, None)
    middle = P(None, both, None)
    return jax.shard_map(
        body,
        mesh=mesh,
        in_specs=(
            cube,
            cube,
            P("dp", None),
            P("dp", None),
            vector,
            vector,
            matrix,
            matrix,
            matrix,
            matrix,
            vector,
            vector,
            matrix,
            middle,
            middle,
        ),
        out_specs=(
            cube,
            cube,
            vector,
            vector,
            matrix,
            matrix,
            matrix,
            matrix,
            vector,
            vector,
            matrix,
            middle,
            middle,
        ),
        check_vma=False,
    )
```

```python
import math
import jax
import jax.numpy as jnp
from jax import lax
from jax.experimental import pallas as pl
from jax.experimental.pallas import tpu as pltpu

HEADS = 8
HEAD = 64
NORM_EPS = 1e-05
MASKED = -1e30
F32 = jnp.float32
BF16 = jnp.bfloat16
MIB = 1 << 20
VMEM_LIMIT = 62 * MIB


def dot(a, b, ca=1, cb=0):
    return lax.dot_general(a, b, (((ca,), (cb,)), ((), ())), preferred_element_type=F32)


def normalize(v):
    center = v - jnp.mean(v, axis=-1, keepdims=True)
    spread = jnp.mean(center * center, axis=-1, keepdims=True)
    scale = lax.rsqrt(spread + NORM_EPS)
    return center * scale, scale


def spread_heads(parts):
    return jnp.concatenate(
        [
            jnp.concatenate(
                [part if i == j else jnp.zeros_like(part) for i in range(len(parts))], axis=0
            )
            for j, part in enumerate(parts)
        ],
        axis=1,
    )


def forward_kernel(count, x, w_t, wk, wo, small, q_t, k, v_t, ctx_t, x1, h, inverse, e_t, logits):
    g1, b1, g2, b2 = (small[i : i + 1] for i in range(4))
    slots, length, width = x.shape
    router = small[8:16].astype(BF16)
    wq_t, wv_t = w_t.at[:width], w_t.at[2 * width :]
    half = length // 2
    causal = lax.broadcasted_iota(jnp.int32, (half, half), 0) <= lax.broadcasted_iota(
        jnp.int32, (half, half), 1
    )

    def one():
        source = x[...].reshape(slots * length, width).astype(F32)
        xhat, _ = normalize(source)
        a = (xhat * g1 + b1).astype(BF16)
        qs = (dot(wq_t[...], a, 1, 1).astype(BF16) * 0.125).astype(BF16)
        ks = dot(a, wk[...]).astype(BF16)
        vs = dot(wv_t[...], a, 1, 1).astype(BF16)
        k[...] = ks.reshape(slots, length, width)
        ones = jnp.ones((16, length), BF16)
        parts = [[] for _ in range(slots)]
        sums = [[] for _ in range(slots)]
        cols = [slice(s * length, (s + 1) * length) for s in range(slots)]
        for s in range(slots):
            q_t[s] = qs[:, cols[s]]
            v_t[s] = vs[:, cols[s]]
        for base in range(0, HEADS, 4):
            for s in range(slots):
                four = slice(base * HEAD, (base + 4) * HEAD)
                spread_q = spread_heads(
                    [
                        qs[(base + i) * HEAD : (base + i + 1) * HEAD, cols[s]] for i in range(4)
                    ]
                )
                scores = dot(ks[cols[s], four], spread_q)
                exps = []
                for j in range(4):
                    st = scores[:, j * length : (j + 1) * length]
                    s00 = jnp.where(causal, st[:half, :half], MASKED)
                    s01 = st[:half, half:]
                    s11 = jnp.where(causal, st[half:, half:], MASKED)
                    m0 = jnp.max(s00, axis=0, keepdims=True)
                    m1 = jnp.maximum(
                        jnp.max(s01, axis=0, keepdims=True), jnp.max(s11, axis=0, keepdims=True)
                    )
                    e00 = jnp.exp(s00 - m0).astype(BF16)
                    e01 = jnp.exp(s01 - m1).astype(BF16)
                    e11 = jnp.exp(s11 - m1).astype(BF16)
                    et = jnp.concatenate(
                        [
                            jnp.concatenate([e00, e01], axis=1),
                            jnp.concatenate([jnp.zeros_like(e00), e11], axis=1),
                        ],
                        axis=0,
                    )
                    e_t[s, base + j] = et
                    exps.append(et)
                for j in range(0, 4, 2):
                    head = base + j
                    va = jnp.concatenate(
                        [
                            vs[head * HEAD : (head + 1) * HEAD, cols[s]],
                            ones,
                            vs[(head + 1) * HEAD : (head + 2) * HEAD, cols[s]],
                            ones,
                        ],
                        axis=0,
                    )
                    both = dot(va, jnp.concatenate(exps[j : j + 2], axis=1))
                    for i in range(2):
                        full = both[i * 80 : i * 80 + 80, i * length : (i + 1) * length]
                        total = full[HEAD : HEAD + 1]
                        scale = 1.0 / total
                        parts[s].append((full[:HEAD] * scale).astype(BF16))
                        sums[s].append(scale)
        outs = []
        for s in range(slots):
            ctx = jnp.concatenate(parts[s], axis=0)
            ctx_t[s] = ctx
            inverse[s] = jnp.concatenate(sums[s], axis=0)
            outs.append(ctx)
        residual = source + dot(jnp.concatenate(outs, axis=1), wo[...], 0, 0)
        x1[...] = residual.reshape(slots, length, width)
        xhat2, _ = normalize(residual)
        hidden = (xhat2 * g2 + b2).astype(BF16)
        h[...] = hidden.reshape(slots, length, width)
        for s in range(slots):
            logits[s] = dot(router, hidden[cols[s], :], 1, 1)

    live = pl.program_id(0) * slots < count[0]
    pl.when(live)(one)

    @pl.when(jnp.logical_not(live))
    def _():
        h[...] = jnp.zeros((slots, length, width), BF16)
        logits[...] = jnp.zeros_like(logits)


def forward(count, x, w_t, wk, wo, small, block=2):
    slots, length, width = x.shape
    per = lambda rows, cols: pl.BlockSpec((block, rows, cols), lambda i, c: (i, 0, 0))
    whole = lambda a: pl.BlockSpec(a.shape, lambda i, c: (0,) * a.ndim)
    shape = lambda rows, cols, kind: jax.ShapeDtypeStruct((slots, rows, cols), kind)
    return pl.pallas_call(
        forward_kernel,
        grid_spec=pltpu.PrefetchScalarGridSpec(
            num_scalar_prefetch=1,
            grid=(slots // block,),
            in_specs=[per(length, width)]
            + [whole(a) for a in (w_t, wk, wo, small)],
            out_specs=[
                per(width, length),
                per(length, width),
                per(width, length),
                per(width, length),
                per(length, width),
                per(length, width),
                per(HEADS, length),
            ]
            + [pl.BlockSpec((block, HEADS, length, length), lambda i, c: (i, 0, 0, 0)), per(HEADS, length)],
        ),
        out_shape=[
            shape(width, length, BF16),
            shape(length, width, BF16),
            shape(width, length, BF16),
            shape(width, length, BF16),
            shape(length, width, F32),
            shape(length, width, BF16),
            shape(HEADS, length, F32),
        ]
        + [jax.ShapeDtypeStruct((slots, HEADS, length, length), BF16), shape(8, length, F32)] ,
        compiler_params=pltpu.CompilerParams(vmem_limit_bytes=VMEM_LIMIT),
        cost_estimate=pl.CostEstimate(
            flops=40_000_000_000, bytes_accessed=40 * MIB, transcendentals=8_000_000
        ),
        name="attention_forward",
    )(count, x, w_t, wk, wo, small)


def norm_back(grad, xhat, scale):
    return scale * (
        grad
        - jnp.mean(grad, axis=-1, keepdims=True)
        - xhat * jnp.mean(grad * xhat, axis=-1, keepdims=True)
    )


def backward_kernel(
    count, x, cot, x1, mix, dh, dc, q_t, k, v_t, ctx_t, inverse, e_t, w_t, wo, small,
    lo, dx, grad_t, out_grad, vecs, back_t,
):
    slots, length, width = x.shape
    half = length // 2
    step = pl.program_id(0)

    @pl.when(step == 0)
    def _():
        grad_t[...] = jnp.zeros_like(grad_t)
        out_grad[...] = jnp.zeros_like(out_grad)
        vecs[...] = jnp.zeros_like(vecs)

    g1, b1, g2, b2 = (small[i : i + 1] for i in range(4))
    router = small[8:16].astype(BF16)

    def one():
        tokens = slots * length
        cols = [slice(s * length, (s + 1) * length) for s in range(slots)]
        row = lax.broadcasted_iota(jnp.int32, (tokens, 1), 0) // length + step * slots
        live = row < count[0]
        keep = lambda v: v if slots == 1 else jnp.where(live, v, 0.0)
        residual = x1[...].reshape(tokens, width)
        xhat2, scale2 = normalize(residual)
        lo[...] = (
            keep(residual + mix[...].reshape(tokens, width).astype(F32))
            .astype(BF16)
            .reshape(slots, length, width)
        )
        hidden = (xhat2 * g2 + b2).astype(BF16)
        routed = []
        for s in range(slots):
            routed.append(dot(dc[s], router, 0, 0))
            vecs[8:16] += dot(dc[s], hidden[cols[s], :])
        grad_h = (
            (dh[...].reshape(tokens, width).astype(F32) + jnp.concatenate(routed, axis=0))
            .astype(BF16)
            .astype(F32)
        )
        vecs[0:1] += jnp.sum(grad_h * xhat2, axis=0, keepdims=True)
        vecs[1:2] += jnp.sum(grad_h, axis=0, keepdims=True)
        dx1 = keep(
            cot[...].reshape(tokens, width).astype(F32) + norm_back(grad_h * g2, xhat2, scale2)
        )
        datt = dx1.astype(BF16)
        dctx = dot(wo[...], datt, 1, 1).astype(BF16)
        out_grad[...] += dot(jnp.concatenate([ctx_t[s] for s in range(slots)], axis=1), datt)
        zero = jnp.zeros((half, half), BF16)
        for s in range(slots):
            kt = jnp.transpose(k[s])
            vn = jnp.transpose(v_t[s])
            scaled = []
            inners = []
            for head in range(HEADS):
                rows = slice(head * HEAD, (head + 1) * HEAD)
                part = dctx[rows, cols[s]].astype(F32) * inverse[s, head : head + 1, :]
                scaled.append(part.astype(BF16))
                inners.append(jnp.sum(ctx_t[s, rows, :].astype(F32) * part, axis=0, keepdims=True))
            for base in range(0, HEADS, 4):
                four = slice(base * HEAD, (base + 4) * HEAD)
                dprobs = dot(vn[:, four], spread_heads(scaled[base : base + 4]))
                grads = []
                exps = []
                for j in range(4):
                    head = base + j
                    et = e_t[s, head]
                    dp = dprobs[:, j * length : (j + 1) * length]
                    inner = inners[head]
                    d00 = et[:half, :half].astype(F32) * (dp[:half, :half] - inner[:, :half])
                    d01 = et[:half, half:].astype(F32) * (dp[:half, half:] - inner[:, half:])
                    d11 = et[half:, half:].astype(F32) * (dp[half:, half:] - inner[:, half:])
                    grads.append(
                        jnp.concatenate(
                            [
                                jnp.concatenate([d00.astype(BF16), d01.astype(BF16)], axis=1),
                                jnp.concatenate([zero, d11.astype(BF16)], axis=1),
                            ],
                            axis=0,
                        )
                    )
                    exps.append(et)
                tall = jnp.concatenate(grads, axis=0)
                dk = dot(q_t[s, four, :], tall, 1, 1)
                dv = dot(
                    jnp.concatenate(scaled[base : base + 4], axis=0),
                    jnp.concatenate(exps, axis=0),
                    1,
                    1,
                )
                dq = [
                    dot(
                        kt[(base + j) * HEAD : (base + j + 2) * HEAD, :],
                        jnp.concatenate(grads[j : j + 2], axis=1),
                    )
                    * 0.125
                    for j in range(0, 4, 2)
                ]
                for j in range(4):
                    begin = (base + j) * HEAD
                    spot = slice(j * length, (j + 1) * length)
                    inside = slice(j * HEAD, (j + 1) * HEAD)
                    i = j % 2
                    back_t[begin : begin + HEAD, cols[s]] = dq[j // 2][
                        i * HEAD : (i + 1) * HEAD, i * length : (i + 1) * length
                    ].astype(BF16)
                    back_t[width + begin : width + begin + HEAD, cols[s]] = dk[inside, spot].astype(
                        BF16
                    )
                    back_t[2 * width + begin : 2 * width + begin + HEAD, cols[s]] = dv[
                        inside, spot
                    ].astype(BF16)
        source = x[...].reshape(tokens, width).astype(F32)
        xhat1, scale1 = normalize(source)
        a = (xhat1 * g1 + b1).astype(BF16)
        back = back_t[...]
        grad_t[...] += dot(back, a)
        da = dot(back, w_t[...], 0, 0)
        vecs[2:3] += jnp.sum(da * xhat1, axis=0, keepdims=True)
        vecs[3:4] += jnp.sum(da, axis=0, keepdims=True)
        dx[...] = (
            keep(dx1 + norm_back(da * g1, xhat1, scale1))
            .astype(BF16)
            .reshape(slots, length, width)
        )

    some = step * slots < count[0]
    pl.when(some)(one)

    @pl.when(jnp.logical_not(some))
    def _():
        dx[...] = jnp.zeros((slots, length, width), BF16)
        lo[...] = jnp.zeros((slots, length, width), BF16)


def backward(count, x, cot, x1, mix, dh, dc, q_t, k, v_t, ctx_t, inverse, e_t, w_t, wo, small, block=2):
    slots, length, width = x.shape
    per = lambda a: pl.BlockSpec(
        (block,) + a.shape[1:], lambda i, c: (i,) + (0,) * (len(a.shape) - 1)
    )
    whole = lambda a: pl.BlockSpec(a.shape, lambda i, c: (0,) * len(a.shape))
    outs = [
        jax.ShapeDtypeStruct((3 * width, width), F32),
        jax.ShapeDtypeStruct((width, width), F32),
        jax.ShapeDtypeStruct((16, width), F32),
    ]
    batched = (x, cot, x1, mix, dh, dc, q_t, k, v_t, ctx_t, inverse, e_t)
    shared = (w_t, wo, small)
    return pl.pallas_call(
        backward_kernel,
        grid_spec=pltpu.PrefetchScalarGridSpec(
            num_scalar_prefetch=1,
            grid=(slots // block,),
            in_specs=[per(a) for a in batched] + [whole(a) for a in shared],
            out_specs=[per(x), per(x)] + [whole(a) for a in outs],
            scratch_shapes=[pltpu.VMEM((3 * width, block * length), BF16)],
        ),
        out_shape=[jax.ShapeDtypeStruct(x.shape, BF16)] * 2 + outs,
        compiler_params=pltpu.CompilerParams(vmem_limit_bytes=VMEM_LIMIT),
        cost_estimate=pl.CostEstimate(
            flops=100_000_000_000, bytes_accessed=60 * MIB, transcendentals=8_000_000
        ),
        name="attention_backward",
    )(count, *batched, *shared)


MESH = pl.DeviceIdType.MESH
TILE = 16


def bits_of(size):
    return size.bit_length() - 1


def orders(count):
    first = list(range(count))
    second = list(first)
    if count > 2:
        second[1], second[2] = second[2], second[1]
    return first, second


def greet(peers):
    barrier = pltpu.get_barrier_semaphore()
    for peer in peers:
        pl.semaphore_signal(barrier, inc=1, device_id=peer, device_id_type=MESH)
    pl.semaphore_wait(barrier, len(peers))


def my_bits(place, count):
    return [lax.rem(place // (1 << bit), 2) for bit in range(count)]


def across(place, bits, bit):
    return place + (1 - 2 * bits[bit]) * (1 << bit)


def pick(remaining, chosen):
    return tuple(chosen[bit] if bit in chosen else slice(None) for bit in remaining)


def remote(src, dst, send, recv, device):
    return pltpu.make_async_remote_copy(
        src_ref=src,
        dst_ref=dst,
        send_sem=send,
        recv_sem=recv,
        device_id=device,
        device_id_type=MESH,
    )


def gather_kernel(
    dp, pos, groups, slots,
    wq, wk, wv, wo, vectors, router, counts, ranks, ein,
    w_t, wk_out, wo_out, vt, member, member_s, live, win,
    held, zsend, zrecv, send, recv, esend, erecv, lsem,
):
    count = bits_of(pos)
    row, place = lax.axis_index("dp"), lax.axis_index("pos")
    bits = my_bits(place, count)
    others = [lax.rem(row + step, dp) for step in range(1, dp)]
    mates = [lax.rem(place + step, pos) for step in range(1, pos)]
    greet([(other, place) for other in others] + [(row, mate) for mate in mates])
    rows, width = wq.shape
    every = list(range(count))[::-1]
    here = pick(every, {bit: bits[bit] for bit in every})
    for index, weight in enumerate((wq, wk, wv, wo)):
        held[(row,) + here + (slice(None), slice(index * width, (index + 1) * width))] = weight[...]
    tall = jnp.concatenate(
        [
            vectors[...].astype(F32),
            jnp.zeros((8 - vectors.shape[0], rows), F32),
            router[...].astype(F32),
            jnp.zeros((120 - router.shape[0], rows), F32),
        ],
        axis=0,
    )
    square = jnp.concatenate([tall, jnp.zeros((128, 128 - rows), F32)], axis=1)
    held[(row,) + here + (slice(None), slice(4 * width, 4 * width + 128))] = jnp.transpose(square)[
        :rows
    ].astype(BF16)

    copies = pos // ein.shape[0]
    local = pltpu.make_async_copy(ein.at[place // copies], win.at[place], lsem.at[0])
    local.start()
    zcopies = []
    for step, other in enumerate(others):
        spot = held.at[(row,) + here]
        zcopies.append(remote(spot, spot, zsend.at[step], zrecv.at[step], (other, place)))
        zcopies[-1].start()

    ecopies = []
    for step, mate in enumerate(mates):
        ecopies.append(
            remote(
                ein.at[mate // copies], win.at[place], esend.at[step], erecv.at[step], (row, mate)
            )
        )
        ecopies[-1].start()

    first, second = orders(count)
    plans = (first[::-1], second[::-1])

    def push(block, stage):
        order = plans[block % 2]
        bit = order[stage]
        whose = lax.rem(row + dp - block, dp)
        spot = held.at[
            (whose,) + pick(every, {b: bits[b] for b in every if b not in order[:stage]})
        ]
        at = block * count + stage
        copy = remote(spot, spot, send.at[at], recv.at[at], (row, across(place, bits, bit)))
        copy.start()
        return copy

    flying = {0: push(0, 0)}
    lanes = slots * TILE
    which = lax.broadcasted_iota(jnp.int32, (1, pos), 1)
    begin = jnp.sum(jnp.where(which < place, counts[...], 0), axis=1, keepdims=True)
    mine = jnp.sum(jnp.where(which == place, counts[...], 0), axis=1, keepdims=True)
    live[...] = jnp.broadcast_to(mine, live.shape)
    slot = lax.broadcasted_iota(jnp.int32, (1, lanes), 1) // TILE
    wanted = jnp.where(slot < mine, begin + slot, -1)
    table = (ranks[...] // 32).astype(F32) + 1.0
    size = table.shape[1]
    if size < 128:
        table = jnp.concatenate([table, jnp.zeros((1, 128 - size), F32)], axis=1)
    column = jnp.transpose(jnp.broadcast_to(table, (128, 128)))[:, :1]
    match = lax.broadcasted_iota(jnp.int32, (128, lanes), 0) == wanted
    ids = jnp.sum(jnp.where(match, column, 0.0), axis=0, keepdims=True)
    for g in range(groups):
        member[g : g + 1, :] = (ids == float(g + 1)).astype(F32)
    slot = lax.broadcasted_iota(jnp.int32, (slots, 1), 0)
    wanted = jnp.where(slot < mine, begin + slot, -1)
    match = lax.broadcasted_iota(jnp.int32, (slots, 128), 1) == wanted
    ids = jnp.sum(jnp.where(match, table, 0.0), axis=1, keepdims=True)
    for g in range(groups):
        member_s[g] = jnp.broadcast_to((ids == float(g + 1)).astype(F32), member_s.shape[1:])

    for block in range(1, dp):
        zcopies[block - 1].wait()
        flying[block] = push(block, 0)
    for stage in range(1, count):
        for block in range(dp):
            flying[block].wait()
            flying[block] = push(block, stage)
    for block in range(dp):
        flying[block].wait()
    full = held[...].reshape(dp * pos * rows, 4 * width + 128)
    for index in range(3):
        w_t[index * width : (index + 1) * width, :] = jnp.transpose(
            full[:, index * width : (index + 1) * width]
        )
    wk_out[...] = full[:, width : 2 * width]
    wo_out[...] = full[:, 3 * width : 4 * width]
    vt[...] = jnp.transpose(full[:, 4 * width :])[:16, :].astype(F32)
    for copy in [local] + ecopies:
        copy.wait()


def gather_weights(dp, pos, groups, slots, wq, wk, wv, wo, vectors, router, counts, ranks, ein):
    rows, width = wq.shape
    whole = rows * dp * pos
    vmem = pl.BlockSpec(memory_space=pltpu.VMEM)
    hbm = pl.BlockSpec(memory_space=pl.ANY)
    count = bits_of(pos)
    dma = pltpu.SemaphoreType.DMA
    return pl.pallas_call(
        lambda *refs: gather_kernel(dp, pos, groups, slots, *refs),
        out_shape=[
            jax.ShapeDtypeStruct((3 * width, whole), BF16),
            jax.ShapeDtypeStruct((whole, width), BF16),
            jax.ShapeDtypeStruct((whole, width), BF16),
            jax.ShapeDtypeStruct((16, whole), F32),
            jax.ShapeDtypeStruct((groups, slots * TILE), F32),
            jax.ShapeDtypeStruct((groups, slots, slots * TILE), F32),
            jax.ShapeDtypeStruct((1, 128), jnp.int32),
            jax.ShapeDtypeStruct((pos,) + ein.shape[1:], BF16),
        ],
        in_specs=[vmem] * 8 + [hbm],
        out_specs=[vmem] * 7 + [hbm],
        scratch_shapes=[
            pltpu.VMEM((dp,) + (2,) * count + (rows, 4 * width + 128), BF16),
            dma((dp - 1,)),
            dma((dp - 1,)),
            dma((dp * count,)),
            dma((dp * count,)),
            dma((pos - 1,)),
            dma((pos - 1,)),
            dma((1,)),
        ],
        compiler_params=pltpu.CompilerParams(
            collective_id=0, has_side_effects=True, vmem_limit_bytes=VMEM_LIMIT
        ),
        name="gather_weights",
    )(wq, wk, wv, wo, vectors, router, counts, ranks, ein)


def scatter_kernel(dp, pos, grad_in, out_in, vecs, *rest):
    count = bits_of(pos)
    parts, rest = rest[:3], rest[3:]
    out, ein_got, eout_got, held, grad_t, out_grad, grads, isem, *rest = rest
    loads = [pltpu.make_async_copy(part, grads.at[i], isem.at[i]) for i, part in enumerate(parts)]
    loads.append(pltpu.make_async_copy(grad_in, grad_t, isem.at[3]))
    loads.append(pltpu.make_async_copy(out_in, out_grad, isem.at[4]))
    for copy in loads:
        copy.start()
    buffers, slots, rest = rest[: 2 * count], rest[2 * count], rest[2 * count + 1 :]
    send, recv, esend, erecv, ein_mine, eout_mine = rest
    row, place = lax.axis_index("dp"), lax.axis_index("pos")
    bits = my_bits(place, count)
    others = [lax.rem(row + step, dp) for step in range(1, dp)]
    mates = [lax.rem(place + step, pos) for step in range(1, pos)]
    greet([(other, place) for other in others] + [(row, mate) for mate in mates])
    width = out_grad.shape[1]
    ecopies = []
    for copy in loads[:3]:
        copy.wait()
    for index, (mine, got) in enumerate(((ein_mine, ein_got), (eout_mine, eout_got))):
        total = grads[0, index].astype(F32)
        for i in range(1, 3):
            total = total + grads[i, index].astype(F32)
        total = total.astype(BF16)
        if index == 0:
            strip = width // dp
            for c in range(0, mine.shape[2], width):
                at = c // width * strip
                mine[:, :, c : c + width] = total[at : at + strip].reshape(
                    mine.shape[:2] + (width,)
                )
        else:
            mine[...] = total.reshape(mine.shape)
        for step, mate in enumerate(mates):
            at = index * (pos - 1) + step
            ecopies.append(
                remote(mine.at[mate], got.at[place], esend.at[at], erecv.at[at], (row, mate))
            )
            if index == 0:
                ecopies[-1].start()
        got[place] = mine[place]
    for copy in loads[3:]:
        copy.wait()
    lead = held.shape[:-1]
    for index in range(3):
        held[..., index * width : (index + 1) * width] = (
            jnp.transpose(grad_t[index * width : (index + 1) * width, :].astype(BF16)).reshape(
                lead + (width,)
            )
        )
    held[..., 3 * width : 4 * width] = out_grad[...].astype(BF16).reshape(lead + (width,))
    tail = jnp.concatenate([vecs[...], jnp.zeros((112, vecs.shape[1]), F32)], axis=0)
    held[..., 4 * width :] = jnp.transpose(tail).astype(BF16).reshape(lead + (128,))
    used = 0
    halves = (slice(0, dp // 2), slice(dp // 2, dp))
    plans = orders(count)
    current = [held.at[half] for half in halves]
    remaining = [list(range(count))[::-1] for _ in halves]
    for stage in range(count):
        copies = []
        for side in range(2):
            bit = plans[side][stage]
            away = (slice(None),) + pick(remaining[side], {bit: 1 - bits[bit]})
            copies.append(
                remote(
                    current[side].at[away],
                    buffers[side * count + stage],
                    send.at[used],
                    recv.at[used],
                    (row, across(place, bits, bit)),
                )
            )
            used += 1
        for copy in copies:
            copy.start()
        if stage == count - 1:
            for copy in ecopies[len(mates) :]:
                copy.start()
        for side in range(2):
            copies[side].wait()
            bit = plans[side][stage]
            near = (slice(None),) + pick(remaining[side], {bit: bits[bit]})
            target = buffers[side * count + stage]
            target[...] = (
                target[...].astype(F32) + current[side][near].astype(F32)
            ).astype(BF16)
            current[side] = target
            remaining[side] = [b for b in remaining[side] if b != bit]
    joined = jnp.concatenate([current[0][...], current[1][...]], axis=0)
    slots[1] = joined
    copies = []
    for step, other in enumerate(others):
        copies.append(
            remote(
                slots.at[1, other],
                slots.at[0, row],
                send.at[used],
                recv.at[used],
                (other, place),
            )
        )
        used += 1
        copies[-1].start()
    for copy in copies:
        copy.wait()
    total = slots[1, row].astype(F32)
    for other in others:
        total = total + slots[0, other].astype(F32)
    out[...] = total
    for copy in ecopies:
        copy.wait()


def scatter_weights(dp, pos, grad_t, out_grad, vecs, *grads):
    width = out_grad.shape[1]
    rows = out_grad.shape[0] // (dp * pos)
    wide = 4 * width + 128
    hidden = grads[0].shape[1] * dp
    hbm = pl.BlockSpec(memory_space=pl.ANY)
    ein_shape = (width // (dp * pos), hidden)
    eout_shape = (hidden // (dp * pos), width)
    vmem = pl.BlockSpec(memory_space=pltpu.VMEM)
    count = bits_of(pos)
    total = dp - 1 + 2 * count
    return pl.pallas_call(
        lambda *refs: scatter_kernel(dp, pos, *refs),
        out_shape=[
            jax.ShapeDtypeStruct((rows, wide), F32),
            jax.ShapeDtypeStruct((pos,) + ein_shape, BF16),
            jax.ShapeDtypeStruct((pos,) + eout_shape, BF16),
        ],
        in_specs=[hbm, hbm, vmem] + [hbm] * 3,
        out_specs=[vmem] * 3,
        scratch_shapes=[
            pltpu.VMEM((dp,) + (2,) * count + (rows, wide), BF16),
            pltpu.VMEM(grad_t.shape, F32),
            pltpu.VMEM(out_grad.shape, F32),
            pltpu.VMEM((3,) + grads[0].shape, BF16),
            pltpu.SemaphoreType.DMA((5,)),
        ]
        + [
            pltpu.VMEM((dp // 2,) + (2,) * (count - 1 - stage) + (rows, wide), BF16)
            for _ in range(2)
            for stage in range(count)
        ]
        + [
            pltpu.VMEM((2, dp, rows, wide), BF16),
            pltpu.SemaphoreType.DMA((total,)),
            pltpu.SemaphoreType.DMA((total,)),
            pltpu.SemaphoreType.DMA((2 * (pos - 1),)),
            pltpu.SemaphoreType.DMA((2 * (pos - 1),)),
            pltpu.VMEM((pos,) + ein_shape, BF16),
            pltpu.VMEM((pos,) + eout_shape, BF16),
        ],
        compiler_params=pltpu.CompilerParams(
            collective_id=1, has_side_effects=True, vmem_limit_bytes=VMEM_LIMIT
        ),
        name="scatter_weights",
    )(grad_t, out_grad, vecs, *grads)


def finish_kernel(shard, ein_got, eout_got, *outs):
    width = outs[0].shape[1]
    rows = shard.shape[0]
    for index in range(4):
        outs[index][...] = shard[:, index * width : (index + 1) * width]
    tail = jnp.transpose(
        jnp.concatenate([shard[:, 4 * width :], jnp.zeros((128 - rows, 128), F32)], axis=0)
    )
    outs[4][...] = tail[8:16, :rows]
    for index in range(4):
        outs[7 + index][...] = tail[index, :rows]
    for got, target in ((ein_got, outs[5]), (eout_got, outs[6])):
        experts = target.shape[0]
        copies = got.shape[0] // experts
        for expert in range(experts):
            total = got[expert * copies].astype(F32)
            for copy in range(1, copies):
                total = total + got[expert * copies + copy].astype(F32)
            target[expert] = total


def finish(experts, shard, ein_got, eout_got):
    rows = shard.shape[0]
    width = (shard.shape[1] - 128) // 4
    vmem = pl.BlockSpec(memory_space=pltpu.VMEM)
    return pl.pallas_call(
        finish_kernel,
        out_shape=[jax.ShapeDtypeStruct((rows, width), F32)] * 4
        + [jax.ShapeDtypeStruct((8, rows), F32)]
        + [
            jax.ShapeDtypeStruct((experts,) + ein_got.shape[1:], F32),
            jax.ShapeDtypeStruct((experts,) + eout_got.shape[1:], F32),
        ]
        + [jax.ShapeDtypeStruct((rows,), F32)] * 4,
        in_specs=[vmem] * 3,
        out_specs=[vmem] * 11,
        compiler_params=pltpu.CompilerParams(vmem_limit_bytes=VMEM_LIMIT),
        name="finish",
    )(shard, ein_got, eout_got)


def turn(parts):
    size = len(parts)
    lanes = parts[0].shape[1]
    tile = lax.broadcasted_iota(jnp.int32, parts[0].shape, 1) // TILE
    step = 1
    while step < size:
        low = lax.rem(tile // step, 2) == 0
        new = list(parts)
        for i in range(size):
            if i & step == 0:
                upper, lower = parts[i], parts[i | step]
                new[i] = jnp.where(low, upper, pltpu.roll(lower, step * TILE, 1))
                new[i | step] = jnp.where(low, pltpu.roll(upper, lanes - step * TILE, 1), lower)
        parts = new
        step *= 2
    return parts


def block_weights(share, member, groups):
    experts, lanes = share.shape
    rounded = share.astype(BF16).astype(F32)
    spot = (
        lax.broadcasted_iota(jnp.int32, (TILE, lanes), 0)
        == lax.rem(lax.broadcasted_iota(jnp.int32, (TILE, lanes), 1), TILE)
    ).astype(F32)
    mask = jnp.stack([spot * member[g : g + 1, :] for g in range(groups)])
    full = rounded[:, None, None, :] * mask[None]
    return full.reshape(experts * groups * TILE, lanes).astype(BF16), mask


def exchange(local, gathered, send, recv, row, place, pos):
    copies = []
    for step in range(1, pos):
        copies.append(
            remote(
                local,
                gathered.at[step - 1],
                send.at[step - 1],
                recv.at[step - 1],
                (row, lax.rem(place + step, pos)),
            )
        )
        copies[-1].start()
    for copy in copies:
        copy.wait()


def expert_kernel(dp, pos, groups, h_in, cot_in, logits, member, member_s, wout_in, *rest):
    count = bits_of(pos)
    wins, rest = rest[:3], rest[3:]
    mix, dh, dc, rest = rest[0], rest[1], rest[2], rest[3:]
    grads_out, rest = rest[:3], rest[3:]
    grads, rest = rest[:dp], rest[dp:]
    (share, share_s, dw, h, win, wout, stats, gathered, inner, gathered_inner), rest = (
        rest[:10],
        rest[10:],
    )
    (m_part, dy_part, m_t, z, slope, du), rest = rest[:6], rest[6:]
    ring_in, rest = rest[0], rest[1:]
    buffers, rest = rest[: 4 * count], rest[4 * count :]
    asend, arecv, bsend, brecv, csend, crecv, psend, precv, wsend, wrecv, gsend, grecv, dsend, drecv, osem, isem = (
        rest
    )
    row, place = lax.axis_index("dp"), lax.axis_index("pos")
    bits = my_bits(place, count)
    slots, length, width = h.shape
    right, left = lax.rem(row + 1, dp), lax.rem(row + dp - 1, dp)
    mates = [lax.rem(place + step, pos) for step in range(1, pos)]
    copies = pos // wout_in.shape[0]
    loads = [
        pltpu.make_async_copy(h_in, h, isem.at[0]),
        pltpu.make_async_copy(wout_in.at[place // copies], wout.at[row, place], isem.at[1]),
    ]
    middle = wout.shape[1] // 2
    halves = (slice(0, middle), slice(middle, 2 * middle))
    for step, part in enumerate(wins):
        loads.append(
            pltpu.make_async_copy(part, win.at[(row, left, right)[step]], isem.at[2 + step])
        )
    for copy in loads:
        copy.start()
    greet([(right, place), (left, place)] + [(row, mate) for mate in mates])
    pcopies = [
        remote(
            wout_in.at[mate // copies],
            wout.at[row, place],
            psend.at[step],
            precv.at[step],
            (row, mate),
        )
        for step, mate in enumerate(mates)
    ]

    for copy in pcopies:
        copy.start()

    def ring(which, distance):
        array = (win, wout)[which]
        sent = []
        for way, other in enumerate((right, left)):
            back = (distance - 1) * (1 - 2 * way)
            spot = (lax.rem(row + 2 * dp - back, dp),)
            if 2 * distance == dp:
                spot = spot + (halves[way],)
            at = (which * dp // 2 + distance - 1) * 2 + way
            sent.append(
                remote(array.at[spot], array.at[spot], wsend.at[at], wrecv.at[at], (other, place))
            )
            sent[-1].start()
        return sent

    def ring_on(which, first, passed):
        for distance in range(first, dp // 2 + 1):
            for copy in passed:
                copy.wait()
            passed = ring(which, distance)
        return passed

    win_ring = ring_on(0, 2, loads[2:])
    blocks = length // TILE
    lanes = slots * TILE
    experts = logits.shape[1]
    inside = [[member_s[g, s : s + 1, :] for s in range(slots)] for g in range(groups)]
    for g in range(groups):
        peak = jnp.full((experts, length), MASKED, F32)
        for s in range(slots):
            peak = jnp.maximum(peak, jnp.where(inside[g][s] > 0, logits[s], MASKED))
        total = jnp.zeros((experts, length), F32)
        for s in range(slots):
            total = total + jnp.where(inside[g][s] > 0, jnp.exp(logits[s] - peak), 0.0)
        stats[g] = peak
        stats[groups + g] = total
    exchange(stats, gathered, asend, arecv, row, place, pos)
    for copy in pcopies + loads[1:2]:
        copy.wait()
    wout_ring = ring(1, 1)
    for g in range(groups):
        peak = stats[g]
        for step in range(pos - 1):
            peak = jnp.maximum(peak, gathered[step, g])
        total = stats[groups + g] * jnp.exp(stats[g] - peak)
        for step in range(pos - 1):
            total = total + gathered[step, groups + g] * jnp.exp(gathered[step, g] - peak)
        stats[g] = peak
        stats[groups + g] = 1.0 / total
    parts = []
    for s in range(slots):
        peak = jnp.zeros((experts, length), F32)
        scale = jnp.zeros((experts, length), F32)
        some = jnp.zeros((1, length), F32)
        for g in range(groups):
            peak = peak + inside[g][s] * stats[g]
            scale = scale + inside[g][s] * stats[groups + g]
            some = some + inside[g][s]
        parts.append(jnp.exp(jnp.where(some > 0, logits[s] - peak, MASKED)) * scale)
        share_s[s] = parts[s]
    for block, part in enumerate(turn(parts)):
        share[block] = part

    lead = (2,) * (count + 1)
    loads[0].wait()

    def mixture(block, carry):
        where = pl.ds(pl.multiple_of(block * TILE, TILE), TILE)
        rows = h[:, where, :].reshape(lanes, width)
        weights, _ = block_weights(share[block], member, groups)
        m_part[..., where, :] = dot(weights, rows).astype(BF16).reshape(lead + (TILE, width))
        return carry

    def gradient(block, carry):
        where = pl.ds(pl.multiple_of(block * TILE, TILE), TILE)
        grads = h[:, where, :].reshape(lanes, width)
        weights, _ = block_weights(share[block], member, groups)
        dy_part[..., where, :] = (
            (32.0 * dot(weights, grads)).astype(BF16).reshape(lead + (TILE, width))
        )
        return carry

    plans = orders(count)
    every = list(range(count))[::-1]
    sources = (m_part, dy_part)
    targets = sources
    partner = lambda bit: (row, across(place, bits, bit))
    half = length // 2
    spans = (slice(0, half), slice(half, length))
    flying = {}

    def start(which, stage, sides=(0, 1)):
        for side in sides:
            lane_of = 2 * which + side
            bit = plans[side][stage]
            left = [b for b in every if b not in plans[side][:stage]]
            away = pick(left, {bit: 1 - bits[bit]})
            src = (
                sources[which].at[away + (slice(None), spans[side])]
                if stage == 0
                else buffers[lane_of * count + stage - 1].at[away]
            )
            at = lane_of * count + stage
            flying[which, side] = remote(
                src, buffers[at], bsend.at[at], brecv.at[at], partner(bit)
            )

    def launch(which, side):
        flying[which, side].start()

    def finish(which, stage, sides=(0, 1)):
        for side in sides:
            lane_of = 2 * which + side
            flying[which, side].wait()
            bit = plans[side][stage]
            left = [b for b in every if b not in plans[side][:stage]]
            near = pick(left, {bit: bits[bit]})
            target = buffers[lane_of * count + stage]
            if stage == 0:
                old = sources[which][near + (slice(None), spans[side])]
            else:
                old = buffers[lane_of * count + stage - 1][near]
            target[...] = (target[...].astype(F32) + old.astype(F32)).astype(BF16)

    def advance(which, stage, sides=(0, 1)):
        for side in sides:
            finish(which, stage, (side,))
            if stage + 1 < count:
                start(which, stage + 1, (side,))
                launch(which, side)

    def final(which):
        return jnp.concatenate(
            [buffers[(2 * which + side) * count + count - 1][...] for side in range(2)], axis=1
        ).reshape(2 * length, width)

    lower, upper = blocks // 2, blocks
    start(0, 0)
    refill = [
        pltpu.make_async_copy(cot_in.at[:, span], h.at[:, span], isem.at[5 + side])
        for side, span in enumerate(spans)
    ]
    lax.fori_loop(0, lower, mixture, 0)
    launch(0, 0)
    refill[0].start()
    lax.fori_loop(lower, upper, mixture, 0)
    launch(0, 1)
    refill[1].start()
    refill[0].wait()
    start(1, 0)
    advance(0, 0, (0,))
    lax.fori_loop(0, lower // 2, gradient, 0)
    advance(0, 0, (1,))
    lax.fori_loop(lower // 2, lower, gradient, 0)
    launch(1, 0)
    refill[1].wait()
    lax.fori_loop(lower, upper, gradient, 0)
    launch(1, 1)

    mine = pick(every, {b: bits[b] for b in every})

    def push(which, stage, sides=(0, 1)):
        for side in sides:
            lane_of = 2 * which + side
            order = plans[side][::-1]
            bit = order[stage]
            spot = targets[which].at[
                pick(every, {b: bits[b] for b in every if b not in order[:stage]})
                + (slice(None), spans[side])
            ]
            at = lane_of * count + stage
            copy = remote(spot, spot, csend.at[at], crecv.at[at], partner(bit))
            copy.start()
            flying[which, side] = copy

    def publish(which, value):
        targets[which][mine] = value.astype(BF16).reshape(2, length, width)
        push(which, 0)

    def relay(which, stage):
        for side in range(2):
            flying[which, side].wait()
            if stage + 1 < count:
                push(which, stage + 1, (side,))

    for stage in range(1, count - 1):
        advance(0, stage)
    advance(1, 0)
    advance(0, count - 1)
    wout_ring = ring_on(1, 2, wout_ring)
    m = final(0)
    m_t[...] = jnp.transpose(m)
    for copy in (loads[2:] if dp < 4 else []) + win_ring:
        copy.wait()
    hidden = win.shape[-1]
    up = win[...].reshape(width, hidden)
    down = wout.reshape(hidden, width)
    piece = hidden // dp
    root = math.sqrt(2 / math.pi)
    for c in range(0, hidden, piece):
        u = dot(m, up[:, c : c + piece])
        square = u * u
        t = jnp.tanh(u * (root + root * 0.044715 * square))
        gate = 0.5 * (1.0 + t)
        active = (u * gate).astype(BF16)
        z[:, c : c + piece] = active
        slope[:, c : c + piece] = gate + (u * gate) * (1.0 - t) * (
            root + 3 * root * 0.044715 * square
        )
    for copy in wout_ring:
        copy.wait()
    y = dot(z[...], down[...])
    for stage in range(1, count - 1):
        advance(1, stage)
    publish(0, y)
    advance(1, count - 1)
    dy = final(1)
    share_of = width // dp

    def out_of(step):
        whose = lax.rem(row + step, dp)
        grads[step][1] = dot(
            z[:, pl.ds(pl.multiple_of(whose * piece, piece), piece)], dy, 0, 0
        ).astype(BF16)

    def in_of(step):
        whose = lax.rem(row + step, dp)
        strip = m_t[pl.ds(pl.multiple_of(whose * share_of, share_of), share_of), :]
        for c in range(0, hidden, width):
            at = c // width * share_of
            grads[step][0, at : at + share_of, :] = dot(strip, du[:, c : c + width]).astype(BF16)

    def weights_of(step):
        in_of(step)
        out_of(step)

    def pass_sums(distance, ways=(0, 1)):
        sent = []
        for way in ways:
            other = (right, left)[way]
            step = distance if way == 0 else dp - distance
            span = slice(0, 2) if 2 * distance < dp else slice(way, way + 1)
            at = 2 * (distance - 2) + way
            arrived = ring_in.at[distance - 2, way, span]
            sent.append(
                (
                    remote(
                        grads[step].at[span], arrived, gsend.at[at], grecv.at[at], (other, place)
                    ),
                    grads[step - 1 if way == 0 else step + 1],
                    arrived,
                    span,
                )
            )
            sent[-1][0].start()
        return sent

    out_of(dp // 2)
    passed = pass_sums(dp // 2, (1,))
    dm = jnp.zeros((2 * length, width), F32)
    for c in range(0, hidden, piece):
        dz = dot(dy, down[c : c + piece, :], 1, 1).astype(BF16).astype(F32)
        grad = (dz * slope[:, c : c + piece]).astype(BF16)
        du[:, c : c + piece] = grad
        dm = dm + dot(grad, up[:, c : c + piece], 1, 1)
    publish(1, dm)
    relay(0, 0)
    columns = hidden // width
    seats = [
        ((z, du)[s * 2 // slots], s % (slots // 2) // columns * length, s % columns * width)
        for s in range(slots)
    ]
    seat = lambda s: seats[s][0].at[
        seats[s][1] : seats[s][1] + length, seats[s][2] : seats[s][2] + width
    ]
    again = [
        pltpu.make_async_copy(h_in.at[s], seat(s), osem.at[1 + s]) for s in range(slots)
    ]
    mix_out = pltpu.make_async_copy(h, mix, osem.at[0])
    dh_out = [
        pltpu.make_async_copy(seat(s), dh.at[s], osem.at[1 + slots + s]) for s in range(slots)
    ]

    leaving = [
        pltpu.make_async_copy(grads[step], grads_out[i], osem.at[1 + 2 * slots + i])
        for i, step in enumerate((0, 1, dp - 1))
    ]

    def chosen(block):
        return pl.ds(pl.multiple_of(block * TILE, TILE), TILE)

    def picked(whole, mask):
        products = whole.reshape(experts, groups, TILE, lanes) * mask[None]
        return jnp.sum(jnp.sum(products, axis=1), axis=1)

    def first_part(block, carry):
        where = chosen(block)
        weights, mask = block_weights(share[block], member, groups)
        rows = targets[0][..., where, :].reshape(experts * groups * TILE, width)
        grads = h[:, where, :].reshape(lanes, width)
        dw[block] = 32.0 * picked(dot(rows, grads, 1, 1), mask)
        h[:, where, :] = (
            (32.0 * dot(weights, rows, 0, 0)).astype(BF16).reshape(slots, TILE, width)
        )
        return carry

    def second_part(block, carry):
        weights, mask = block_weights(share[block], member, groups)
        rows = targets[1][..., chosen(block), :].reshape(experts * groups * TILE, width)
        places = [
            (
                ref,
                pl.ds(pl.multiple_of(top + block * TILE, TILE), TILE),
                slice(left_edge, left_edge + width),
            )
            for ref, top, left_edge in seats
        ]
        tokens = jnp.concatenate([ref[span, cols] for ref, span, cols in places], axis=0)
        dw[block] = dw[block] + picked(dot(rows, tokens, 1, 1), mask)
        back = dot(weights, rows, 0, 0).astype(BF16)
        for s, (ref, span, cols) in enumerate(places):
            ref[span, cols] = back[s * TILE : (s + 1) * TILE]
        return carry

    in_of(dp // 2)
    passed = passed + pass_sums(dp // 2, (0,))
    relay(1, 0)
    for distance in range(dp // 2 - 1, 0, -1):
        weights_of(distance)
        weights_of(dp - distance)
        if distance == 1:
            weights_of(0)
            for stage in range(1, count):
                relay(0, stage)
            for copy in again:
                copy.start()
            leaving[0].start()
            lax.fori_loop(0, blocks, first_part, 0)
            mix_out.start()
            for stage in range(1, count - 1):
                relay(1, stage)
        for copy, target, arrived, span in passed:
            copy.wait()
            target[span] = (target[span].astype(F32) + arrived[...].astype(F32)).astype(BF16)
        passed = pass_sums(distance) if distance > 1 else []
    leaving[1].start()
    leaving[2].start()
    for copy in again:
        copy.wait()
    flying[1, 0].wait()
    lax.fori_loop(0, lower, second_part, 0)
    flying[1, 1].wait()
    lax.fori_loop(lower, upper, second_part, 0)
    for copy in dh_out:
        copy.start()
    grads_s = turn([dw[b] for b in range(blocks)])
    for g in range(groups):
        total = jnp.zeros((experts, length), F32)
        for s in range(slots):
            total = total + inside[g][s] * share_s[s] * grads_s[s]
        inner[g] = total
    exchange(inner, gathered_inner, dsend, drecv, row, place, pos)
    sums = []
    for g in range(groups):
        total = inner[g]
        for step in range(pos - 1):
            total = total + gathered_inner[step, g]
        sums.append(total)
    for s in range(slots):
        mean = jnp.zeros((experts, length), F32)
        for g in range(groups):
            mean = mean + inside[g][s] * sums[g]
        dc[s] = (share_s[s] * (grads_s[s] - mean)).astype(BF16)
    for copy in [mix_out] + dh_out + leaving:
        copy.wait()


def mix_experts(dp, pos, groups, h, cot, logits, member, member_s, expert_out, win_parts):
    slots, length, width = h.shape
    experts = logits.shape[1]
    part = expert_out.shape[1:]
    lead = (2,) * (bits_of(pos) + 1)
    hidden = win_parts[0].shape[-1]
    blocks = length // TILE
    count = bits_of(pos)
    vmem = pl.BlockSpec(memory_space=pltpu.VMEM)
    hbm = pl.BlockSpec(memory_space=pl.ANY)
    rows = 2 * length
    dma = pltpu.SemaphoreType.DMA
    return pl.pallas_call(
        lambda *refs: expert_kernel(dp, pos, groups, *refs),
        out_shape=[
            jax.ShapeDtypeStruct(h.shape, BF16),
            jax.ShapeDtypeStruct(h.shape, BF16),
            jax.ShapeDtypeStruct(logits.shape, BF16),
        ]
        + [jax.ShapeDtypeStruct((2, hidden // dp, width), BF16)] * 3,
        in_specs=[hbm, hbm, vmem, vmem, vmem, hbm] + [hbm] * 3,
        out_specs=[hbm, hbm, vmem] + [hbm] * 3,
        scratch_shapes=[pltpu.VMEM((2, hidden // dp, width), BF16)] * dp
        + [
            pltpu.VMEM((blocks, experts, slots * TILE), F32),
            pltpu.VMEM(logits.shape, F32),
            pltpu.VMEM((blocks, experts, slots * TILE), F32),
            pltpu.VMEM(h.shape, BF16),
            pltpu.VMEM((dp,) + win_parts[0].shape, BF16),
            pltpu.VMEM((dp, pos) + part, BF16),
            pltpu.VMEM((2 * groups, experts, slots * TILE), F32),
            pltpu.VMEM((pos - 1, 2 * groups, experts, slots * TILE), F32),
            pltpu.VMEM((groups, experts, length), F32),
            pltpu.VMEM((pos - 1, groups, experts, length), F32),
            pltpu.VMEM(lead + (length, width), BF16),
            pltpu.VMEM(lead + (length, width), BF16),
            pltpu.VMEM((width, rows), BF16),
            pltpu.VMEM((rows, hidden), BF16),
            pltpu.VMEM((rows, hidden), F32),
            pltpu.VMEM((rows, hidden), BF16),
            pltpu.VMEM((dp // 2 - 1, 2, 2, hidden // dp, width), BF16),
        ]
        + [
            pltpu.VMEM((2,) * (count - stage) + (length // 2, width), BF16)
            for _ in range(4)
            for stage in range(count)
        ]
        + [
            dma((pos - 1,)),
            dma((pos - 1,)),
            dma((4 * count,)),
            dma((4 * count,)),
            dma((4 * count,)),
            dma((4 * count,)),
            dma((pos - 1,)),
            dma((pos - 1,)),
            dma((2 * dp,)),
            dma((2 * dp,)),
            dma((2 * (dp // 2 - 1),)),
            dma((2 * (dp // 2 - 1),)),
            dma((pos - 1,)),
            dma((pos - 1,)),
            dma((4 + 2 * slots,)),
            dma((7,)),
        ],
        compiler_params=pltpu.CompilerParams(
            collective_id=2, has_side_effects=True, vmem_limit_bytes=VMEM_LIMIT
        ),
        name="mix_experts",
    )(h, cot, logits, member, member_s, expert_out, *win_parts)


from jax.sharding import PartitionSpec as P

MIXED_SEQUENCES = 32


def body(
    inputs,
    cotangent,
    counts,
    seq_rank,
    first_gain,
    first_bias,
    query_weight,
    key_weight,
    value_weight,
    output_weight,
    second_gain,
    second_bias,
    control_weight,
    expert_in,
    expert_out,
):
    capacity, length, features = inputs.shape
    dp, pos = lax.axis_size("dp"), lax.axis_size("pos")
    experts = control_weight.shape[1]
    groups = seq_rank.shape[1] // MIXED_SEQUENCES

    w_t, wk, wo, small, member, member_s, live, win = gather_weights(
        dp,
        pos,
        groups,
        capacity,
        query_weight,
        key_weight,
        value_weight,
        output_weight,
        jnp.stack([first_gain, first_bias, second_gain, second_bias]),
        control_weight.T,
        counts,
        seq_rank,
        expert_in,
    )
    count = live[0, :1]

    def send_rows(array, step):
        return lax.ppermute(array, "dp", [(i, (i + step) % dp) for i in range(dp)])

    wins = (win, send_rows(win, 1), send_rows(win, -1))

    q_t, k, v_t, ctx_t, x1, h, inverse, e_t, logits = forward(count, inputs, w_t, wk, wo, small)
    mix, dh, dc, *grads = mix_experts(
        dp, pos, groups, h, cotangent, logits, member, member_s, expert_out, wins
    )
    grads = (grads[0], send_rows(grads[1], 1), send_rows(grads[2], -1))
    layer_output, input_grad, grad_t, out_grad, vecs = backward(
        count, inputs, cotangent, x1, mix, dh, dc, q_t, k, v_t, ctx_t, inverse, e_t, w_t, wo, small
    )
    shard, *grads = scatter_weights(
        dp, pos, grad_t, out_grad, vecs, *grads
    )
    query_grad, key_grad, value_grad, output_grad, control, ein_grad, eout_grad, *vectors = finish(
        experts, shard, *grads
    )
    return (
        layer_output,
        input_grad,
        vectors[2],
        vectors[3],
        query_grad,
        key_grad,
        value_grad,
        output_grad,
        vectors[0],
        vectors[1],
        control.T,
        ein_grad,
        eout_grad,
    )


def solution(mesh):
    both = ("dp", "pos")
    vector, matrix, cube = P(both), P(both, None), P(both, None, None)
    middle = P(None, both, None)
    return jax.shard_map(
        body,
        mesh=mesh,
        in_specs=(
            cube,
            cube,
            P("dp", None),
            P("dp", None),
            vector,
            vector,
            matrix,
            matrix,
            matrix,
            matrix,
            vector,
            vector,
            matrix,
            middle,
            middle,
        ),
        out_specs=(
            cube,
            cube,
            vector,
            vector,
            matrix,
            matrix,
            matrix,
            matrix,
            vector,
            vector,
            matrix,
            middle,
            middle,
        ),
        check_vma=False,
    )
```

```python
import math
import jax
import jax.numpy as jnp
from jax import lax
from jax.experimental import pallas as pl
from jax.experimental.pallas import tpu as pltpu

HEADS = 8
HEAD = 64
NORM_EPS = 1e-05
MASKED = -1e30
F32 = jnp.float32
BF16 = jnp.bfloat16
MIB = 1 << 20
VMEM_LIMIT = 62 * MIB


def dot(a, b, ca=1, cb=0):
    return lax.dot_general(a, b, (((ca,), (cb,)), ((), ())), preferred_element_type=F32)


def normalize(v):
    center = v - jnp.mean(v, axis=-1, keepdims=True)
    spread = jnp.mean(center * center, axis=-1, keepdims=True)
    scale = lax.rsqrt(spread + NORM_EPS)
    return center * scale, scale


def spread_heads(parts):
    return jnp.concatenate(
        [
            jnp.concatenate(
                [part if i == j else jnp.zeros_like(part) for i in range(len(parts))], axis=0
            )
            for j, part in enumerate(parts)
        ],
        axis=1,
    )


def forward_kernel(count, x, w_t, wk, wo, small, q_t, k, v_t, ctx_t, x1, h, inverse, e_t, logits):
    g1, b1, g2, b2 = (small[i : i + 1] for i in range(4))
    slots, length, width = x.shape
    router = small[8:16].astype(BF16)
    wq_t, wv_t = w_t.at[:width], w_t.at[2 * width :]
    half = length // 2
    causal = lax.broadcasted_iota(jnp.int32, (half, half), 0) <= lax.broadcasted_iota(
        jnp.int32, (half, half), 1
    )

    def one():
        source = x[...].reshape(slots * length, width).astype(F32)
        xhat, _ = normalize(source)
        a = (xhat * g1 + b1).astype(BF16)
        qs = (dot(wq_t[...], a, 1, 1).astype(BF16) * 0.125).astype(BF16)
        ks = dot(a, wk[...]).astype(BF16)
        vs = dot(wv_t[...], a, 1, 1).astype(BF16)
        k[...] = ks.reshape(slots, length, width)
        ones = jnp.ones((16, length), BF16)
        parts = [[] for _ in range(slots)]
        sums = [[] for _ in range(slots)]
        cols = [slice(s * length, (s + 1) * length) for s in range(slots)]
        for s in range(slots):
            q_t[s] = qs[:, cols[s]]
            v_t[s] = vs[:, cols[s]]
        for base in range(0, HEADS, 4):
            for s in range(slots):
                four = slice(base * HEAD, (base + 4) * HEAD)
                spread_q = spread_heads(
                    [
                        qs[(base + i) * HEAD : (base + i + 1) * HEAD, cols[s]] for i in range(4)
                    ]
                )
                scores = dot(ks[cols[s], four], spread_q)
                exps = []
                for j in range(4):
                    st = scores[:, j * length : (j + 1) * length]
                    s00 = jnp.where(causal, st[:half, :half], MASKED)
                    s01 = st[:half, half:]
                    s11 = jnp.where(causal, st[half:, half:], MASKED)
                    m0 = jnp.max(s00, axis=0, keepdims=True)
                    m1 = jnp.maximum(
                        jnp.max(s01, axis=0, keepdims=True), jnp.max(s11, axis=0, keepdims=True)
                    )
                    e00 = jnp.exp(s00 - m0).astype(BF16)
                    e01 = jnp.exp(s01 - m1).astype(BF16)
                    e11 = jnp.exp(s11 - m1).astype(BF16)
                    et = jnp.concatenate(
                        [
                            jnp.concatenate([e00, e01], axis=1),
                            jnp.concatenate([jnp.zeros_like(e00), e11], axis=1),
                        ],
                        axis=0,
                    )
                    e_t[s, base + j] = et
                    exps.append(et)
                for j in range(0, 4, 2):
                    head = base + j
                    va = jnp.concatenate(
                        [
                            vs[head * HEAD : (head + 1) * HEAD, cols[s]],
                            ones,
                            vs[(head + 1) * HEAD : (head + 2) * HEAD, cols[s]],
                            ones,
                        ],
                        axis=0,
                    )
                    both = dot(va, jnp.concatenate(exps[j : j + 2], axis=1))
                    for i in range(2):
                        full = both[i * 80 : i * 80 + 80, i * length : (i + 1) * length]
                        total = full[HEAD : HEAD + 1]
                        scale = 1.0 / total
                        parts[s].append((full[:HEAD] * scale).astype(BF16))
                        sums[s].append(scale)
        outs = []
        for s in range(slots):
            ctx = jnp.concatenate(parts[s], axis=0)
            ctx_t[s] = ctx
            inverse[s] = jnp.concatenate(sums[s], axis=0)
            outs.append(ctx)
        residual = source + dot(jnp.concatenate(outs, axis=1), wo[...], 0, 0)
        x1[...] = residual.reshape(slots, length, width)
        xhat2, _ = normalize(residual)
        hidden = (xhat2 * g2 + b2).astype(BF16)
        h[...] = hidden.reshape(slots, length, width)
        for s in range(slots):
            logits[s] = dot(router, hidden[cols[s], :], 1, 1)

    live = pl.program_id(0) * slots < count[0]
    pl.when(live)(one)

    @pl.when(jnp.logical_not(live))
    def _():
        h[...] = jnp.zeros((slots, length, width), BF16)
        logits[...] = jnp.zeros_like(logits)


def forward(count, x, w_t, wk, wo, small, block=2):
    slots, length, width = x.shape
    per = lambda rows, cols: pl.BlockSpec((block, rows, cols), lambda i, c: (i, 0, 0))
    whole = lambda a: pl.BlockSpec(a.shape, lambda i, c: (0,) * a.ndim)
    shape = lambda rows, cols, kind: jax.ShapeDtypeStruct((slots, rows, cols), kind)
    return pl.pallas_call(
        forward_kernel,
        grid_spec=pltpu.PrefetchScalarGridSpec(
            num_scalar_prefetch=1,
            grid=(slots // block,),
            in_specs=[per(length, width)]
            + [whole(a) for a in (w_t, wk, wo, small)],
            out_specs=[
                per(width, length),
                per(length, width),
                per(width, length),
                per(width, length),
                per(length, width),
                per(length, width),
                per(HEADS, length),
            ]
            + [pl.BlockSpec((block, HEADS, length, length), lambda i, c: (i, 0, 0, 0)), per(HEADS, length)],
        ),
        out_shape=[
            shape(width, length, BF16),
            shape(length, width, BF16),
            shape(width, length, BF16),
            shape(width, length, BF16),
            shape(length, width, F32),
            shape(length, width, BF16),
            shape(HEADS, length, F32),
        ]
        + [jax.ShapeDtypeStruct((slots, HEADS, length, length), BF16), shape(8, length, F32)] ,
        compiler_params=pltpu.CompilerParams(vmem_limit_bytes=VMEM_LIMIT),
        cost_estimate=pl.CostEstimate(
            flops=40_000_000_000, bytes_accessed=40 * MIB, transcendentals=8_000_000
        ),
        name="attention_forward",
    )(count, x, w_t, wk, wo, small)


def norm_back(grad, xhat, scale):
    return scale * (
        grad
        - jnp.mean(grad, axis=-1, keepdims=True)
        - xhat * jnp.mean(grad * xhat, axis=-1, keepdims=True)
    )


def backward_kernel(
    count, x, cot, x1, mix, dh, dc, q_t, k, v_t, ctx_t, inverse, e_t, w_t, wo, small,
    lo, dx, grad_t, out_grad, vecs, back_t,
):
    slots, length, width = x.shape
    half = length // 2
    step = pl.program_id(0)

    @pl.when(step == 0)
    def _():
        grad_t[...] = jnp.zeros_like(grad_t)
        out_grad[...] = jnp.zeros_like(out_grad)
        vecs[...] = jnp.zeros_like(vecs)

    g1, b1, g2, b2 = (small[i : i + 1] for i in range(4))
    router = small[8:16].astype(BF16)

    def one():
        tokens = slots * length
        cols = [slice(s * length, (s + 1) * length) for s in range(slots)]
        row = lax.broadcasted_iota(jnp.int32, (tokens, 1), 0) // length + step * slots
        live = row < count[0]
        keep = lambda v: v if slots == 1 else jnp.where(live, v, 0.0)
        residual = x1[...].reshape(tokens, width)
        xhat2, scale2 = normalize(residual)
        lo[...] = (
            keep(residual + mix[...].reshape(tokens, width).astype(F32))
            .astype(BF16)
            .reshape(slots, length, width)
        )
        hidden = (xhat2 * g2 + b2).astype(BF16)
        routed = []
        for s in range(slots):
            routed.append(dot(dc[s], router, 0, 0))
            vecs[8:16] += dot(dc[s], hidden[cols[s], :])
        grad_h = (
            (dh[...].reshape(tokens, width).astype(F32) + jnp.concatenate(routed, axis=0))
            .astype(BF16)
            .astype(F32)
        )
        vecs[0:1] += jnp.sum(grad_h * xhat2, axis=0, keepdims=True)
        vecs[1:2] += jnp.sum(grad_h, axis=0, keepdims=True)
        dx1 = keep(
            cot[...].reshape(tokens, width).astype(F32) + norm_back(grad_h * g2, xhat2, scale2)
        )
        datt = dx1.astype(BF16)
        dctx = dot(wo[...], datt, 1, 1).astype(BF16)
        out_grad[...] += dot(jnp.concatenate([ctx_t[s] for s in range(slots)], axis=1), datt)
        zero = jnp.zeros((half, half), BF16)
        for s in range(slots):
            kt = jnp.transpose(k[s])
            vn = jnp.transpose(v_t[s])
            scaled = []
            inners = []
            for head in range(HEADS):
                rows = slice(head * HEAD, (head + 1) * HEAD)
                part = dctx[rows, cols[s]].astype(F32) * inverse[s, head : head + 1, :]
                scaled.append(part.astype(BF16))
                inners.append(jnp.sum(ctx_t[s, rows, :].astype(F32) * part, axis=0, keepdims=True))
            for base in range(0, HEADS, 4):
                four = slice(base * HEAD, (base + 4) * HEAD)
                dprobs = dot(vn[:, four], spread_heads(scaled[base : base + 4]))
                grads = []
                exps = []
                for j in range(4):
                    head = base + j
                    et = e_t[s, head]
                    dp = dprobs[:, j * length : (j + 1) * length]
                    inner = inners[head]
                    d00 = et[:half, :half].astype(F32) * (dp[:half, :half] - inner[:, :half])
                    d01 = et[:half, half:].astype(F32) * (dp[:half, half:] - inner[:, half:])
                    d11 = et[half:, half:].astype(F32) * (dp[half:, half:] - inner[:, half:])
                    grads.append(
                        jnp.concatenate(
                            [
                                jnp.concatenate([d00.astype(BF16), d01.astype(BF16)], axis=1),
                                jnp.concatenate([zero, d11.astype(BF16)], axis=1),
                            ],
                            axis=0,
                        )
                    )
                    exps.append(et)
                tall = jnp.concatenate(grads, axis=0)
                dk = dot(q_t[s, four, :], tall, 1, 1)
                dv = dot(
                    jnp.concatenate(scaled[base : base + 4], axis=0),
                    jnp.concatenate(exps, axis=0),
                    1,
                    1,
                )
                dq = [
                    dot(
                        kt[(base + j) * HEAD : (base + j + 2) * HEAD, :],
                        jnp.concatenate(grads[j : j + 2], axis=1),
                    )
                    * 0.125
                    for j in range(0, 4, 2)
                ]
                for j in range(4):
                    begin = (base + j) * HEAD
                    spot = slice(j * length, (j + 1) * length)
                    inside = slice(j * HEAD, (j + 1) * HEAD)
                    i = j % 2
                    back_t[begin : begin + HEAD, cols[s]] = dq[j // 2][
                        i * HEAD : (i + 1) * HEAD, i * length : (i + 1) * length
                    ].astype(BF16)
                    back_t[width + begin : width + begin + HEAD, cols[s]] = dk[inside, spot].astype(
                        BF16
                    )
                    back_t[2 * width + begin : 2 * width + begin + HEAD, cols[s]] = dv[
                        inside, spot
                    ].astype(BF16)
        source = x[...].reshape(tokens, width).astype(F32)
        xhat1, scale1 = normalize(source)
        a = (xhat1 * g1 + b1).astype(BF16)
        back = back_t[...]
        grad_t[...] += dot(back, a)
        da = dot(back, w_t[...], 0, 0)
        vecs[2:3] += jnp.sum(da * xhat1, axis=0, keepdims=True)
        vecs[3:4] += jnp.sum(da, axis=0, keepdims=True)
        dx[...] = (
            keep(dx1 + norm_back(da * g1, xhat1, scale1))
            .astype(BF16)
            .reshape(slots, length, width)
        )

    some = step * slots < count[0]
    pl.when(some)(one)

    @pl.when(jnp.logical_not(some))
    def _():
        dx[...] = jnp.zeros((slots, length, width), BF16)
        lo[...] = jnp.zeros((slots, length, width), BF16)


def backward(count, x, cot, x1, mix, dh, dc, q_t, k, v_t, ctx_t, inverse, e_t, w_t, wo, small, block=2):
    slots, length, width = x.shape
    per = lambda a: pl.BlockSpec(
        (block,) + a.shape[1:], lambda i, c: (i,) + (0,) * (len(a.shape) - 1)
    )
    whole = lambda a: pl.BlockSpec(a.shape, lambda i, c: (0,) * len(a.shape))
    outs = [
        jax.ShapeDtypeStruct((3 * width, width), F32),
        jax.ShapeDtypeStruct((width, width), F32),
        jax.ShapeDtypeStruct((16, width), F32),
    ]
    batched = (x, cot, x1, mix, dh, dc, q_t, k, v_t, ctx_t, inverse, e_t)
    shared = (w_t, wo, small)
    return pl.pallas_call(
        backward_kernel,
        grid_spec=pltpu.PrefetchScalarGridSpec(
            num_scalar_prefetch=1,
            grid=(slots // block,),
            in_specs=[per(a) for a in batched] + [whole(a) for a in shared],
            out_specs=[per(x), per(x)] + [whole(a) for a in outs],
            scratch_shapes=[pltpu.VMEM((3 * width, block * length), BF16)],
        ),
        out_shape=[jax.ShapeDtypeStruct(x.shape, BF16)] * 2 + outs,
        compiler_params=pltpu.CompilerParams(vmem_limit_bytes=VMEM_LIMIT),
        cost_estimate=pl.CostEstimate(
            flops=100_000_000_000, bytes_accessed=60 * MIB, transcendentals=8_000_000
        ),
        name="attention_backward",
    )(count, *batched, *shared)


MESH = pl.DeviceIdType.MESH
TILE = 16


def bits_of(size):
    return size.bit_length() - 1


def orders(count):
    first = list(range(count))
    second = list(first)
    if count > 2:
        second[1], second[2] = second[2], second[1]
    return first, second


def greet(peers):
    barrier = pltpu.get_barrier_semaphore()
    for peer in peers:
        pl.semaphore_signal(barrier, inc=1, device_id=peer, device_id_type=MESH)
    pl.semaphore_wait(barrier, len(peers))


def my_bits(place, count):
    return [lax.rem(place // (1 << bit), 2) for bit in range(count)]


def across(place, bits, bit):
    return place + (1 - 2 * bits[bit]) * (1 << bit)


def pick(remaining, chosen):
    return tuple(chosen[bit] if bit in chosen else slice(None) for bit in remaining)


def remote(src, dst, send, recv, device):
    return pltpu.make_async_remote_copy(
        src_ref=src,
        dst_ref=dst,
        send_sem=send,
        recv_sem=recv,
        device_id=device,
        device_id_type=MESH,
    )


def gather_kernel(
    dp, pos, groups, slots,
    wq, wk, wv, wo, vec0, vec1, vec2, vec3, router, counts, ranks, ein,
    w_t, wk_out, wo_out, vt, member, member_s, live, win,
    held, zsend, zrecv, send, recv, esend, erecv, lsem,
):
    count = bits_of(pos)
    row, place = lax.axis_index("dp"), lax.axis_index("pos")
    bits = my_bits(place, count)
    others = [lax.rem(row + step, dp) for step in range(1, dp)]
    mates = [lax.rem(place + step, pos) for step in range(1, pos)]
    greet([(other, place) for other in others] + [(row, mate) for mate in mates])
    rows, width = wq.shape
    every = list(range(count))[::-1]
    here = pick(every, {bit: bits[bit] for bit in every})
    for index, weight in enumerate((wq, wk, wv, wo)):
        held[(row,) + here + (slice(None), slice(index * width, (index + 1) * width))] = weight[...]
    tall = jnp.concatenate(
        [
            *[vec[...].astype(F32) for vec in (vec0, vec1, vec2, vec3)],
            jnp.zeros((4, rows), F32),
            router[...].astype(F32),
            jnp.zeros((120 - router.shape[0], rows), F32),
        ],
        axis=0,
    )
    square = jnp.concatenate([tall, jnp.zeros((128, 128 - rows), F32)], axis=1)
    held[(row,) + here + (slice(None), slice(4 * width, 4 * width + 128))] = jnp.transpose(square)[
        :rows
    ].astype(BF16)

    copies = pos // ein.shape[0]
    local = pltpu.make_async_copy(ein.at[place // copies], win.at[place], lsem.at[0])
    local.start()
    zcopies = []
    for step, other in enumerate(others):
        spot = held.at[(row,) + here]
        zcopies.append(remote(spot, spot, zsend.at[step], zrecv.at[step], (other, place)))
        zcopies[-1].start()

    ecopies = []
    for step, mate in enumerate(mates):
        ecopies.append(
            remote(
                ein.at[mate // copies], win.at[place], esend.at[step], erecv.at[step], (row, mate)
            )
        )
        ecopies[-1].start()

    first, second = orders(count)
    plans = (first[::-1], second[::-1])

    def push(block, stage):
        order = plans[block % 2]
        bit = order[stage]
        whose = lax.rem(row + dp - block, dp)
        spot = held.at[
            (whose,) + pick(every, {b: bits[b] for b in every if b not in order[:stage]})
        ]
        at = block * count + stage
        copy = remote(spot, spot, send.at[at], recv.at[at], (row, across(place, bits, bit)))
        copy.start()
        return copy

    flying = {0: push(0, 0)}
    lanes = slots * TILE
    which = lax.broadcasted_iota(jnp.int32, (1, pos), 1)
    begin = jnp.sum(jnp.where(which < place, counts[...], 0), axis=1, keepdims=True)
    mine = jnp.sum(jnp.where(which == place, counts[...], 0), axis=1, keepdims=True)
    live[...] = jnp.broadcast_to(mine, live.shape)
    slot = lax.broadcasted_iota(jnp.int32, (1, lanes), 1) // TILE
    wanted = jnp.where(slot < mine, begin + slot, -1)
    table = (ranks[...] // 32).astype(F32) + 1.0
    size = table.shape[1]
    if size < 128:
        table = jnp.concatenate([table, jnp.zeros((1, 128 - size), F32)], axis=1)
    column = jnp.transpose(jnp.broadcast_to(table, (128, 128)))[:, :1]
    match = lax.broadcasted_iota(jnp.int32, (128, lanes), 0) == wanted
    ids = jnp.sum(jnp.where(match, column, 0.0), axis=0, keepdims=True)
    for g in range(groups):
        member[g : g + 1, :] = (ids == float(g + 1)).astype(F32)
    slot = lax.broadcasted_iota(jnp.int32, (slots, 1), 0)
    wanted = jnp.where(slot < mine, begin + slot, -1)
    match = lax.broadcasted_iota(jnp.int32, (slots, 128), 1) == wanted
    ids = jnp.sum(jnp.where(match, table, 0.0), axis=1, keepdims=True)
    for g in range(groups):
        member_s[g] = jnp.broadcast_to((ids == float(g + 1)).astype(F32), member_s.shape[1:])

    for block in range(1, dp):
        zcopies[block - 1].wait()
        flying[block] = push(block, 0)
    for stage in range(1, count):
        for block in range(dp):
            flying[block].wait()
            flying[block] = push(block, stage)
    for block in range(dp):
        flying[block].wait()
    full = held[...].reshape(dp * pos * rows, 4 * width + 128)
    for index in range(3):
        w_t[index * width : (index + 1) * width, :] = jnp.transpose(
            full[:, index * width : (index + 1) * width]
        )
    wk_out[...] = full[:, width : 2 * width]
    wo_out[...] = full[:, 3 * width : 4 * width]
    vt[...] = jnp.transpose(full[:, 4 * width :])[:16, :].astype(F32)
    for copy in [local] + ecopies:
        copy.wait()


def gather_weights(dp, pos, groups, slots, wq, wk, wv, wo, *rest):
    rows, width = wq.shape
    ein = rest[-1]
    whole = rows * dp * pos
    vmem = pl.BlockSpec(memory_space=pltpu.VMEM)
    hbm = pl.BlockSpec(memory_space=pl.ANY)
    count = bits_of(pos)
    dma = pltpu.SemaphoreType.DMA
    return pl.pallas_call(
        lambda *refs: gather_kernel(dp, pos, groups, slots, *refs),
        out_shape=[
            jax.ShapeDtypeStruct((3 * width, whole), BF16),
            jax.ShapeDtypeStruct((whole, width), BF16),
            jax.ShapeDtypeStruct((whole, width), BF16),
            jax.ShapeDtypeStruct((16, whole), F32),
            jax.ShapeDtypeStruct((groups, slots * TILE), F32),
            jax.ShapeDtypeStruct((groups, slots, slots * TILE), F32),
            jax.ShapeDtypeStruct((1, 128), jnp.int32),
            jax.ShapeDtypeStruct((pos,) + ein.shape[1:], BF16),
        ],
        in_specs=[vmem] * 11 + [hbm],
        out_specs=[vmem] * 7 + [hbm],
        scratch_shapes=[
            pltpu.VMEM((dp,) + (2,) * count + (rows, 4 * width + 128), BF16),
            dma((dp - 1,)),
            dma((dp - 1,)),
            dma((dp * count,)),
            dma((dp * count,)),
            dma((pos - 1,)),
            dma((pos - 1,)),
            dma((1,)),
        ],
        compiler_params=pltpu.CompilerParams(
            collective_id=0, has_side_effects=True, vmem_limit_bytes=VMEM_LIMIT
        ),
        name="gather_weights",
    )(wq, wk, wv, wo, *rest)


def scatter_kernel(dp, pos, grad_in, out_in, vecs, *rest):
    count = bits_of(pos)
    parts, rest = rest[:3], rest[3:]
    out, ein_got, eout_got, held, grad_t, out_grad, grads, isem, *rest = rest
    loads = [pltpu.make_async_copy(part, grads.at[i], isem.at[i]) for i, part in enumerate(parts)]
    loads.append(pltpu.make_async_copy(grad_in, grad_t, isem.at[3]))
    loads.append(pltpu.make_async_copy(out_in, out_grad, isem.at[4]))
    for copy in loads:
        copy.start()
    buffers, slots, rest = rest[: 2 * count], rest[2 * count], rest[2 * count + 1 :]
    send, recv, esend, erecv, ein_mine, eout_mine = rest
    row, place = lax.axis_index("dp"), lax.axis_index("pos")
    bits = my_bits(place, count)
    others = [lax.rem(row + step, dp) for step in range(1, dp)]
    mates = [lax.rem(place + step, pos) for step in range(1, pos)]
    greet([(other, place) for other in others] + [(row, mate) for mate in mates])
    width = out_grad.shape[1]
    ecopies = []
    for copy in loads[:3]:
        copy.wait()
    for index, (mine, got) in enumerate(((ein_mine, ein_got), (eout_mine, eout_got))):
        total = grads[0, index].astype(F32)
        for i in range(1, 3):
            total = total + grads[i, index].astype(F32)
        total = total.astype(BF16)
        if index == 0:
            strip = width // dp
            for c in range(0, mine.shape[2], width):
                at = c // width * strip
                mine[:, :, c : c + width] = total[at : at + strip].reshape(
                    mine.shape[:2] + (width,)
                )
        else:
            mine[...] = total.reshape(mine.shape)
        for step, mate in enumerate(mates):
            at = index * (pos - 1) + step
            ecopies.append(
                remote(mine.at[mate], got.at[place], esend.at[at], erecv.at[at], (row, mate))
            )
            if index == 0:
                ecopies[-1].start()
        got[place] = mine[place]
    for copy in loads[3:]:
        copy.wait()
    lead = held.shape[:-1]
    for index in range(3):
        held[..., index * width : (index + 1) * width] = (
            jnp.transpose(grad_t[index * width : (index + 1) * width, :].astype(BF16)).reshape(
                lead + (width,)
            )
        )
    held[..., 3 * width : 4 * width] = out_grad[...].astype(BF16).reshape(lead + (width,))
    tail = jnp.concatenate([vecs[...], jnp.zeros((112, vecs.shape[1]), F32)], axis=0)
    held[..., 4 * width :] = jnp.transpose(tail).astype(BF16).reshape(lead + (128,))
    halves = (slice(0, dp // 2), slice(dp // 2, dp))
    plans = orders(count)
    current = [held.at[half] for half in halves]
    remaining = [list(range(count))[::-1] for _ in halves]

    def begin(side, stage):
        bit = plans[side][stage]
        away = (slice(None),) + pick(remaining[side], {bit: 1 - bits[bit]})
        at = side * count + stage
        copy = remote(
            current[side].at[away],
            buffers[at],
            send.at[at],
            recv.at[at],
            (row, across(place, bits, bit)),
        )
        copy.start()
        return copy

    flying = [begin(side, 0) for side in range(2)]
    for stage in range(count):
        for side in range(2):
            flying[side].wait()
            bit = plans[side][stage]
            near = (slice(None),) + pick(remaining[side], {bit: bits[bit]})
            target = buffers[side * count + stage]
            target[...] = (
                target[...].astype(F32) + current[side][near].astype(F32)
            ).astype(BF16)
            current[side] = target
            remaining[side] = [b for b in remaining[side] if b != bit]
            if stage + 1 < count:
                flying[side] = begin(side, stage + 1)
        if stage == count - 2:
            for copy in ecopies[len(mates) :]:
                copy.start()
    used = 2 * count
    joined = jnp.concatenate([current[0][...], current[1][...]], axis=0)
    slots[1] = joined
    copies = []
    for step, other in enumerate(others):
        copies.append(
            remote(
                slots.at[1, other],
                slots.at[0, row],
                send.at[used],
                recv.at[used],
                (other, place),
            )
        )
        used += 1
        copies[-1].start()
    for copy in copies:
        copy.wait()
    total = slots[1, row].astype(F32)
    for other in others:
        total = total + slots[0, other].astype(F32)
    out[...] = total
    for copy in ecopies:
        copy.wait()


def scatter_weights(dp, pos, grad_t, out_grad, vecs, *grads):
    width = out_grad.shape[1]
    rows = out_grad.shape[0] // (dp * pos)
    wide = 4 * width + 128
    hidden = grads[0].shape[1] * dp
    hbm = pl.BlockSpec(memory_space=pl.ANY)
    ein_shape = (width // (dp * pos), hidden)
    eout_shape = (hidden // (dp * pos), width)
    vmem = pl.BlockSpec(memory_space=pltpu.VMEM)
    count = bits_of(pos)
    total = dp - 1 + 2 * count
    return pl.pallas_call(
        lambda *refs: scatter_kernel(dp, pos, *refs),
        out_shape=[
            jax.ShapeDtypeStruct((rows, wide), F32),
            jax.ShapeDtypeStruct((pos,) + ein_shape, BF16),
            jax.ShapeDtypeStruct((pos,) + eout_shape, BF16),
        ],
        in_specs=[hbm, hbm, vmem] + [hbm] * 3,
        out_specs=[vmem] * 3,
        scratch_shapes=[
            pltpu.VMEM((dp,) + (2,) * count + (rows, wide), BF16),
            pltpu.VMEM(grad_t.shape, F32),
            pltpu.VMEM(out_grad.shape, F32),
            pltpu.VMEM((3,) + grads[0].shape, BF16),
            pltpu.SemaphoreType.DMA((5,)),
        ]
        + [
            pltpu.VMEM((dp // 2,) + (2,) * (count - 1 - stage) + (rows, wide), BF16)
            for _ in range(2)
            for stage in range(count)
        ]
        + [
            pltpu.VMEM((2, dp, rows, wide), BF16),
            pltpu.SemaphoreType.DMA((total,)),
            pltpu.SemaphoreType.DMA((total,)),
            pltpu.SemaphoreType.DMA((2 * (pos - 1),)),
            pltpu.SemaphoreType.DMA((2 * (pos - 1),)),
            pltpu.VMEM((pos,) + ein_shape, BF16),
            pltpu.VMEM((pos,) + eout_shape, BF16),
        ],
        compiler_params=pltpu.CompilerParams(
            collective_id=1, has_side_effects=True, vmem_limit_bytes=VMEM_LIMIT
        ),
        name="scatter_weights",
    )(grad_t, out_grad, vecs, *grads)


def finish_kernel(shard, ein_got, eout_got, *outs):
    width = outs[0].shape[1]
    rows = shard.shape[0]
    for index in range(4):
        outs[index][...] = shard[:, index * width : (index + 1) * width]
    tail = jnp.transpose(
        jnp.concatenate([shard[:, 4 * width :], jnp.zeros((128 - rows, 128), F32)], axis=0)
    )
    outs[4][...] = tail[8:16, :rows]
    for index in range(4):
        outs[7 + index][...] = tail[index, :rows]
    for got, target in ((ein_got, outs[5]), (eout_got, outs[6])):
        experts = target.shape[0]
        copies = got.shape[0] // experts
        for expert in range(experts):
            total = got[expert * copies].astype(F32)
            for copy in range(1, copies):
                total = total + got[expert * copies + copy].astype(F32)
            target[expert] = total


def finish(experts, shard, ein_got, eout_got):
    rows = shard.shape[0]
    width = (shard.shape[1] - 128) // 4
    vmem = pl.BlockSpec(memory_space=pltpu.VMEM)
    return pl.pallas_call(
        finish_kernel,
        out_shape=[jax.ShapeDtypeStruct((rows, width), F32)] * 4
        + [jax.ShapeDtypeStruct((8, rows), F32)]
        + [
            jax.ShapeDtypeStruct((experts,) + ein_got.shape[1:], F32),
            jax.ShapeDtypeStruct((experts,) + eout_got.shape[1:], F32),
        ]
        + [jax.ShapeDtypeStruct((rows,), F32)] * 4,
        in_specs=[vmem] * 3,
        out_specs=[vmem] * 11,
        compiler_params=pltpu.CompilerParams(vmem_limit_bytes=VMEM_LIMIT),
        name="finish",
    )(shard, ein_got, eout_got)


def turn(parts):
    size = len(parts)
    lanes = parts[0].shape[1]
    tile = lax.broadcasted_iota(jnp.int32, parts[0].shape, 1) // TILE
    step = 1
    while step < size:
        low = lax.rem(tile // step, 2) == 0
        new = list(parts)
        for i in range(size):
            if i & step == 0:
                upper, lower = parts[i], parts[i | step]
                new[i] = jnp.where(low, upper, pltpu.roll(lower, step * TILE, 1))
                new[i | step] = jnp.where(low, pltpu.roll(upper, lanes - step * TILE, 1), lower)
        parts = new
        step *= 2
    return parts


def block_weights(share, member, groups):
    experts, lanes = share.shape
    rounded = share.astype(BF16).astype(F32)
    spot = (
        lax.broadcasted_iota(jnp.int32, (TILE, lanes), 0)
        == lax.rem(lax.broadcasted_iota(jnp.int32, (TILE, lanes), 1), TILE)
    ).astype(F32)
    mask = jnp.stack([spot * member[g : g + 1, :] for g in range(groups)])
    full = rounded[:, None, None, :] * mask[None]
    return full.reshape(experts * groups * TILE, lanes).astype(BF16), mask


def exchange(local, gathered, send, recv, row, place, pos):
    copies = []
    for step in range(1, pos):
        copies.append(
            remote(
                local,
                gathered.at[step - 1],
                send.at[step - 1],
                recv.at[step - 1],
                (row, lax.rem(place + step, pos)),
            )
        )
        copies[-1].start()
    for copy in copies:
        copy.wait()


def expert_kernel(dp, pos, groups, h_in, cot_in, logits, member, member_s, wout_in, *rest):
    count = bits_of(pos)
    wins, rest = rest[:3], rest[3:]
    mix, dh, dc, rest = rest[0], rest[1], rest[2], rest[3:]
    grads_out, rest = rest[:3], rest[3:]
    grads, rest = rest[:dp], rest[dp:]
    (share, share_s, dw, h, win, wout, stats, gathered, inner, gathered_inner), rest = (
        rest[:10],
        rest[10:],
    )
    (m_part, dy_part, m_t, z, slope, du), rest = rest[:6], rest[6:]
    ring_in, rest = rest[0], rest[1:]
    buffers, rest = rest[: 4 * count], rest[4 * count :]
    asend, arecv, bsend, brecv, csend, crecv, psend, precv, wsend, wrecv, gsend, grecv, dsend, drecv, osem, isem = (
        rest
    )
    row, place = lax.axis_index("dp"), lax.axis_index("pos")
    bits = my_bits(place, count)
    slots, length, width = h.shape
    right, left = lax.rem(row + 1, dp), lax.rem(row + dp - 1, dp)
    mates = [lax.rem(place + step, pos) for step in range(1, pos)]
    copies = pos // wout_in.shape[0]
    loads = [
        pltpu.make_async_copy(h_in, h, isem.at[0]),
        pltpu.make_async_copy(wout_in.at[place // copies], wout.at[row, place], isem.at[1]),
    ]
    middle = wout.shape[1] // 2
    halves = (slice(0, middle), slice(middle, 2 * middle))
    for step, part in enumerate(wins):
        loads.append(
            pltpu.make_async_copy(part, win.at[(row, left, right)[step]], isem.at[2 + step])
        )
    for copy in loads:
        copy.start()
    greet([(right, place), (left, place)] + [(row, mate) for mate in mates])
    pcopies = [
        remote(
            wout_in.at[mate // copies],
            wout.at[row, place],
            psend.at[step],
            precv.at[step],
            (row, mate),
        )
        for step, mate in enumerate(mates)
    ]

    for copy in pcopies:
        copy.start()

    def ring(which, distance):
        array = (win, wout)[which]
        sent = []
        for way, other in enumerate((right, left)):
            back = (distance - 1) * (1 - 2 * way)
            spot = (lax.rem(row + 2 * dp - back, dp),)
            if 2 * distance == dp:
                spot = spot + (halves[way],)
            at = (which * dp // 2 + distance - 1) * 2 + way
            sent.append(
                remote(array.at[spot], array.at[spot], wsend.at[at], wrecv.at[at], (other, place))
            )
            sent[-1].start()
        return sent

    def ring_on(which, first, passed):
        for distance in range(first, dp // 2 + 1):
            for copy in passed:
                copy.wait()
            passed = ring(which, distance)
        return passed

    win_ring = ring_on(0, 2, loads[2:])
    blocks = length // TILE
    lanes = slots * TILE
    experts = logits.shape[1]
    inside = [[member_s[g, s : s + 1, :] for s in range(slots)] for g in range(groups)]
    for g in range(groups):
        peak = jnp.full((experts, length), MASKED, F32)
        for s in range(slots):
            peak = jnp.maximum(peak, jnp.where(inside[g][s] > 0, logits[s], MASKED))
        total = jnp.zeros((experts, length), F32)
        for s in range(slots):
            total = total + jnp.where(inside[g][s] > 0, jnp.exp(logits[s] - peak), 0.0)
        stats[g] = peak
        stats[groups + g] = total
    exchange(stats, gathered, asend, arecv, row, place, pos)
    for copy in pcopies + loads[1:2]:
        copy.wait()
    wout_ring = ring(1, 1)
    for g in range(groups):
        peak = stats[g]
        for step in range(pos - 1):
            peak = jnp.maximum(peak, gathered[step, g])
        total = stats[groups + g] * jnp.exp(stats[g] - peak)
        for step in range(pos - 1):
            total = total + gathered[step, groups + g] * jnp.exp(gathered[step, g] - peak)
        stats[g] = peak
        stats[groups + g] = 1.0 / total
    parts = []
    for s in range(slots):
        peak = jnp.zeros((experts, length), F32)
        scale = jnp.zeros((experts, length), F32)
        some = jnp.zeros((1, length), F32)
        for g in range(groups):
            peak = peak + inside[g][s] * stats[g]
            scale = scale + inside[g][s] * stats[groups + g]
            some = some + inside[g][s]
        parts.append(jnp.exp(jnp.where(some > 0, logits[s] - peak, MASKED)) * scale)
        share_s[s] = parts[s]
    for block, part in enumerate(turn(parts)):
        share[block] = part

    lead = (2,) * (count + 1)
    loads[0].wait()

    def mixture(block, carry):
        where = pl.ds(pl.multiple_of(block * TILE, TILE), TILE)
        rows = h[:, where, :].reshape(lanes, width)
        weights, _ = block_weights(share[block], member, groups)
        m_part[..., where, :] = dot(weights, rows).astype(BF16).reshape(lead + (TILE, width))
        return carry

    def gradient(block, carry):
        where = pl.ds(pl.multiple_of(block * TILE, TILE), TILE)
        grads = h[:, where, :].reshape(lanes, width)
        weights, _ = block_weights(share[block], member, groups)
        dy_part[..., where, :] = (
            (32.0 * dot(weights, grads)).astype(BF16).reshape(lead + (TILE, width))
        )
        return carry

    plans = orders(count)
    every = list(range(count))[::-1]
    sources = (m_part, dy_part)
    targets = sources
    partner = lambda bit: (row, across(place, bits, bit))
    half = length // 2
    spans = (slice(0, half), slice(half, length))
    flying = {}

    def start(which, stage, sides=(0, 1)):
        for side in sides:
            lane_of = 2 * which + side
            bit = plans[side][stage]
            left = [b for b in every if b not in plans[side][:stage]]
            away = pick(left, {bit: 1 - bits[bit]})
            src = (
                sources[which].at[away + (slice(None), spans[side])]
                if stage == 0
                else buffers[lane_of * count + stage - 1].at[away]
            )
            at = lane_of * count + stage
            flying[which, side] = remote(
                src, buffers[at], bsend.at[at], brecv.at[at], partner(bit)
            )

    def launch(which, side):
        flying[which, side].start()

    def finish(which, stage, sides=(0, 1)):
        for side in sides:
            lane_of = 2 * which + side
            flying[which, side].wait()
            bit = plans[side][stage]
            left = [b for b in every if b not in plans[side][:stage]]
            near = pick(left, {bit: bits[bit]})
            target = buffers[lane_of * count + stage]
            if stage == 0:
                old = sources[which][near + (slice(None), spans[side])]
            else:
                old = buffers[lane_of * count + stage - 1][near]
            target[...] = (target[...].astype(F32) + old.astype(F32)).astype(BF16)

    def advance(which, stage, sides=(0, 1)):
        for side in sides:
            finish(which, stage, (side,))
            if stage + 1 < count:
                start(which, stage + 1, (side,))
                launch(which, side)

    def final(which):
        return jnp.concatenate(
            [buffers[(2 * which + side) * count + count - 1][...] for side in range(2)], axis=1
        ).reshape(2 * length, width)

    lower, upper = blocks // 2, blocks
    start(0, 0)
    refill = [
        pltpu.make_async_copy(cot_in.at[:, span], h.at[:, span], isem.at[5 + side])
        for side, span in enumerate(spans)
    ]
    lax.fori_loop(0, lower, mixture, 0)
    launch(0, 0)
    refill[0].start()
    lax.fori_loop(lower, upper, mixture, 0)
    launch(0, 1)
    refill[1].start()
    refill[0].wait()
    start(1, 0)
    advance(0, 0, (0,))
    lax.fori_loop(0, lower // 2, gradient, 0)
    advance(0, 0, (1,))
    lax.fori_loop(lower // 2, lower, gradient, 0)
    launch(1, 0)
    refill[1].wait()
    lax.fori_loop(lower, upper, gradient, 0)
    launch(1, 1)

    mine = pick(every, {b: bits[b] for b in every})

    def push(which, stage, sides=(0, 1)):
        for side in sides:
            lane_of = 2 * which + side
            order = plans[side][::-1]
            bit = order[stage]
            spot = targets[which].at[
                pick(every, {b: bits[b] for b in every if b not in order[:stage]})
                + (slice(None), spans[side])
            ]
            at = lane_of * count + stage
            copy = remote(spot, spot, csend.at[at], crecv.at[at], partner(bit))
            copy.start()
            flying[which, side] = copy

    def publish(which, value):
        targets[which][mine] = value.astype(BF16).reshape(2, length, width)
        push(which, 0)

    def relay(which, stage):
        for side in range(2):
            flying[which, side].wait()
            if stage + 1 < count:
                push(which, stage + 1, (side,))

    for stage in range(1, count - 1):
        advance(0, stage)
    advance(1, 0)
    advance(0, count - 1)
    wout_ring = ring_on(1, 2, wout_ring)
    m = final(0)
    m_t[...] = jnp.transpose(m)
    for copy in (loads[2:] if dp < 4 else []) + win_ring:
        copy.wait()
    hidden = win.shape[-1]
    up = win[...].reshape(width, hidden)
    down = wout.reshape(hidden, width)
    piece = hidden // dp
    root = math.sqrt(2 / math.pi)
    for c in range(0, hidden, piece):
        u = dot(m, up[:, c : c + piece])
        square = u * u
        t = jnp.tanh(u * (root + root * 0.044715 * square))
        gate = 0.5 * (1.0 + t)
        active = (u * gate).astype(BF16)
        z[:, c : c + piece] = active
        slope[:, c : c + piece] = gate + (u * gate) * (1.0 - t) * (
            root + 3 * root * 0.044715 * square
        )
    for copy in wout_ring:
        copy.wait()
    y = dot(z[...], down[...])
    for stage in range(1, count - 1):
        advance(1, stage)
    publish(0, y)
    advance(1, count - 1)
    dy = final(1)
    share_of = width // dp

    def out_of(step):
        whose = lax.rem(row + step, dp)
        grads[step][1] = dot(
            z[:, pl.ds(pl.multiple_of(whose * piece, piece), piece)], dy, 0, 0
        ).astype(BF16)

    def in_of(step):
        whose = lax.rem(row + step, dp)
        strip = m_t[pl.ds(pl.multiple_of(whose * share_of, share_of), share_of), :]
        for c in range(0, hidden, width):
            at = c // width * share_of
            grads[step][0, at : at + share_of, :] = dot(strip, du[:, c : c + width]).astype(BF16)

    def weights_of(step):
        in_of(step)
        out_of(step)

    def pass_sums(distance, ways=(0, 1)):
        sent = []
        for way in ways:
            other = (right, left)[way]
            step = distance if way == 0 else dp - distance
            span = slice(0, 2) if 2 * distance < dp else slice(way, way + 1)
            at = 2 * (distance - 2) + way
            arrived = ring_in.at[distance - 2, way, span]
            sent.append(
                (
                    remote(
                        grads[step].at[span], arrived, gsend.at[at], grecv.at[at], (other, place)
                    ),
                    grads[step - 1 if way == 0 else step + 1],
                    arrived,
                    span,
                )
            )
            sent[-1][0].start()
        return sent

    out_of(dp // 2)
    passed = pass_sums(dp // 2, (1,))
    dm = jnp.zeros((2 * length, width), F32)
    for c in range(0, hidden, piece):
        dz = dot(dy, down[c : c + piece, :], 1, 1).astype(BF16).astype(F32)
        grad = (dz * slope[:, c : c + piece]).astype(BF16)
        du[:, c : c + piece] = grad
        dm = dm + dot(grad, up[:, c : c + piece], 1, 1)
    publish(1, dm)
    relay(0, 0)
    columns = hidden // width
    seats = [
        ((z, du)[s * 2 // slots], s % (slots // 2) // columns * length, s % columns * width)
        for s in range(slots)
    ]
    seat = lambda s: seats[s][0].at[
        seats[s][1] : seats[s][1] + length, seats[s][2] : seats[s][2] + width
    ]
    again = [
        pltpu.make_async_copy(h_in.at[s], seat(s), osem.at[1 + s]) for s in range(slots)
    ]
    mix_out = pltpu.make_async_copy(h, mix, osem.at[0])
    dh_out = [
        pltpu.make_async_copy(seat(s), dh.at[s], osem.at[1 + slots + s]) for s in range(slots)
    ]

    leaving = [
        pltpu.make_async_copy(grads[step], grads_out[i], osem.at[1 + 2 * slots + i])
        for i, step in enumerate((0, 1, dp - 1))
    ]

    def chosen(block):
        return pl.ds(pl.multiple_of(block * TILE, TILE), TILE)

    def picked(whole, mask):
        products = whole.reshape(experts, groups, TILE, lanes) * mask[None]
        return jnp.sum(jnp.sum(products, axis=1), axis=1)

    def first_part(block, carry):
        where = chosen(block)
        weights, mask = block_weights(share[block], member, groups)
        rows = targets[0][..., where, :].reshape(experts * groups * TILE, width)
        grads = h[:, where, :].reshape(lanes, width)
        dw[block] = 32.0 * picked(dot(rows, grads, 1, 1), mask)
        h[:, where, :] = (
            (32.0 * dot(weights, rows, 0, 0)).astype(BF16).reshape(slots, TILE, width)
        )
        return carry

    def second_part(block, carry):
        weights, mask = block_weights(share[block], member, groups)
        rows = targets[1][..., chosen(block), :].reshape(experts * groups * TILE, width)
        places = [
            (
                ref,
                pl.ds(pl.multiple_of(top + block * TILE, TILE), TILE),
                slice(left_edge, left_edge + width),
            )
            for ref, top, left_edge in seats
        ]
        tokens = jnp.concatenate([ref[span, cols] for ref, span, cols in places], axis=0)
        dw[block] = dw[block] + picked(dot(rows, tokens, 1, 1), mask)
        back = dot(weights, rows, 0, 0).astype(BF16)
        for s, (ref, span, cols) in enumerate(places):
            ref[span, cols] = back[s * TILE : (s + 1) * TILE]
        return carry

    in_of(dp // 2)
    passed = passed + pass_sums(dp // 2, (0,))
    relay(1, 0)
    for distance in range(dp // 2 - 1, 0, -1):
        weights_of(distance)
        weights_of(dp - distance)
        if distance == 1:
            weights_of(0)
            for stage in range(1, count):
                relay(0, stage)
            for copy in again:
                copy.start()
            leaving[0].start()
            lax.fori_loop(0, lower, first_part, 0)
            for stage in range(1, count - 1):
                relay(1, stage)
            lax.fori_loop(lower, blocks, first_part, 0)
            mix_out.start()
        for copy, target, arrived, span in passed:
            copy.wait()
            target[span] = (target[span].astype(F32) + arrived[...].astype(F32)).astype(BF16)
        passed = pass_sums(distance) if distance > 1 else []
    leaving[1].start()
    leaving[2].start()
    for copy in again:
        copy.wait()
    flying[1, 0].wait()
    lax.fori_loop(0, lower, second_part, 0)
    flying[1, 1].wait()
    lax.fori_loop(lower, upper, second_part, 0)
    for copy in dh_out:
        copy.start()
    grads_s = turn([dw[b] for b in range(blocks)])
    for g in range(groups):
        total = jnp.zeros((experts, length), F32)
        for s in range(slots):
            total = total + inside[g][s] * share_s[s] * grads_s[s]
        inner[g] = total
    exchange(inner, gathered_inner, dsend, drecv, row, place, pos)
    sums = []
    for g in range(groups):
        total = inner[g]
        for step in range(pos - 1):
            total = total + gathered_inner[step, g]
        sums.append(total)
    for s in range(slots):
        mean = jnp.zeros((experts, length), F32)
        for g in range(groups):
            mean = mean + inside[g][s] * sums[g]
        dc[s] = (share_s[s] * (grads_s[s] - mean)).astype(BF16)
    for copy in [mix_out] + dh_out + leaving:
        copy.wait()


def mix_experts(dp, pos, groups, h, cot, logits, member, member_s, expert_out, win_parts):
    slots, length, width = h.shape
    experts = logits.shape[1]
    part = expert_out.shape[1:]
    lead = (2,) * (bits_of(pos) + 1)
    hidden = win_parts[0].shape[-1]
    blocks = length // TILE
    count = bits_of(pos)
    vmem = pl.BlockSpec(memory_space=pltpu.VMEM)
    hbm = pl.BlockSpec(memory_space=pl.ANY)
    rows = 2 * length
    dma = pltpu.SemaphoreType.DMA
    return pl.pallas_call(
        lambda *refs: expert_kernel(dp, pos, groups, *refs),
        out_shape=[
            jax.ShapeDtypeStruct(h.shape, BF16),
            jax.ShapeDtypeStruct(h.shape, BF16),
            jax.ShapeDtypeStruct(logits.shape, BF16),
        ]
        + [jax.ShapeDtypeStruct((2, hidden // dp, width), BF16)] * 3,
        in_specs=[hbm, hbm, vmem, vmem, vmem, hbm] + [hbm] * 3,
        out_specs=[hbm, hbm, vmem] + [hbm] * 3,
        scratch_shapes=[pltpu.VMEM((2, hidden // dp, width), BF16)] * dp
        + [
            pltpu.VMEM((blocks, experts, slots * TILE), F32),
            pltpu.VMEM(logits.shape, F32),
            pltpu.VMEM((blocks, experts, slots * TILE), F32),
            pltpu.VMEM(h.shape, BF16),
            pltpu.VMEM((dp,) + win_parts[0].shape, BF16),
            pltpu.VMEM((dp, pos) + part, BF16),
            pltpu.VMEM((2 * groups, experts, slots * TILE), F32),
            pltpu.VMEM((pos - 1, 2 * groups, experts, slots * TILE), F32),
            pltpu.VMEM((groups, experts, length), F32),
            pltpu.VMEM((pos - 1, groups, experts, length), F32),
            pltpu.VMEM(lead + (length, width), BF16),
            pltpu.VMEM(lead + (length, width), BF16),
            pltpu.VMEM((width, rows), BF16),
            pltpu.VMEM((rows, hidden), BF16),
            pltpu.VMEM((rows, hidden), F32),
            pltpu.VMEM((rows, hidden), BF16),
            pltpu.VMEM((dp // 2 - 1, 2, 2, hidden // dp, width), BF16),
        ]
        + [
            pltpu.VMEM((2,) * (count - stage) + (length // 2, width), BF16)
            for _ in range(4)
            for stage in range(count)
        ]
        + [
            dma((pos - 1,)),
            dma((pos - 1,)),
            dma((4 * count,)),
            dma((4 * count,)),
            dma((4 * count,)),
            dma((4 * count,)),
            dma((pos - 1,)),
            dma((pos - 1,)),
            dma((2 * dp,)),
            dma((2 * dp,)),
            dma((2 * (dp // 2 - 1),)),
            dma((2 * (dp // 2 - 1),)),
            dma((pos - 1,)),
            dma((pos - 1,)),
            dma((4 + 2 * slots,)),
            dma((7,)),
        ],
        compiler_params=pltpu.CompilerParams(
            collective_id=2, has_side_effects=True, vmem_limit_bytes=VMEM_LIMIT
        ),
        name="mix_experts",
    )(h, cot, logits, member, member_s, expert_out, *win_parts)


from jax.sharding import PartitionSpec as P

MIXED_SEQUENCES = 32


def body(
    inputs,
    cotangent,
    counts,
    seq_rank,
    first_gain,
    first_bias,
    query_weight,
    key_weight,
    value_weight,
    output_weight,
    second_gain,
    second_bias,
    control_weight,
    expert_in,
    expert_out,
):
    capacity, length, features = inputs.shape
    dp, pos = lax.axis_size("dp"), lax.axis_size("pos")
    experts = control_weight.shape[1]
    groups = seq_rank.shape[1] // MIXED_SEQUENCES

    w_t, wk, wo, small, member, member_s, live, win = gather_weights(
        dp,
        pos,
        groups,
        capacity,
        query_weight,
        key_weight,
        value_weight,
        output_weight,
        *[part[None] for part in (first_gain, first_bias, second_gain, second_bias)],
        control_weight.T,
        counts,
        seq_rank,
        expert_in,
    )
    count = live[0, :1]

    def send_rows(array, step):
        return lax.ppermute(array, "dp", [(i, (i + step) % dp) for i in range(dp)])

    wins = (win, send_rows(win, 1), send_rows(win, -1))

    q_t, k, v_t, ctx_t, x1, h, inverse, e_t, logits = forward(count, inputs, w_t, wk, wo, small)
    mix, dh, dc, *grads = mix_experts(
        dp, pos, groups, h, cotangent, logits, member, member_s, expert_out, wins
    )
    grads = (grads[0], send_rows(grads[1], 1), send_rows(grads[2], -1))
    layer_output, input_grad, grad_t, out_grad, vecs = backward(
        count, inputs, cotangent, x1, mix, dh, dc, q_t, k, v_t, ctx_t, inverse, e_t, w_t, wo, small
    )
    shard, *grads = scatter_weights(
        dp, pos, grad_t, out_grad, vecs, *grads
    )
    query_grad, key_grad, value_grad, output_grad, control, ein_grad, eout_grad, *vectors = finish(
        experts, shard, *grads
    )
    return (
        layer_output,
        input_grad,
        vectors[2],
        vectors[3],
        query_grad,
        key_grad,
        value_grad,
        output_grad,
        vectors[0],
        vectors[1],
        control.T,
        ein_grad,
        eout_grad,
    )


def solution(mesh):
    both = ("dp", "pos")
    vector, matrix, cube = P(both), P(both, None), P(both, None, None)
    middle = P(None, both, None)
    return jax.shard_map(
        body,
        mesh=mesh,
        in_specs=(
            cube,
            cube,
            P("dp", None),
            P("dp", None),
            vector,
            vector,
            matrix,
            matrix,
            matrix,
            matrix,
            vector,
            vector,
            matrix,
            middle,
            middle,
        ),
        out_specs=(
            cube,
            cube,
            vector,
            vector,
            matrix,
            matrix,
            matrix,
            matrix,
            vector,
            vector,
            matrix,
            middle,
            middle,
        ),
        check_vma=False,
    )
```
